32 devices in a mesh: ga: 4 (over y, x), ea: 8 (over z, core).
Axes of the slice: x: 2, y: 2, z: 4, core: 2. Of those that a mesh axis runs over, the one named last changes fastest.
Arguments:
- layer_input: bfloat16 [8192, 2048], P(('ga', 'ea')), may hold values from -6 to 6
- w_query: bfloat16 [2048, 4096], P('ga'), may hold values from -0.125 to 0.125
- w_key: bfloat16 [2048, 512], P('ga'), may hold values from -0.125 to 0.125
- w_value: bfloat16 [2048, 512], P('ga'), may hold values from -0.125 to 0.125
- w_out: bfloat16 [4096, 2048], P('ga'), may hold values from -1 to 1
- attn_gain: bfloat16 [2048], P('ga'), may hold values from 0.5 to 1.5
- query_gain: bfloat16 [128], P('ga'), may hold values from 0.5 to 1.5
- key_gain: bfloat16 [128], P('ga'), may hold values from 0.5 to 1.5
- ffn_gain: bfloat16 [2048], P('ga'), may hold values from 0.5 to 1.5
- w_router: bfloat16 [2048, 16], P('ga'), may hold values from -0.0625 to 0.0625
- w_gate: bfloat16 [16, 2048, 768], P('ea', 'ga'), may hold values from -0.125 to 0.125
- w_up: bfloat16 [16, 2048, 768], P('ea', 'ga'), may hold values from -0.125 to 0.125
- w_down: bfloat16 [16, 768, 2048], P('ea', None, 'ga'), may hold values from -0.875 to 0.875
- routes: int32 [8192, 8], P(('ga', 'ea')), may hold values from 0 to 15, all different within a row; in each aligned block of 256 rows (0 to 255, 256 to 511, ...) at most 144 rows name the same one
- pic_starts: int32 [4, 4], P('ga'), may hold values from -1 to 1792, as said below
- cotangent: bfloat16 [8192, 2048], P(('ga', 'ea')), may hold values from -6 to 6
Outputs:
- layer_output: bfloat16 [8192, 2048], P(('ga', 'ea'))
- input_grad: bfloat16 [8192, 2048], P(('ga', 'ea'))
- w_query_grad: float32 [2048, 4096], P('ga')
- w_key_grad: float32 [2048, 512], P('ga')
- w_value_grad: float32 [2048, 512], P('ga')
- w_out_grad: float32 [4096, 2048], P('ga')
- attn_gain_grad: float32 [2048], P('ga')
- query_gain_grad: float32 [128], P('ga')
- key_gain_grad: float32 [128], P('ga')
- ffn_gain_grad: float32 [2048], P('ga')
- w_router_grad: float32 [2048, 16], P('ga')
- w_gate_grad: float32 [16, 2048, 768], P('ea', 'ga')
- w_up_grad: float32 [16, 2048, 768], P('ea', 'ga')
- w_down_grad: float32 [16, 768, 2048], P('ea', None, 'ga')
The draws below stay inside these ranges and needn't reach their ends.
Inputs may be any that keep to these rules, and one draw needn't show every extreme that they name: `routes`: each row names 8 different experts. In each aligned block of 256 rows (the rows of one device) no expert is named by more than 144 rows. `pic_starts`: row s lists the first positions of sequence s's picture pieces, each of 256 positions; entry j, if present, lies between j * 512 and (j + 1) * 512 - 256; present entries come first, at least one is present, and -1 marks an absent one.
All inputs are finite; a program needn't handle non-finite values.
Results may differ from the reference program's by a relative error of at most 0.025.
Values may be sent and summed in bfloat16 or wider, within the bound.
No kernel may reach another device: no remote copies, remote signals or barrier semaphores. Data moves between devices by JAX's collectives and lax.ppermute only.
A program may use at most 320 MiB of HBM per device.

```python
import math
import jax
import jax.numpy as jnp
import numpy as np
from jax import lax

D = 2048
HEADS = 32
KV = 4
HD = 128
FF = 768
TOP = 8
TOK_DEV = 256
PIC = 256
PICS = 4
QW = 4096
KVW = 512
EXPERTS = 16
SEQ_LEN = 2048
SEQS = 4
TOKENS = 8192
MOST = 144


def draw_pic_starts(key, part):
    key = jax.random.fold_in(key, 7)
    key_count, key_offset, key_pick = jax.random.split(key, 3)
    region = SEQ_LEN // PICS
    piece_count = jax.random.randint(key_count, (SEQS, 1), 1, PICS + 1)
    offsets = jax.random.randint(key_offset, (SEQS, PICS), 0, region - PIC + 1)
    rows = jnp.arange(SEQS, dtype=jnp.int32)[:, None]
    columns = jnp.arange(PICS, dtype=jnp.int32)[None, :]
    fullest = jax.random.randint(key_pick, (), 0, SEQS)
    sparse = (fullest + 1) % SEQS
    piece_count = jnp.where(rows == fullest, PICS, jnp.where(rows == sparse, 1, piece_count))
    offsets = jnp.where((rows == fullest) & (columns == PICS - 1), region - PIC, offsets)
    starts = columns * region + offsets
    return jnp.where(columns < piece_count, starts, -1).astype(jnp.int32)


def level_of(stream_key, extent, shards, low, top_value):
    level = 1.0
    for position, blocks in shards:
        heights = jax.random.uniform(jax.random.fold_in(jax.random.fold_in(stream_key, 6), position), (blocks,), jnp.float32, low / len(shards), top_value / len(shards))
        level = level * jnp.repeat(jnp.exp(heights), extent[position] // blocks).reshape((-1,) + (1,) * (len(extent) - 1 - position))
    return level


def assign_block(rng, own, number, rows, number_of, top, reach, lean):
    sequence = jax.random.permutation(rng, number_of)
    heavy_load, common = portions_of(number_of, rows * top, reach, lean, True), portions_of(number_of, rows * top, reach, lean, False)
    places = jnp.arange(number_of)

    def named(tallies, turn):
        used = int((tallies > 0).sum())
        fixed = max(1, used // 4)
        passed = fixed + (places - fixed + turn * (used - fixed)) % max(1, number_of - fixed)
        return jnp.zeros((number_of,), jnp.int32).at[sequence[jnp.where(places < fixed, places, passed)]].set(jnp.asarray(tallies, jnp.int32))

    tallies = jnp.where(number % 4 == 0, named(heavy_load, number // 4), named(common, number - number // 4 - 1))
    mixed = jax.random.permutation(jax.random.fold_in(own, 3), number_of)
    giver, receiver = mixed[0:number_of // 2 * 2:2], mixed[1:number_of // 2 * 2:2]
    slack = jnp.minimum(tallies[giver] - 1, reach - tallies[receiver]) // 2
    slack = jnp.where((giver == sequence[0]) | (receiver == sequence[0]) | (tallies[receiver] == 0), 0, jnp.maximum(slack, 0))
    passed = jax.random.randint(jax.random.fold_in(own, 4), (number_of // 2,), 0, 1 << 20) % (slack + 1)
    tallies = tallies.at[giver].add(-passed).at[receiver].add(passed)
    items = jnp.searchsorted(jnp.cumsum(tallies), jnp.arange(rows * top), side="right").astype(jnp.int32)
    grid = items.reshape(top, rows).T
    grid = grid[jax.random.permutation(jax.random.fold_in(own, 1), rows)]
    turn = jax.random.randint(jax.random.fold_in(own, 2), (rows, 1), 0, top)
    return jnp.take_along_axis(grid, (jnp.arange(top)[None, :] + turn) % top, axis=1)


def portions_of(count, total, bound, lean, full):
    weights = [(1 << 20) // math.isqrt(rank ** lean) + 1 for rank in range(1, count + 1)]
    largest = bound if full else min(bound, max(-(-total // count), total * weights[0] // sum(weights)))
    least = 1 if total - largest >= count - 1 else 0
    given, spare = [largest] + [least] * (count - 1), total - largest - least * (count - 1)
    while spare > 0:
        candidates = [i for i in range(1, count) if given[i] < largest] or [i for i in range(1, count) if given[i] < bound]
        mass, remaining = sum([weights[i] for i in candidates]), spare
        for i in candidates:
            more = min(bound - given[i], max(1, remaining * weights[i] // mass), spare)
            given[i] = given[i] + more
            spare = spare - more
    return np.array(given)


def normal_values(rng, extent, scale, reach, shards=(), held_as=jnp.bfloat16):
    values = jax.random.normal(rng, extent, jnp.float32) * scale
    if len(shards) > 0:
        values = level_of(rng, extent, shards, -0.22, 0.18) * values
    return jnp.clip(values, min=-reach, max=reach).astype(held_as)


def setup_inputs(seed: int = 0) -> dict:
    seeds = jax.random.split(jax.random.key(seed), 17)
    layer_input = normal_values(seeds[0], (TOKENS, D), 1.0, 6.0, ((0, 32),))
    w_query = normal_values(seeds[1], (D, QW), D ** -0.5, 0.125, ((0, 4),))
    w_key = normal_values(seeds[2], (D, KVW), D ** -0.5, 0.125, ((0, 4),))
    w_value = normal_values(seeds[3], (D, KVW), D ** -0.5, 0.125, ((0, 4),))
    w_out = normal_values(seeds[4], (QW, D), (QW // 128) ** -0.5, 1.0, ((0, 4),))
    attn_gain = jnp.clip(1.0 + 0.1 * jax.random.normal(seeds[5], (D,), jnp.float32), 0.5, 1.5).astype(jnp.bfloat16)
    query_gain = jnp.clip(1.0 + 0.1 * jax.random.normal(seeds[6], (HD,), jnp.float32), 0.5, 1.5).astype(jnp.bfloat16)
    key_gain = jnp.clip(1.0 + 0.1 * jax.random.normal(seeds[7], (HD,), jnp.float32), 0.5, 1.5).astype(jnp.bfloat16)
    ffn_gain = jnp.clip(1.0 + 0.1 * jax.random.normal(seeds[8], (D,), jnp.float32), 0.5, 1.5).astype(jnp.bfloat16)
    w_router = normal_values(seeds[9], (D, EXPERTS), (4 * D) ** -0.5, 0.0625, ((0, 4),))
    w_gate = normal_values(seeds[10], (EXPERTS, D, FF), D ** -0.5, 0.125, ((0, 8), (1, 4)))
    w_up = normal_values(seeds[11], (EXPERTS, D, FF), D ** -0.5, 0.125, ((0, 8), (1, 4)))
    w_down = normal_values(seeds[12], (EXPERTS, FF, D), (FF // 16) ** -0.5, 0.875, ((0, 8), (2, 4)))
    routes_keys = jax.random.split(jax.random.fold_in(seeds[13], 1), TOKENS // TOK_DEV)
    routes_turns = jax.random.permutation(jax.random.fold_in(seeds[13], 3), TOKENS // TOK_DEV)
    routes = jax.vmap(lambda own, number: assign_block(jax.random.fold_in(seeds[13], 2), own, number, TOK_DEV, EXPERTS, TOP, MOST, 1))(routes_keys, routes_turns).reshape((TOKENS, TOP))
    pic_starts = draw_pic_starts(jax.random.fold_in(seeds[16], 71), 0)
    cotangent = normal_values(seeds[15], (TOKENS, D), 1.0, 6.0, ((0, 32),))
    return dict(layer_input=layer_input, w_query=w_query, w_key=w_key, w_value=w_value, w_out=w_out, attn_gain=attn_gain, query_gain=query_gain, key_gain=key_gain, ffn_gain=ffn_gain, w_router=w_router, w_gate=w_gate, w_up=w_up, w_down=w_down, routes=routes, pic_starts=pic_starts, cotangent=cotangent)


NORM_EPS = 1e-06
ROPE_THETA = 1000000.0
MASKED_SCORE = -1e+30
PRECISE = lax.Precision.HIGHEST

@jax.custom_vjp
def low(v):
    return lax.optimization_barrier(v.astype(jnp.bfloat16)).astype(jnp.float32)

@jax.custom_vjp
def low_back(v):
    return v

def low_keep(v):
    return (low(v), None)

def low_pass(kept, grad):
    return (grad,)

def back_keep(v):
    return (v, None)

def back_low(kept, grad):
    return (low(grad),)
low.defvjp(low_keep, low_pass)
low_back.defvjp(back_keep, back_low)

def rms_norm(values, norm_gain):
    inverse = lax.rsqrt(lax.optimization_barrier(jnp.mean(values * values, axis=-1, keepdims=True)) + NORM_EPS)
    return values * inverse * norm_gain

def rotate(values, positions):
    half_dim = values.shape[-1] // 2
    frequency = ROPE_THETA ** (-jnp.arange(half_dim, dtype=jnp.float32) * 2.0 / values.shape[-1])
    angles = positions.astype(jnp.float32)[:, None] * frequency[None, :]
    cosine = jnp.cos(angles)[:, None, :]
    sine_part = jnp.sin(angles)[:, None, :]
    first_half = values[..., :half_dim]
    second_half = values[..., half_dim:]
    return jnp.concatenate([first_half * cosine - second_half * sine_part, second_half * cosine + first_half * sine_part], axis=-1)

def swiglu(gate_pre, up_pre):
    return gate_pre / (1.0 + jnp.exp(-gate_pre)) * up_pre

def softmax_last(scores):
    row_peak = lax.optimization_barrier(jnp.max(scores, axis=-1, keepdims=True))
    weights = jnp.exp(scores - row_peak)
    return weights / lax.optimization_barrier(jnp.sum(weights, axis=-1, keepdims=True))

def piece_ids(starts, positions):
    inside = (starts[:, None] >= 0) & (positions[None, :] >= starts[:, None]) & (positions[None, :] < starts[:, None] + PIC)
    labels = jnp.arange(1, starts.shape[0] + 1, dtype=jnp.int32)[:, None]
    return lax.optimization_barrier(jnp.sum(jnp.where(inside, labels, 0), axis=0)).astype(jnp.int32)

def allowed_mask(starts, query_pos, key_pos):
    query_piece = piece_ids(starts, query_pos)
    key_piece = piece_ids(starts, key_pos)
    causal = key_pos[None, :] <= query_pos[:, None]
    shared = (query_piece[:, None] == key_piece[None, :]) & (query_piece[:, None] > 0)
    return causal | shared

def slot_tables(routes):
    blocks = TOKENS // TOK_DEV
    route_count = TOK_DEV * TOP
    block_routes = routes.reshape(blocks, route_count).astype(jnp.int32)
    onehot = (block_routes[:, :, None] == jnp.arange(EXPERTS, dtype=jnp.int32)[None, None, :]).astype(jnp.int32)
    slot_rank = lax.optimization_barrier(jnp.sum((jnp.cumsum(onehot, axis=1).astype(jnp.int32) - onehot) * onehot, axis=2)).astype(jnp.int32)
    block_ids = jnp.arange(blocks, dtype=jnp.int32)[:, None]
    columns = (block_ids * MOST + slot_rank).reshape(-1).astype(jnp.int32)
    token_ids = (block_ids * TOK_DEV + jnp.arange(route_count, dtype=jnp.int32)[None, :] // TOP).reshape(-1).astype(jnp.int32)
    expert_ids = block_routes.reshape(-1)
    token_table = jnp.zeros((EXPERTS, blocks * MOST), jnp.int32).at[expert_ids, columns].set(token_ids)
    slot_live = jnp.zeros((EXPERTS, blocks * MOST), jnp.float32).at[expert_ids, columns].set(1.0)
    return (token_table, slot_live)

def attend_sequence(operands):
    queries, keys, values, starts = operands
    positions = jnp.arange(SEQ_LEN, dtype=jnp.int32)
    allowed = allowed_mask(starts, positions, positions)
    scores = jnp.einsum('qcgh,kch->cgqk', queries, keys, precision=PRECISE) * HD ** (-0.5)
    scores = jnp.where(allowed[None, None], low_back(scores), MASKED_SCORE)
    attn_probs = low(softmax_last(scores))
    return jnp.einsum('cgqk,kch->qcgh', attn_probs, values, precision=PRECISE).reshape(SEQ_LEN, HEADS * HD)

def layer(layer_input, w_query, w_key, w_value, w_out, attn_gain, query_gain, key_gain, ffn_gain, w_router, w_gate, w_up, w_down, routes, pic_starts, token_table, slot_live):
    group_size = HEADS // KV
    positions = (jnp.arange(TOKENS, dtype=jnp.int32) % SEQ_LEN).astype(jnp.int32)
    normed = low(rms_norm(layer_input, attn_gain))
    q_raw = low_back(jnp.dot(normed, w_query, precision=PRECISE)).reshape(TOKENS, HEADS, HD)
    k_raw = low_back(jnp.dot(normed, w_key, precision=PRECISE)).reshape(TOKENS, KV, HD)
    values = low_back(low(jnp.dot(normed, w_value, precision=PRECISE))).reshape(SEQS, SEQ_LEN, KV, HD)
    queries = low_back(low(rotate(rms_norm(q_raw, query_gain), positions))).reshape(SEQS, SEQ_LEN, KV, group_size, HD)
    keys = low_back(low(rotate(rms_norm(k_raw, key_gain), positions))).reshape(SEQS, SEQ_LEN, KV, HD)
    attended = lax.map(jax.checkpoint(attend_sequence), (queries, keys, values, pic_starts))
    attended = low_back(low(attended.reshape(TOKENS, HEADS * HD)))
    hidden = layer_input + low_back(jnp.dot(attended, w_out, precision=PRECISE))
    ffn_in = low(rms_norm(hidden, ffn_gain))
    logits = jnp.dot(ffn_in, w_router, precision=PRECISE)
    gates = softmax_last(jnp.take_along_axis(logits, routes, axis=1))
    picks = (routes[:, :, None] == jnp.arange(EXPERTS, dtype=jnp.int32)[None, None, :]).astype(jnp.float32)
    gate_table = jnp.einsum('tk,tke->et', gates, picks, precision=PRECISE)

    def expert_step(mixture, operands):
        gate_weight, up_weight, down_weight, tokens_of, live, gate_column = operands
        rows = low_back(ffn_in[tokens_of]) * live[:, None]
        gate_pre = low_back(jnp.dot(rows, gate_weight, precision=PRECISE))
        up_pre = low_back(jnp.dot(rows, up_weight, precision=PRECISE))
        act = low(swiglu(gate_pre, up_pre))
        expert_out = low_back(low(jnp.dot(act, down_weight, precision=PRECISE)))
        route_weight = gate_column[tokens_of] * live
        return (mixture.at[tokens_of].add(route_weight[:, None] * expert_out), None)
    start = jnp.zeros((TOKENS, D), jnp.float32)
    mixture, unused = lax.scan(jax.checkpoint(expert_step), start, (w_gate, w_up, w_down, token_table, slot_live, gate_table))
    return hidden + mixture

def reference(layer_input, w_query, w_key, w_value, w_out, attn_gain, query_gain, key_gain, ffn_gain, w_router, w_gate, w_up, w_down, routes, pic_starts, cotangent):
    token_table, slot_live = slot_tables(routes)
    floats = tuple((array.astype(jnp.float32) for array in (layer_input, w_query, w_key, w_value, w_out, attn_gain, query_gain, key_gain, ffn_gain, w_router, w_gate, w_up, w_down)))

    def forward(*operands):
        return layer(*operands, routes, pic_starts, token_table, slot_live)
    output, pullback = jax.vjp(forward, *floats)
    grads = pullback(cotangent.astype(jnp.float32))
    return (output.astype(jnp.bfloat16), grads[0].astype(jnp.bfloat16), grads[1], grads[2], grads[3], grads[4], grads[5], grads[6], grads[7], grads[8], grads[9], grads[10], grads[11], grads[12])
```

```python
import functools

import jax
import jax.numpy as jnp
from jax import lax
from jax.experimental import pallas as pl
from jax.experimental.pallas import tpu as pltpu
from jax.sharding import Mesh
from jax.sharding import PartitionSpec as P

HEADS = 32
KV = 4
HD = 128
PIC = 256


NORM_EPS = 1e-06
ROPE_THETA = 1000000.0
MASKED_SCORE = -1e30
PRECISE = lax.Precision.HIGHEST
F32 = jnp.float32
BF16 = jnp.bfloat16
EXTRA = 128
LOG2E = 1.4426950408889634
VMEM = 56 << 20


def rms_norm(values, norm_gain):
    inverse = lax.rsqrt(jnp.mean(values * values, axis=-1, keepdims=True) + NORM_EPS)
    return values * inverse * norm_gain


def piece_ids(starts, positions):
    inside = (
        (starts[:, None] >= 0)
        & (positions[None, :] >= starts[:, None])
        & (positions[None, :] < starts[:, None] + PIC)
    )
    labels = jnp.arange(1, starts.shape[0] + 1, dtype=jnp.int32)[:, None]
    return jnp.sum(jnp.where(inside, labels, 0), axis=0)


def allowed_mask(starts, query_pos, key_pos):
    query_piece = piece_ids(starts, query_pos)
    key_piece = piece_ids(starts, key_pos)
    causal = key_pos[None, :] <= query_pos[:, None]
    shared = (query_piece[:, None] == key_piece[None, :]) & (query_piece[:, None] > 0)
    return causal | shared


def dot_nn(left, right):
    return lax.dot_general(left, right, (((1,), (0,)), ((), ())), preferred_element_type=F32)


def dot_tn(left, right):
    return lax.dot_general(left, right, (((0,), (0,)), ((), ())), preferred_element_type=F32)


def dot_nt(left, right):
    return lax.dot_general(left, right, (((1,), (1,)), ((), ())), preferred_element_type=F32)


def after(value, *others):
    return lax.optimization_barrier((value,) + others)[0]


def swap_core(value):
    return lax.ppermute(value, "core", [(0, 1), (1, 0)])


def swap_axis(value, axis, bit):
    return lax.ppermute(value, axis, [(i, i ^ bit) for i in range(lax.axis_size(axis))])


def plus(*terms):
    total = terms[0].astype(F32)
    for term in terms[1:]:
        total = total + term.astype(F32)
    return total.astype(BF16)


def line_gather(value, before=None, steps=None):
    count = lax.axis_size("z")
    place = lax.axis_index("z")
    below, above = {}, {}
    up = down = value
    for step in range(1, count):
        if before and step in before:
            up, down = lax.optimization_barrier((up, down) + tuple(before[step]))[:2]
        up = lax.ppermute(up, "z", [(p, p + 1) for p in range(step - 1, count - 1)])
        down = lax.ppermute(down, "z", [(p, p - 1) for p in range(1, count - step + 1)])
        up, down = lax.optimization_barrier((up, down))
        below[step], above[step] = up, down
        if steps is not None:
            steps.append((up, down))
    return [value] + [
        jnp.where(place >= step, below[step], above[count - step]) for step in range(1, count)
    ]


class LineSum:
    def __init__(self, slots):
        self.slots, self.done = slots, 0

    def step(self, *before):
        count = lax.axis_size("z")
        self.done += 1
        up, down = self.slots[self.done], self.slots[count - self.done]
        if self.done > 1:
            up, down = plus(up, self.held[0]), plus(down, self.held[1])
        if before:
            up, down = lax.optimization_barrier((up, down) + before)[:2]
        up = lax.ppermute(up, "z", [(p, p + 1) for p in range(self.done)])
        down = lax.ppermute(
            down, "z", [(p, p - 1) for p in range(count - 1, count - 1 - self.done, -1)]
        )
        self.held = lax.optimization_barrier((up, down))
        return self.held

    def result(self):
        while self.done < lax.axis_size("z") - 1:
            self.step()
        return plus(self.slots[0], *self.held)


def ea_gather(value, before=None):
    mine = jnp.concatenate(line_gather(value, before))
    return mine, swap_core(mine)


def core_slots(mine, other):
    got = swap_core(other)
    return [plus(mine[s], got[s]) for s in range(lax.axis_size("z"))]


def z_all_sum(value):
    return lax.psum(value, "z")


def z_all_sum_small(value):
    count = lax.axis_size("z")
    place = lax.axis_index("z")
    bits, bit = [], 1
    while bit < count:
        rows = value.shape[0] // 2
        upper = (place // bit) % 2
        keep = lax.dynamic_slice_in_dim(value, upper * rows, rows, 0)
        send = lax.dynamic_slice_in_dim(value, (1 - upper) * rows, rows, 0)
        value = plus(keep, swap_axis(send, "z", bit))
        bits.append(bit)
        bit *= 2
    for bit in reversed(bits):
        got = swap_axis(value, "z", bit)
        upper = (place // bit) % 2
        low, high = jnp.where(upper == 0, value, got), jnp.where(upper == 0, got, value)
        value = jnp.concatenate([low, high])
    return value


def ga_order():
    return lax.axis_index("ga") ^ jnp.arange(lax.axis_size("ga"))


def ga_first_hop(value):
    if lax.axis_size("ga") != 4:
        whole = lax.all_gather(value, "ga", axis=0)
        return [jnp.take(whole, ga_order(), axis=0).reshape((-1,) + value.shape[1:])]
    return [value, swap_axis(value, "ga", 1), swap_axis(value, "ga", 2)]


def ga_second_hop(first, part, parts, before):
    if len(first) == 1:
        return []
    half = first[0].shape[0] // 2
    rows = half // parts
    to_y = first[1][part * rows : (part + 1) * rows]
    to_x = first[2][half + part * rows : half + (part + 1) * rows]
    to_y, to_x = lax.optimization_barrier((to_y, to_x) + tuple(before))[:2]
    return [swap_axis(to_y, "ga", 2), swap_axis(to_x, "ga", 1)]


def shard_list(first, seconds, shape):
    if len(first) == 1:
        blocks = jnp.take(first[0].reshape((-1,) + shape), ga_order(), axis=0)
        blocks = blocks.reshape((4, -1) + shape).swapaxes(1, 2)
        blocks = blocks.reshape(4, shape[0], -1, shape[2])
        return [blocks[q] for q in range(4)], jnp.arange(4, dtype=jnp.int32)
    across = [hop[0] for hop in seconds] + [hop[1] for hop in seconds]
    blocks = first + [jnp.concatenate(across)]
    return [block.reshape(shape) for block in blocks], ga_order().astype(jnp.int32)


def ga_sum_first(value):
    if lax.axis_size("ga") != 4:
        return (value,)
    rows = value.shape[0] // 4
    half = rows // 2
    own, for_x, for_y = [value[r * rows : (r + 1) * rows] for r in range(3)]
    low = swap_axis(value[3 * rows : 3 * rows + half], "ga", 1)
    high = swap_axis(value[3 * rows + half :], "ga", 2)
    to_x = jnp.concatenate([for_x[:half], plus(for_x[half:], high)])
    to_y = jnp.concatenate([plus(for_y[:half], low), for_y[half:]])
    return own, to_x, to_y


def ga_sum_second(parts):
    if len(parts) == 1:
        return ga_sum_whole(parts[0])
    own, to_x, to_y = parts
    return plus(own, swap_axis(to_x, "ga", 1), swap_axis(to_y, "ga", 2))


def ga_sum_whole(value):
    blocks = value.reshape((lax.axis_size("ga"), -1) + value.shape[1:])
    blocks = jnp.take(blocks, ga_order(), axis=0).reshape(value.shape)
    return lax.psum_scatter(blocks, "ga", scatter_dimension=0, tiled=True)


def ga_gather_small(value):
    count = lax.axis_size("ga")
    held, bit = value[None], 1
    while bit < count:
        held = jnp.concatenate([held, swap_axis(held, "ga", bit)])
        bit *= 2
    return jnp.take(held, ga_order(), axis=0)


def sum_small(rows):
    total = rows + swap_core(rows)
    count, bit = lax.axis_size("z"), 1
    while bit < count:
        total = total + swap_axis(total, "z", bit)
        bit *= 2
    count = lax.axis_size("ga")
    total = jnp.take(total, ga_order(), axis=0)
    while count > 1:
        count //= 2
        total = total[:count] + swap_axis(total[count:], "ga", count)
    return total[0]


def core_halves(value):
    core = lax.axis_index("core")
    rows = value.shape[0] // 2
    return (
        lax.dynamic_slice_in_dim(value, core * rows, rows, 0),
        lax.dynamic_slice_in_dim(value, (1 - core) * rows, rows, 0),
    )


def dense_other(mine, other_half):
    if len(mine) == 1:
        return [swap_core(mine[0])]
    return [other_half] + [swap_core(piece) for piece in mine[1:]]


def split_cols(value, half):
    groups = lax.axis_size("ga")
    width = value.shape[1] // groups // 2
    order = ga_order()
    return jnp.concatenate(
        [
            lax.dynamic_slice_in_dim(value, (order[r] * 2 + half) * width, width, 1)
            for r in range(groups)
        ],
        axis=1,
    )


def join_cols(mine, other):
    groups = lax.axis_size("ga")
    core = lax.axis_index("core")
    width = mine.shape[1] // groups
    order = ga_order()
    parts = []
    for g in range(groups):
        a = lax.dynamic_slice_in_dim(mine, order[g] * width, width, 1)
        b = lax.dynamic_slice_in_dim(other, order[g] * width, width, 1)
        parts += [jnp.where(core == 0, a, b), jnp.where(core == 0, b, a)]
    return jnp.concatenate(parts, axis=1)


def core_sum(mine, other):
    return plus(mine, swap_core(other))


def whole_shard(share):
    core = lax.axis_index("core")
    other_share = swap_core(share)
    low = jnp.where(core == 0, share, other_share)
    high = jnp.where(core == 0, other_share, share)
    return jnp.concatenate([low, high], axis=0).astype(F32)


def cost(micros):
    return pl.CostEstimate(flops=micros * 10**9, bytes_accessed=1024, transcendentals=0)


def pieces_kernel(plan, *refs):
    acc = None
    lefts, out_ref = refs[: 1 + max(which for which, _, _ in plan)], refs[-1]
    for (which, at, size), ref in zip(plan, refs[len(lefts) : -1]):
        term = dot_nn(lefts[which][:, at : at + size], ref[...])
        acc = term if acc is None else acc + term
    out_ref[...] = acc


def pieces_matmul(lefts, piece_lists):
    plan, pieces = [], []
    for which, some in enumerate(piece_lists):
        at = 0
        for piece in some:
            plan.append((which, at, piece.shape[0]))
            pieces.append(piece)
            at += piece.shape[0]
    rows, width = lefts[0].shape[0], pieces[0].shape[1]
    tile = min(1024 if width > 4096 else 512, width)
    return pl.pallas_call(
        functools.partial(pieces_kernel, plan),
        grid=(width // tile,),
        in_specs=[pl.BlockSpec(left.shape, lambda n: (0, 0)) for left in lefts]
        + [pl.BlockSpec((piece.shape[0], tile), lambda n: (0, n)) for piece in pieces],
        out_specs=pl.BlockSpec((rows, tile), lambda n: (0, n)),
        out_shape=jax.ShapeDtypeStruct((rows, width), F32),
        compiler_params=pltpu.CompilerParams(vmem_limit_bytes=VMEM),
        cost_estimate=cost(6),
        name="dense_matmul",
    )(*lefts, *pieces)


def pieces_back_kernel(sizes, left_ref, *refs):
    n = pl.program_id(0)
    out_ref, acc = refs[-2:]

    @pl.when(n == 0)
    def _():
        acc[...] = jnp.zeros_like(acc)

    at = 0
    for ref, size in zip(refs[:-2], sizes):
        acc[:, at : at + size] += dot_nt(left_ref[...], ref[...])
        at += size

    @pl.when(n == pl.num_programs(0) - 1)
    def _():
        out_ref[...] = acc[...].astype(out_ref.dtype)


def pieces_back(left, pieces, dtype):
    rows, width = left.shape
    tile = min(512, width)
    sizes = [piece.shape[0] for piece in pieces]
    return pl.pallas_call(
        functools.partial(pieces_back_kernel, sizes),
        grid=(width // tile,),
        in_specs=[pl.BlockSpec((rows, tile), lambda n: (0, n))]
        + [pl.BlockSpec((size, tile), lambda n: (0, n)) for size in sizes],
        out_specs=pl.BlockSpec((rows, sum(sizes)), lambda n: (0, 0)),
        out_shape=jax.ShapeDtypeStruct((rows, sum(sizes)), dtype),
        scratch_shapes=[pltpu.VMEM((rows, sum(sizes)), F32)],
        compiler_params=pltpu.CompilerParams(vmem_limit_bytes=VMEM),
        cost_estimate=cost(6),
        name="dense_back",
    )(left, *pieces)


def prep_head(raw, gain, cosine, sine):
    inverse = lax.rsqrt(jnp.mean(raw * raw, axis=-1, keepdims=True) + NORM_EPS)
    scaled = raw * inverse * gain
    turned = scaled * cosine + pltpu.roll(scaled, HD // 2, 1) * sine
    return turned.astype(BF16), inverse


def head_cols(index):
    return pl.ds(pl.multiple_of(index * HD, HD), HD)


def prep_kv_kernel(raw_ref, cos_ref, sin_ref, gain_ref, out_ref):
    for h in range(KV):
        span = slice(h * HD, (h + 1) * HD)
        keys, _ = prep_head(raw_ref[:, span], gain_ref[...], cos_ref[...], sin_ref[...])
        out_ref[:, span] = keys
    out_ref[:, KV * HD :] = raw_ref[:, KV * HD :].astype(BF16)


def prep_kv(raw, cosine, sine, gain):
    rows, width = raw.shape[0], 2 * KV * HD
    whole = lambda a: pl.BlockSpec(a.shape, lambda i: (0, 0))
    return pl.pallas_call(
        prep_kv_kernel,
        grid=(1,),
        in_specs=[
            pl.BlockSpec((rows, width), lambda i: (0, raw.shape[1] // width - 1)),
            whole(cosine),
            whole(sine),
            whole(gain),
        ],
        out_specs=pl.BlockSpec((rows, width), lambda i: (0, 0)),
        out_shape=jax.ShapeDtypeStruct((rows, width), BF16),
        compiler_params=pltpu.CompilerParams(vmem_limit_bytes=VMEM),
        cost_estimate=cost(1),
        name="prep_kv",
    )(raw, cosine, sine, gain)


def head_back(raw, inverse, grad, gain, cosine, sine):
    scaled_grad = grad * cosine + pltpu.roll(grad * sine, HD // 2, 1)
    unit = raw * inverse
    gain_grad = jnp.sum(scaled_grad * unit, axis=0, keepdims=True)
    unit_grad = scaled_grad * gain
    mean = jnp.mean(unit_grad * unit, axis=-1, keepdims=True)
    return inverse * (unit_grad - unit * mean), gain_grad


def kv_back_kernel(raw_ref, grad_ref, cos_ref, sin_ref, gain_ref, out_ref, gain_grad_ref):
    total = jnp.zeros((1, HD), F32)
    for h in range(KV):
        span = slice(h * HD, (h + 1) * HD)
        raw = raw_ref[:, span]
        cosine, sine, gain = cos_ref[...], sin_ref[...], gain_ref[...]
        _, inverse = prep_head(raw, gain, cosine, sine)
        grad = grad_ref[:, 2 * h * HD : (2 * h + 1) * HD].astype(F32)
        raw_grad, gain_grad = head_back(raw, inverse, grad, gain, cosine, sine)
        out_ref[:, span] = raw_grad.astype(BF16)
        out_ref[:, (KV + h) * HD : (KV + h + 1) * HD] = grad_ref[
            :, (2 * h + 1) * HD : (2 * h + 2) * HD
        ]
        total = total + gain_grad
    gain_grad_ref[...] = jnp.broadcast_to(total, gain_grad_ref.shape)


def kv_back(raw, grad, cosine, sine, gain):
    rows, width = raw.shape[0], 2 * KV * HD
    whole = lambda a: pl.BlockSpec(a.shape, lambda i: (0, 0))
    return pl.pallas_call(
        kv_back_kernel,
        grid=(1,),
        in_specs=[
            pl.BlockSpec((rows, width), lambda i: (0, raw.shape[1] // width - 1)),
            whole(grad),
            whole(cosine),
            whole(sine),
            whole(gain),
        ],
        out_specs=[
            pl.BlockSpec((rows, width), lambda i: (0, 0)),
            pl.BlockSpec((8, HD), lambda i: (0, 0)),
        ],
        out_shape=[
            jax.ShapeDtypeStruct((rows, width), BF16),
            jax.ShapeDtypeStruct((8, HD), F32),
        ],
        compiler_params=pltpu.CompilerParams(vmem_limit_bytes=VMEM),
        cost_estimate=cost(1),
        name="kv_back",
    )(raw, grad, cosine, sine, gain)


def attend_kernel(
    place,
    raw_ref,
    key_a,
    key_b,
    value_a,
    value_b,
    bias_ref,
    cos_ref,
    sin_ref,
    gain_ref,
    mine_ref,
    other_ref,
    log_ref,
):
    half = key_a.shape[0]
    chunk = min(512, half)
    to_log2 = LOG2E * HD**-0.5
    count = raw_ref.shape[1] // HD

    def one_head(at_head, out_ref, column):
        head = place[KV + at_head]
        query, _ = prep_head(
            raw_ref[:, head_cols(head)], gain_ref[...], cos_ref[...], sin_ref[...]
        )
        total = jnp.zeros((query.shape[0], 1), F32)
        acc = jnp.zeros(query.shape, F32)
        for side, (key_ref, value_ref) in enumerate(((key_a, value_a), (key_b, value_b))):
            for at in range(0, half, chunk):
                scores = dot_nt(query, key_ref[at : at + chunk, :])
                first = side * half + at
                weights = jnp.exp2(scores * to_log2 + bias_ref[:, first : first + chunk])
                total = total + jnp.sum(weights, axis=1, keepdims=True)
                acc = acc + dot_nn(weights.astype(BF16), value_ref[at : at + chunk, :])
        out_ref[:, head_cols(column)] = (acc / total).astype(BF16)
        logs = jnp.transpose(jnp.broadcast_to(jnp.log2(total), query.shape))
        log_ref[0, pl.ds(at_head, 1), :] = logs[0:1, :]

    @pl.loop(0, count // 2)
    def _(i):
        one_head(i, mine_ref, i)
        one_head(count // 2 + i, other_ref, i)


def attend_specs(rows, group, half, tables):
    whole = lambda h, place: (0, 0)
    side = lambda first: pl.BlockSpec((half, HD), lambda h, place: (0, first + h))
    return [
        pl.BlockSpec((rows, group), lambda h, place: (0, h)),
        side(0),
        side(0),
        side(KV),
        side(KV),
    ] + [pl.BlockSpec(t.shape, whole) for t in tables]


def attend(place, raw, kv_mine, kv_other, bias, cosine, sine, gain):
    rows = raw.shape[0]
    group = HEADS * HD // KV
    half = kv_mine.shape[0]
    tables = (bias, cosine, sine, gain)
    half_spec = pl.BlockSpec((rows, group // 2), lambda h, place: (0, place[h]))
    return pl.pallas_call(
        attend_kernel,
        grid_spec=pltpu.PrefetchScalarGridSpec(
            num_scalar_prefetch=1,
            grid=(KV,),
            in_specs=attend_specs(rows, group, half, tables),
            out_specs=[
                half_spec,
                half_spec,
                pl.BlockSpec((1, HEADS // KV, rows), lambda h, place: (h, 0, 0)),
            ],
        ),
        out_shape=[
            jax.ShapeDtypeStruct((rows, HEADS * HD // 2), BF16),
            jax.ShapeDtypeStruct((rows, HEADS * HD // 2), BF16),
            jax.ShapeDtypeStruct((KV, HEADS // KV, rows), F32),
        ],
        compiler_params=pltpu.CompilerParams(vmem_limit_bytes=VMEM),
        cost_estimate=cost(18),
        name="attend",
    )(place, raw, kv_mine, kv_other, kv_mine, kv_other, *tables)


def attend_back_kernel(
    place,
    raw_ref,
    key_a,
    key_b,
    value_a,
    value_b,
    bias_ref,
    cos_ref,
    sin_ref,
    gain_ref,
    grad_mine,
    grad_other,
    out_mine,
    out_other,
    log_ref,
    raw_grad_ref,
    kv_grad_ref,
    gain_grad_ref,
    key_acc,
    value_acc,
):
    h = pl.program_id(0)
    half = key_a.shape[0]
    chunk = min(512, half)
    scale = HD**-0.5
    to_log2 = LOG2E * scale
    count = raw_ref.shape[1] // HD
    key_acc[...] = jnp.zeros_like(key_acc)
    value_acc[...] = jnp.zeros_like(value_acc)

    @pl.when(h == 0)
    def _():
        gain_grad_ref[...] = jnp.zeros_like(gain_grad_ref)

    def one_head(at_head, grad_ref, out_ref, column):
        head = place[KV + at_head]
        raw = raw_ref[:, head_cols(head)]
        cosine, sine, gain = cos_ref[...], sin_ref[...], gain_ref[...]
        query, inverse = prep_head(raw, gain, cosine, sine)
        grad = grad_ref[:, head_cols(column)]
        product = grad.astype(F32) * out_ref[:, head_cols(column)].astype(F32)
        inner = jnp.sum(jnp.transpose(product), axis=0, keepdims=True)
        logs = log_ref[0, pl.ds(at_head, 1), :]
        query_grad = jnp.zeros(query.shape, F32)
        for side, (key_ref, value_ref) in enumerate(((key_a, value_a), (key_b, value_b))):
            for at in range(0, half, chunk):
                keys = key_ref[at : at + chunk, :]
                first = side * half + at
                span = slice(first, first + chunk)
                scores = dot_nt(keys, query)
                probs = jnp.exp2(scores * to_log2 + bias_ref[span, :] - logs)
                prob_grad = dot_nt(value_ref[at : at + chunk, :], grad)
                score_grad = (probs * (prob_grad - inner)).astype(BF16)
                value_acc[span, :] += dot_nn(probs.astype(BF16), grad)
                key_acc[span, :] += dot_nn(score_grad, query)
                query_grad = query_grad + dot_tn(score_grad, keys)
        query_grad = (query_grad * scale).astype(BF16).astype(F32)
        raw_grad, gain_grad = head_back(raw, inverse, query_grad, gain, cosine, sine)
        gain_grad_ref[0:1, :] += gain_grad
        raw_grad_ref[:, head_cols(head)] = raw_grad.astype(BF16)

    @pl.loop(0, count // 2)
    def _(i):
        one_head(i, grad_mine, out_mine, i)
        one_head(count // 2 + i, grad_other, out_other, i)

    heads = kv_grad_ref.shape[1] // HD // 2
    kv_grad_ref[:, head_cols(h)] = (key_acc[...] * scale).astype(BF16)
    kv_grad_ref[:, head_cols(heads + h)] = value_acc[...].astype(BF16)


def attend_back(
    first, count, place, raw, kv_mine, kv_other, bias, cosine, sine, gain, grad, outs, logs
):
    rows = raw.shape[0]
    group = HEADS * HD // KV
    half = kv_mine.shape[0]
    tables = (bias, cosine, sine, gain)
    half_spec = pl.BlockSpec((rows, group // 2), lambda h, place: (0, place[first + h]))
    other_spec = pl.BlockSpec((rows, group // 2), lambda h, place: (0, KV + place[first + h]))
    whole = lambda h, place: (0, 0)
    side = lambda at: pl.BlockSpec((half, HD), lambda h, place: (0, at + first + h))
    return pl.pallas_call(
        attend_back_kernel,
        grid_spec=pltpu.PrefetchScalarGridSpec(
            num_scalar_prefetch=1,
            grid=(count,),
            in_specs=[
                pl.BlockSpec((rows, group), lambda h, place: (0, first + h)),
                side(0),
                side(0),
                side(KV),
                side(KV),
            ]
            + [pl.BlockSpec(t.shape, whole) for t in tables]
            + [half_spec, other_spec, half_spec, half_spec]
            + [pl.BlockSpec((1,) + logs.shape[1:], lambda h, place: (first + h, 0, 0))],
            out_specs=[
                pl.BlockSpec((rows, group), lambda h, place: (0, h)),
                pl.BlockSpec((2 * half, 2 * count * HD), whole),
                pl.BlockSpec((8, HD), whole),
            ],
            scratch_shapes=[pltpu.VMEM((2 * half, HD), F32), pltpu.VMEM((2 * half, HD), F32)],
        ),
        out_shape=[
            jax.ShapeDtypeStruct((rows, count * group), BF16),
            jax.ShapeDtypeStruct((2 * half, 2 * count * HD), BF16),
            jax.ShapeDtypeStruct((8, HD), F32),
        ],
        compiler_params=pltpu.CompilerParams(vmem_limit_bytes=VMEM),
        cost_estimate=cost(9),
        name="attend_back",
    )(place, raw, kv_mine, kv_other, kv_mine, kv_other, *tables, grad, grad, *outs, logs)


def pick_rows(spot_row, cap):
    places = lax.broadcasted_iota(jnp.int32, (cap, spot_row.shape[1]), 0)
    return jnp.where(places == spot_row, 1.0, 0.0).astype(BF16)


def put_rows(spot_col, cap):
    places = lax.broadcasted_iota(jnp.int32, (spot_col.shape[0], cap), 1)
    return jnp.where(places == spot_col, 1.0, 0.0).astype(BF16)


def pick_kernel(cap, rows_ref, spot_ref, out_ref):
    block = spot_ref.shape[2]
    for e in range(spot_ref.shape[0]):
        for b in range(spot_ref.shape[1]):
            pick = pick_rows(spot_ref[e, b : b + 1, :], cap)
            rows = rows_ref[b * block : (b + 1) * block, :]
            out_ref[e, b * cap : (b + 1) * cap, :] = dot_nn(pick, rows).astype(BF16)


def pick(rows, spots, cap, width):
    experts, blocks, block = spots.shape
    tile = min(512, width)
    return pl.pallas_call(
        functools.partial(pick_kernel, cap),
        grid=(width // tile,),
        in_specs=[
            pl.BlockSpec((blocks * block, tile), lambda n: (0, n)),
            pl.BlockSpec(spots.shape, lambda n: (0, 0, 0)),
        ],
        out_specs=pl.BlockSpec((experts, blocks * cap, tile), lambda n: (0, 0, n)),
        out_shape=jax.ShapeDtypeStruct((experts, blocks * cap, width), BF16),
        compiler_params=pltpu.CompilerParams(vmem_limit_bytes=VMEM),
        cost_estimate=cost(3),
        name="pick",
    )(rows, spots)


def expert_kernel(
    cap,
    first_ref,
    rows_ref,
    spot_ref,
    mark_ref,
    cot_ref,
    router_ref,
    *refs,
):
    weight_refs = refs[:-5]
    row_out, act_out, pre_out, extra_out, acc = refs[-5:]
    _, depth, all_ff = weight_refs[0].shape
    ff = all_ff // 3
    experts = first_ref[1]
    block = spot_ref.shape[2]
    blocks = spot_ref.shape[1]
    marks = []
    for b in range(blocks):
        pick = pick_rows(spot_ref[0, b : b + 1, :], cap)
        span = slice(b * block, (b + 1) * block)
        row_out[0, b * cap : (b + 1) * cap, :] = dot_nn(pick, rows_ref[span, :]).astype(BF16)
        marks.append(dot_nn(pick, mark_ref[span, :]))
    marked = jnp.concatenate(marks, axis=0) > 0.5
    rows = row_out[0]
    logits = dot_nn(rows, router_ref[...])
    peak = jnp.max(jnp.where(marked, logits, MASKED_SCORE), axis=1, keepdims=True)
    weights = jnp.where(marked, jnp.exp(jnp.where(marked, logits - peak, 0.0)), 0.0)
    lanes = lax.broadcasted_iota(jnp.int32, weights.shape, 1)
    own = first_ref[0] + pl.program_id(0)
    total = jnp.sum(weights, axis=1, keepdims=True)
    gate = jnp.sum(jnp.where(lanes == own, weights, 0.0), axis=1, keepdims=True)
    gate = gate / jnp.where(total > 0.0, total, 1.0)
    for r, ref in enumerate(weight_refs):
        cols = pl.ds(pl.multiple_of(first_ref[2 + r] * depth, depth), depth)
        for left, span in ((row_out, slice(2 * ff)), (cot_ref, slice(2 * ff, all_ff))):
            term = dot_nn(left[0, :, cols], ref[0, :, span])
            if r == 0:
                acc[:, span] = term
            else:
                acc[:, span] += term
    act_grad = acc[:, 2 * ff :]
    gate_pre, up_pre = acc[:, :ff], acc[:, ff : 2 * ff]
    sig = 1.0 / (1.0 + jnp.exp(-gate_pre))
    silu = gate_pre * sig
    act = silu * up_pre
    gate_grad = jnp.sum(act * act_grad, axis=1, keepdims=True)
    act_grad = act_grad * gate
    act_out[0] = (act * gate).astype(BF16)
    slope = sig * (1.0 + gate_pre * (1.0 - sig))
    pre_out[0, :, :ff] = (act_grad * up_pre * slope).astype(BF16)
    pre_out[0, :, ff:] = (act_grad * silu).astype(BF16)
    high = gate_grad.astype(BF16).astype(F32)
    low = gate_grad - high
    extra = jnp.where(lanes == own, high, jnp.where(lanes == own + experts, low, 0.0))
    extra_out[0] = extra.astype(BF16)


def expert_rows(first, rows, spots, marks, cot_rows, router, weights, cap):
    experts, blocks, block = spots.shape
    depth, all_ff = weights[0].shape[1:]
    both = all_ff // 3 * 2
    width = rows.shape[1]
    count = blocks * cap
    one = lambda *shape: pl.BlockSpec((1,) + shape, lambda e, first: (e,) + (0,) * len(shape))
    whole = lambda a: pl.BlockSpec(a.shape, lambda e, first: (0, 0))
    return pl.pallas_call(
        functools.partial(expert_kernel, cap),
        grid_spec=pltpu.PrefetchScalarGridSpec(
            num_scalar_prefetch=1,
            grid=(experts,),
            in_specs=[
                whole(rows),
                one(blocks, block),
                whole(marks),
                one(count, width),
                whole(router),
            ]
            + [one(depth, all_ff)] * len(weights),
            out_specs=[
                one(count, width),
                one(count, both // 2),
                one(count, both),
                one(count, EXTRA),
            ],
            scratch_shapes=[pltpu.VMEM((count, all_ff), F32)],
        ),
        out_shape=[
            jax.ShapeDtypeStruct((experts, count, width), BF16),
            jax.ShapeDtypeStruct((experts, count, both // 2), BF16),
            jax.ShapeDtypeStruct((experts, count, both), BF16),
            jax.ShapeDtypeStruct((experts, count, EXTRA), BF16),
        ],
        compiler_params=pltpu.CompilerParams(vmem_limit_bytes=VMEM),
        cost_estimate=cost(11),
        name="expert_rows",
    )(first, rows, spots, marks, cot_rows, router, *weights)


def rows_back_kernel(cap, order, left_ref, spot_ref, *refs):
    out_ref, acc = refs[-2:]
    e = pl.program_id(0)
    blocks, block, wide = out_ref.shape
    weight_refs = refs[: order.shape[0]]
    depth = weight_refs[0].shape[1]

    @pl.when(e == 0)
    def _():
        acc[...] = jnp.zeros_like(acc)

    lane = lax.broadcasted_iota(jnp.int32, spot_ref.shape, 1)
    spot = jnp.sum(jnp.where(lane == e, spot_ref[...], 0), axis=1, keepdims=True)
    puts = [put_rows(spot[b * block : (b + 1) * block], cap) for b in range(blocks)]
    for r, ref in enumerate(weight_refs):
        cols = pl.ds(pl.multiple_of(order[r] * depth, depth), depth)
        rows = dot_nt(left_ref[0], ref[0]).astype(BF16)
        for b in range(blocks):
            acc[b * block : (b + 1) * block, cols] += dot_nn(
                puts[b], rows[b * cap : (b + 1) * cap, :]
            )
    if len(refs) > order.shape[0] + 2:
        extra_ref = refs[order.shape[0]]
        for b in range(blocks):
            acc[b * block : (b + 1) * block, wide - EXTRA :] += dot_nn(
                puts[b], extra_ref[0, b * cap : (b + 1) * cap, :]
            )

    @pl.when(e == pl.num_programs(0) - 1)
    def _():
        out_ref[...] = acc[...].astype(BF16).reshape(out_ref.shape)


def rows_back(order, left, weights, at, spot_cols, cap, extra=None):
    experts, count, size = left.shape
    depth = weights[0].shape[1]
    blocks = count // cap
    block = spot_cols.shape[0] // blocks
    width = depth * len(weights) + (0 if extra is None else EXTRA)
    shape = (blocks, block, width)
    one = lambda *shape: pl.BlockSpec((1,) + shape, lambda e, order: (e,) + (0,) * len(shape))
    extras = [] if extra is None else [extra]
    return pl.pallas_call(
        functools.partial(rows_back_kernel, cap),
        grid_spec=pltpu.PrefetchScalarGridSpec(
            num_scalar_prefetch=1,
            grid=(experts,),
            in_specs=[one(count, size), pl.BlockSpec(spot_cols.shape, lambda e, order: (0, 0))]
            + [pl.BlockSpec((1, depth, size), lambda e, order: (e, 0, at))] * len(weights)
            + [one(count, EXTRA)] * len(extras),
            out_specs=pl.BlockSpec(shape, lambda e, order: (0, 0, 0)),
            scratch_shapes=[pltpu.VMEM((blocks * block, width), F32)],
        ),
        out_shape=jax.ShapeDtypeStruct(shape, BF16),
        compiler_params=pltpu.CompilerParams(vmem_limit_bytes=VMEM),
        cost_estimate=cost(5 if extra is None else 10),
        name="mixtures" if extra is None else "row_grads",
    )(order, left, spot_cols, *weights, *extras)


def expert_grad_kernel(row_a, row_b, cot_a, cot_b, pre_a, pre_b, act_a, act_b, out_ref):
    both = pre_a.shape[2]
    total = dot_tn(row_a[0], pre_a[0]) + dot_tn(row_b[0], pre_b[0])
    out_ref[0, 0, :, :both] = total.astype(BF16)
    total = dot_tn(cot_a[0], act_a[0]) + dot_tn(cot_b[0], act_b[0])
    out_ref[0, 0, :, both:] = total.astype(BF16)


def expert_grads(rows, cots, pres, acts, shards):
    experts, count, width = rows[0].shape
    both, ff = pres[0].shape[2], acts[0].shape[2]
    depth = width // shards
    part = pl.BlockSpec((1, count, depth), lambda e, n: (e, 0, n))
    full = lambda size: pl.BlockSpec((1, count, size), lambda e, n: (e, 0, 0))
    return pl.pallas_call(
        expert_grad_kernel,
        grid=(experts, shards),
        in_specs=[part] * 4 + [full(both)] * 2 + [full(ff)] * 2,
        out_specs=pl.BlockSpec((1, 1, depth, both + ff), lambda e, n: (n, e, 0, 0)),
        out_shape=jax.ShapeDtypeStruct((shards, experts, depth, both + ff), BF16),
        compiler_params=pltpu.CompilerParams(vmem_limit_bytes=VMEM),
        cost_estimate=cost(18),
        name="expert_grads",
    )(rows[0], rows[1], cots[0], cots[1], pres[0], pres[1], acts[0], acts[1])


def body(
    layer_input,
    w_query,
    w_key,
    w_value,
    w_out,
    attn_gain,
    query_gain,
    key_gain,
    ffn_gain,
    w_router,
    w_gate,
    w_up,
    w_down,
    routes,
    pic_starts,
    cotangent,
):
    tok_count, model_width = layer_input.shape
    top_count = routes.shape[1]
    ga_count = lax.axis_size("ga")
    z_count = lax.axis_size("z")
    ea_count = 2 * z_count
    core = lax.axis_index("core")
    chip = lax.axis_index("z")
    local_experts, _, ff = w_gate.shape
    expert_total = local_experts * ea_count
    cap = max(2, 9 * tok_count * top_count // (8 * expert_total))
    group_size = HEADS // KV
    kv_width = KV * HD
    q_width = HEADS * HD

    small = [attn_gain, query_gain, key_gain, ffn_gain, w_router.reshape(-1)]
    small_all = ga_gather_small(jnp.concatenate(small))
    at, smalls = 0, []
    for piece in small:
        smalls.append(small_all[:, at : at + piece.shape[0]].reshape(-1))
        at += piece.shape[0]
    attn_gain_f, query_gain_f, key_gain_f, ffn_gain_f = [s.astype(F32) for s in smalls[:4]]
    router_full = smalls[4].reshape(model_width, expert_total)
    router_wide = jnp.pad(router_full, ((0, 0), (0, EXTRA - expert_total)))

    qkv_weights = (w_query, w_key, w_value)
    qkv_own = jnp.concatenate([core_halves(w)[0] for w in qkv_weights], axis=1)

    marks = jnp.sum(
        (routes[:, :, None] == jnp.arange(EXTRA, dtype=jnp.int32)[None, None, :]).astype(F32), axis=1
    )
    cot_steps = []
    qkv_first = ga_first_hop(after(qkv_own, small_all))
    cot_mine = line_gather(
        after(jnp.concatenate([cotangent, marks.astype(BF16)], axis=1), small_all), steps=cot_steps
    )
    qkv_twin = jnp.concatenate(
        [core_halves(after(w, *cot_steps[0]))[1] for w in qkv_weights], axis=1
    )
    qkv_second = ga_second_hop(qkv_first, 0, 1, cot_steps[1])
    qkv_mine = qkv_first + qkv_second
    qkv_other = dense_other(qkv_mine, qkv_twin)
    cot_mine = after(jnp.concatenate(cot_mine), *qkv_second)
    cot_sides = [cot_mine, swap_core(cot_mine)]
    first_expert = (chip * 2 + core) * local_experts
    mark_sides, spot_rows, spot_cols, cot_rows = [], [], [], []
    before = jnp.tril(jnp.ones((tok_count, tok_count), BF16))
    for side in cot_sides:
        side_marks = side[:, model_width:]
        chosen = lax.dynamic_slice_in_dim(side_marks, first_expert, local_experts, 1)
        chosen = chosen.reshape(z_count, tok_count, local_experts)
        rank = jnp.einsum("ts,bse->bte", before, chosen, preferred_element_type=F32)
        spots = jnp.where(chosen > 0, rank - 1.0, -1.0).astype(jnp.int32)
        mark_sides.append(side_marks)
        spot_rows.append(jnp.transpose(spots, (2, 0, 1)))
        spot_cols.append(spots.reshape(z_count * tok_count, local_experts))
        cot_rows.append(pick(side, spot_rows[-1], cap, model_width))

    ea_index = chip * 2 + core
    positions = ea_index * tok_count + jnp.arange(tok_count, dtype=jnp.int32)
    holder = ((chip - jnp.arange(z_count)) % z_count * 2)[None, :] + jnp.stack([core, 1 - core])[
        :, None
    ]
    key_pos = (holder.reshape(-1, 1) * tok_count + jnp.arange(tok_count)[None, :]).reshape(-1)
    key_pos = key_pos.astype(jnp.int32)
    allowed = allowed_mask(pic_starts[0], positions, key_pos)
    bias = jnp.where(allowed, 0.0, MASKED_SCORE).astype(F32)
    bias_turned = jnp.where(jnp.transpose(allowed), 0.0, MASKED_SCORE).astype(F32)
    frequency = ROPE_THETA ** (-jnp.arange(HD // 2, dtype=F32) * 2.0 / HD)
    angles = positions.astype(F32)[:, None] * frequency[None, :]
    cosine = jnp.concatenate([jnp.cos(angles), jnp.cos(angles)], axis=1)
    sine = jnp.concatenate([-jnp.sin(angles), jnp.sin(angles)], axis=1)
    per_key = max(1, ga_count // KV)
    ga_index = lax.axis_index("ga")
    run = group_size // 2 // per_key
    step = jnp.arange(per_key) ^ (ga_index % per_key)
    own_heads = (step[:, None] * 2 * run + jnp.arange(run)[None, :]).reshape(-1)
    key_place = jnp.arange(KV) ^ (ga_index // per_key)
    place = jnp.concatenate(
        [key_place, own_heads + core * run, own_heads + (1 - core) * run]
    ).astype(jnp.int32)

    input_f = layer_input.astype(F32)
    normed = rms_norm(input_f, attn_gain_f).astype(BF16)
    normed_mine = split_cols(normed, core)
    normed_other = split_cols(normed, 1 - core)
    normed_used = after(normed_mine, bias, bias_turned, cosine, sine)
    qkv = pieces_matmul((normed_used, normed_other), (qkv_mine, qkv_other))
    query_gain_row, key_gain_row = query_gain_f.reshape(1, HD), key_gain_f.reshape(1, HD)
    kv_own = prep_kv(qkv, cosine, sine, key_gain_row)

    out_own, out_twin = core_halves(w_out)
    out_first = ga_first_hop(after(out_own, *qkv_second))
    kv_mine, kv_other = ea_gather(kv_own, {2: cot_rows[:1], 3: cot_rows[1:] + out_first[1:]})
    out_mine = out_first + ga_second_hop(out_first, 0, 1, ())
    expert_own = jnp.concatenate([w_gate, w_up, jnp.swapaxes(w_down, 1, 2)], axis=2)
    expert_flat = expert_own.reshape(-1, 3 * ff)
    expert_gather = ga_first_hop(after(expert_flat, *out_first[1:]))

    att_mine, att_other, log_rows = attend(
        place,
        qkv,
        kv_mine,
        kv_other,
        bias,
        cosine,
        sine,
        query_gain_row,
    )
    out_other = dense_other(out_first + [after(p, att_mine) for p in out_mine[3:]], out_twin)
    hidden = input_f + pieces_matmul((att_mine, att_other), (out_mine, out_other))
    ffn_in = rms_norm(hidden, ffn_gain_f).astype(BF16)

    row_slots = line_gather(ffn_in, {3: expert_gather[1:]})
    hops = [ga_second_hop(expert_gather, 0, 2, ())]
    row_mine = after(jnp.concatenate(row_slots), *hops[0])
    row_sides = [row_mine, swap_core(row_mine)]
    hops.append(ga_second_hop(expert_gather, 1, 2, hops[0]))
    expert_all, order = shard_list(expert_gather, hops, expert_own.shape)
    logits = dot_nn(ffn_in, router_full)
    own_marks = marks[:, :expert_total] > 0
    peak = jnp.max(jnp.where(own_marks, logits, MASKED_SCORE), axis=1, keepdims=True)
    weights = jnp.exp(jnp.where(own_marks, logits - peak, MASKED_SCORE))
    gates = weights / jnp.sum(weights, axis=1, keepdims=True)

    first = jnp.concatenate([jnp.stack([first_expert, expert_total]).astype(jnp.int32), order])
    picked, acts, pres, extras = [], [], [], []
    for side in range(2):
        rows, act, pre, extra = expert_rows(
            first,
            row_sides[side],
            spot_rows[side],
            mark_sides[side],
            cot_rows[side],
            router_wide,
            expert_all,
            cap,
        )
        picked.append(rows)
        acts.append(act)
        pres.append(pre)
        extras.append(extra)
    expert_grad = expert_grads(picked, cot_rows, pres, acts, ga_count)
    expert_sum = lax.psum_scatter(expert_grad, "ga", scatter_dimension=0)
    row_other = rows_back(
        order, after(pres[1], expert_grad), expert_all, 0, spot_cols[1], cap, extras[1]
    )
    row_mine = rows_back(
        order, after(pres[0], row_other), expert_all, 0, spot_cols[0], cap, extras[0]
    )
    rows = LineSum(core_slots(row_mine, row_other))
    rows.step()
    mix_other = rows_back(order, after(acts[1], rows.slots[1]), expert_all, 2, spot_cols[1], cap)
    rows.step(mix_other)
    mix_mine = rows_back(order, after(acts[0], *rows.held), expert_all, 2, spot_cols[0], cap)
    rows.step(mix_mine)
    row_sum = rows.result()

    grad_out = cotangent.astype(F32)
    gate_grad = (
        row_sum[:, model_width : model_width + expert_total].astype(F32)
        + row_sum[:, model_width + expert_total : model_width + 2 * expert_total].astype(F32)
    )
    inner = jnp.sum(gates * gate_grad, axis=1, keepdims=True)
    logit_grad = gates * (gate_grad - inner)
    router_grad = lax.dot_general(
        ffn_in.astype(F32), logit_grad, (((0,), (0,)), ((), ())), precision=PRECISE
    )
    ffn_in_grad = row_sum[:, :model_width].astype(F32) + jnp.dot(
        logit_grad, router_full.astype(F32).T, precision=PRECISE
    )
    unused, ffn_back = jax.vjp(rms_norm, hidden, ffn_gain_f)
    hidden_part, ffn_gain_grad = ffn_back(ffn_in_grad)
    hidden_grad = grad_out + hidden_part
    branch_grad = hidden_grad.astype(BF16)
    out_terms = [dot_tn(a, branch_grad) for a in (att_mine, att_other)]
    out_terms[1] = out_terms[1].astype(BF16)
    att_grads = pieces_back(after(branch_grad, out_terms[1]), out_mine + out_other, BF16)
    raw_grads, kv_grads, gain_grads = [], [], []

    def back(head, *before):
        raw_grad, kv_grad, gain_grad = attend_back(
            head,
            1,
            place,
            qkv,
            kv_mine,
            kv_other,
            bias_turned,
            cosine,
            sine,
            query_gain_row,
            after(att_grads, *before),
            (att_mine, att_other),
            log_rows,
        )
        raw_grads.append(raw_grad)
        kv_grads.append(kv_grad)
        gain_grads.append(gain_grad[0])

    def weight_terms(grad):
        return dot_tn(normed_mine, grad), dot_tn(normed_other, grad).astype(BF16)

    mix = LineSum(core_slots(mix_mine, after(mix_other, out_terms[1])))
    held = [mix.step()]
    back(0, mix.slots[1], expert_sum)
    held.append(mix.step(raw_grads[0]))
    out_total = core_sum(*out_terms)
    out_share = ga_sum_whole(out_total)
    back(1, raw_grads[0], out_total, *held[0])
    held.append(mix.step(raw_grads[1]))
    back(2, raw_grads[1], *held[1])
    back(3, raw_grads[2], *held[2])
    mix_sum = mix.result()
    layer_output = (hidden + mix_sum.astype(F32)).astype(BF16)
    query_raw_grad = jnp.concatenate(raw_grads, axis=1)
    query_terms = weight_terms(query_raw_grad)
    query_gain_grad = sum(gain_grads)
    kv_grad = after(jnp.concatenate(kv_grads, axis=1), mix_sum)
    kv_grad = kv_grad.reshape(2, z_count, tok_count, 2 * kv_width)
    keys_values = LineSum(core_slots(kv_grad[0], kv_grad[1]))
    keys_values.step(query_terms[1])
    query_total = core_sum(*query_terms)
    keys_values.step(query_total)
    query_first = ga_sum_first(query_total)
    keys_values.step(out_share)
    kv_raw_grad, key_gain_grad = kv_back(
        qkv, after(keys_values.result(), *query_first), cosine, sine, key_gain_row
    )
    key_gain_grad = key_gain_grad[0]
    out_all = z_all_sum(out_share)
    query_share = ga_sum_second(query_first)
    kv_total = core_sum(*weight_terms(kv_raw_grad))
    kv_share = ga_sum_second(ga_sum_first(after(kv_total, query_share)))
    query_all = z_all_sum(after(query_share, out_all))
    out_sum, query_sum = whole_shard(out_all), whole_shard(query_all)
    kv_sum = whole_shard(z_all_sum_small(kv_share))
    key_sum, value_sum = kv_sum[:, :kv_width], kv_sum[:, kv_width:]
    chunks = [query_raw_grad, kv_raw_grad]
    qkv_grad = jnp.concatenate(chunks, axis=1)
    both_grads = pieces_back(qkv_grad, qkv_mine + qkv_other, F32)
    half_width = model_width // 2
    normed_grad = join_cols(both_grads[:, :half_width], both_grads[:, half_width:])
    unused, attn_back = jax.vjp(rms_norm, input_f, attn_gain_f)
    input_part, attn_gain_grad = attn_back(normed_grad)
    input_grad = (hidden_grad + input_part).astype(BF16)

    tiny = [attn_gain_grad, query_gain_grad, key_gain_grad, ffn_gain_grad, router_grad.reshape(-1)]
    tiny_own = sum_small(jnp.concatenate([t.reshape(ga_count, -1) for t in tiny], axis=1))
    at, tiny_sums = 0, []
    for piece in tiny:
        width = piece.shape[0] // ga_count
        tiny_sums.append(tiny_own[at : at + width])
        at += width
    attn_sum, qgain_sum, kgain_sum, ffn_sum, router_sum = tiny_sums
    return (
        layer_output,
        input_grad,
        query_sum,
        key_sum,
        value_sum,
        out_sum,
        attn_sum,
        qgain_sum,
        kgain_sum,
        ffn_sum,
        router_sum.reshape(-1, expert_total),
        expert_sum[:, :, :ff].astype(F32),
        expert_sum[:, :, ff : 2 * ff].astype(F32),
        jnp.swapaxes(expert_sum[:, :, 2 * ff :], 1, 2).astype(F32),
    )


def solution(mesh):
    ga_count, ea_count = mesh.shape["ga"], mesh.shape["ea"]
    inner = Mesh(mesh.devices.reshape(ga_count, ea_count // 2, 2), ("ga", "z", "core"))
    everyone = ("ga", "z", "core")
    owners = ("z", "core")
    in_specs = (
        P(everyone, None),
        P("ga", None),
        P("ga", None),
        P("ga", None),
        P("ga", None),
        P("ga"),
        P("ga"),
        P("ga"),
        P("ga"),
        P("ga", None),
        P(owners, "ga", None),
        P(owners, "ga", None),
        P(owners, None, "ga"),
        P(everyone, None),
        P("ga", None),
        P(everyone, None),
    )
    out_specs = (
        P(everyone, None),
        P(everyone, None),
        P("ga", None),
        P("ga", None),
        P("ga", None),
        P("ga", None),
        P("ga"),
        P("ga"),
        P("ga"),
        P("ga"),
        P("ga", None),
        P(owners, "ga", None),
        P(owners, "ga", None),
        P(owners, None, "ga"),
    )
    return jax.shard_map(body, mesh=inner, in_specs=in_specs, out_specs=out_specs, check_vma=False)
```

```python
import functools

import jax
import jax.numpy as jnp
from jax import lax
from jax.experimental import pallas as pl
from jax.experimental.pallas import tpu as pltpu
from jax.sharding import Mesh
from jax.sharding import PartitionSpec as P

HEADS = 32
KV = 4
HD = 128
PIC = 256


NORM_EPS = 1e-06
ROPE_THETA = 1000000.0
MASKED_SCORE = -1e30
PRECISE = lax.Precision.HIGHEST
F32 = jnp.float32
BF16 = jnp.bfloat16
EXTRA = 128
LOG2E = 1.4426950408889634
VMEM = 56 << 20


def rms_norm(values, norm_gain):
    inverse = lax.rsqrt(jnp.mean(values * values, axis=-1, keepdims=True) + NORM_EPS)
    return values * inverse * norm_gain


def piece_ids(starts, positions):
    inside = (
        (starts[:, None] >= 0)
        & (positions[None, :] >= starts[:, None])
        & (positions[None, :] < starts[:, None] + PIC)
    )
    labels = jnp.arange(1, starts.shape[0] + 1, dtype=jnp.int32)[:, None]
    return jnp.sum(jnp.where(inside, labels, 0), axis=0)


def allowed_mask(starts, query_pos, key_pos):
    query_piece = piece_ids(starts, query_pos)
    key_piece = piece_ids(starts, key_pos)
    causal = key_pos[None, :] <= query_pos[:, None]
    shared = (query_piece[:, None] == key_piece[None, :]) & (query_piece[:, None] > 0)
    return causal | shared


def dot_nn(left, right):
    return lax.dot_general(left, right, (((1,), (0,)), ((), ())), preferred_element_type=F32)


def dot_tn(left, right):
    return lax.dot_general(left, right, (((0,), (0,)), ((), ())), preferred_element_type=F32)


def dot_nt(left, right):
    return lax.dot_general(left, right, (((1,), (1,)), ((), ())), preferred_element_type=F32)


def after(value, *others):
    return lax.optimization_barrier((value,) + others)[0]


def swap_core(value):
    return lax.ppermute(value, "core", [(0, 1), (1, 0)])


def swap_axis(value, axis, bit):
    return lax.ppermute(value, axis, [(i, i ^ bit) for i in range(lax.axis_size(axis))])


def plus(*terms):
    total = terms[0].astype(F32)
    for term in terms[1:]:
        total = total + term.astype(F32)
    return total.astype(BF16)


def line_gather(value, before=None, steps=None):
    count = lax.axis_size("z")
    place = lax.axis_index("z")
    below, above = {}, {}
    up = down = value
    for step in range(1, count):
        if before and step in before:
            up, down = lax.optimization_barrier((up, down) + tuple(before[step]))[:2]
        up = lax.ppermute(up, "z", [(p, p + 1) for p in range(step - 1, count - 1)])
        down = lax.ppermute(down, "z", [(p, p - 1) for p in range(1, count - step + 1)])
        up, down = lax.optimization_barrier((up, down))
        below[step], above[step] = up, down
        if steps is not None:
            steps.append((up, down))
    return [value] + [
        jnp.where(place >= step, below[step], above[count - step]) for step in range(1, count)
    ]


class LineSum:
    def __init__(self, slots):
        self.slots, self.done = slots, 0

    def step(self, *before):
        count = lax.axis_size("z")
        self.done += 1
        up, down = self.slots[self.done], self.slots[count - self.done]
        if before:
            up, down = lax.optimization_barrier((up, down) + before)[:2]
        if self.done > 1:
            up, down = plus(up, self.held[0]), plus(down, self.held[1])
        self.sent = (up, down)
        up = lax.ppermute(up, "z", [(p, p + 1) for p in range(self.done)])
        down = lax.ppermute(
            down, "z", [(p, p - 1) for p in range(count - 1, count - 1 - self.done, -1)]
        )
        self.held = lax.optimization_barrier((up, down))
        return self.held

    def result(self):
        while self.done < lax.axis_size("z") - 1:
            self.step()
        return plus(self.slots[0], *self.held)


def ea_gather(value, before=None, steps=None):
    mine = jnp.concatenate(line_gather(value, before, steps))
    return mine, swap_core(mine)


def core_slots(mine, other):
    got = swap_core(other)
    return [plus(mine[s], got[s]) for s in range(lax.axis_size("z"))]


def z_all_sum(value):
    return lax.psum(value, "z")


def z_all_sum_small(value):
    count = lax.axis_size("z")
    place = lax.axis_index("z")
    bits, bit = [], 1
    while bit < count:
        rows = value.shape[0] // 2
        upper = (place // bit) % 2
        keep = lax.dynamic_slice_in_dim(value, upper * rows, rows, 0)
        send = lax.dynamic_slice_in_dim(value, (1 - upper) * rows, rows, 0)
        value = plus(keep, swap_axis(send, "z", bit))
        bits.append(bit)
        bit *= 2
    for bit in reversed(bits):
        got = swap_axis(value, "z", bit)
        upper = (place // bit) % 2
        low, high = jnp.where(upper == 0, value, got), jnp.where(upper == 0, got, value)
        value = jnp.concatenate([low, high])
    return value


def ga_order():
    return lax.axis_index("ga") ^ jnp.arange(lax.axis_size("ga"))


def ga_first_hop(value):
    if lax.axis_size("ga") != 4:
        whole = lax.all_gather(value, "ga", axis=0)
        return [jnp.take(whole, ga_order(), axis=0).reshape((-1,) + value.shape[1:])]
    return [value, swap_axis(value, "ga", 1), swap_axis(value, "ga", 2)]


def ga_second_hop(first, part, parts, before):
    if len(first) == 1:
        return []
    half = first[0].shape[0] // 2
    rows = half // parts
    to_y = first[1][part * rows : (part + 1) * rows]
    to_x = first[2][half + part * rows : half + (part + 1) * rows]
    to_y, to_x = lax.optimization_barrier((to_y, to_x) + tuple(before))[:2]
    return [swap_axis(to_y, "ga", 2), swap_axis(to_x, "ga", 1)]


def ga_sum_first(value):
    if lax.axis_size("ga") != 4:
        return (value,)
    rows = value.shape[0] // 4
    half = rows // 2
    own, for_x, for_y = [value[r * rows : (r + 1) * rows] for r in range(3)]
    low = swap_axis(value[3 * rows : 3 * rows + half], "ga", 1)
    high = swap_axis(value[3 * rows + half :], "ga", 2)
    to_x = jnp.concatenate([for_x[:half], plus(for_x[half:], high)])
    to_y = jnp.concatenate([plus(for_y[:half], low), for_y[half:]])
    return own, to_x, to_y


def ga_sum_second(parts, before=()):
    if len(parts) == 1:
        return ga_sum_whole(parts[0])
    own, to_x, to_y = parts
    terms = (own, swap_axis(to_x, "ga", 1), swap_axis(to_y, "ga", 2))
    return plus(*lax.optimization_barrier(terms + tuple(before))[:3])


def ga_sum_whole(value):
    blocks = value.reshape((lax.axis_size("ga"), -1) + value.shape[1:])
    blocks = jnp.take(blocks, ga_order(), axis=0).reshape(value.shape)
    return lax.psum_scatter(blocks, "ga", scatter_dimension=0, tiled=True)


def ga_gather_small(value):
    count = lax.axis_size("ga")
    held, bit = value[None], 1
    while bit < count:
        held = jnp.concatenate([held, swap_axis(held, "ga", bit)])
        bit *= 2
    return jnp.take(held, ga_order(), axis=0)


def sum_small(rows):
    total = rows + swap_core(rows)
    count, bit = lax.axis_size("z"), 1
    while bit < count:
        total = total + swap_axis(total, "z", bit)
        bit *= 2
    count = lax.axis_size("ga")
    total = jnp.take(total, ga_order(), axis=0)
    while count > 1:
        count //= 2
        total = total[:count] + swap_axis(total[count:], "ga", count)
    return total[0]


def core_halves(value):
    core = lax.axis_index("core")
    rows = value.shape[0] // 2
    return (
        lax.dynamic_slice_in_dim(value, core * rows, rows, 0),
        lax.dynamic_slice_in_dim(value, (1 - core) * rows, rows, 0),
    )


def swap_pieces(pieces):
    return [swap_core(piece) for piece in pieces]


def split_cols(value, half):
    groups = lax.axis_size("ga")
    width = value.shape[1] // groups // 2
    order = ga_order()
    return jnp.concatenate(
        [
            lax.dynamic_slice_in_dim(value, (order[r] * 2 + half) * width, width, 1)
            for r in range(groups)
        ],
        axis=1,
    )


def device_cols(value):
    groups = lax.axis_size("ga")
    width = value.shape[1] // groups
    order = ga_order()
    return jnp.concatenate(
        [lax.dynamic_slice_in_dim(value, order[g] * width, width, 1) for g in range(groups)], axis=1
    )


def join_cols(mine, other):
    groups = lax.axis_size("ga")
    core = lax.axis_index("core")
    width = mine.shape[1] // groups
    order = ga_order()
    parts = []
    for g in range(groups):
        a = lax.dynamic_slice_in_dim(mine, order[g] * width, width, 1)
        b = lax.dynamic_slice_in_dim(other, order[g] * width, width, 1)
        parts += [jnp.where(core == 0, a, b), jnp.where(core == 0, b, a)]
    return jnp.concatenate(parts, axis=1)


def core_sum(mine, other):
    return plus(mine, swap_core(other))


def whole_shard(shares):
    core = lax.axis_index("core")
    rows = shares[0].shape[0]
    out = jnp.zeros((2 * rows, sum(share.shape[1] for share in shares)), F32)
    at = 0
    for share in shares:
        for half, part in ((core, share), (1 - core, swap_core(share))):
            out = lax.dynamic_update_slice(out, part.astype(F32), (half * rows, at))
        at += share.shape[1]
    return out


def cost(micros):
    return pl.CostEstimate(flops=micros * 10**9, bytes_accessed=1024, transcendentals=0)


def pieces_kernel(plan, *refs):
    acc = None
    lefts, out_ref = refs[: 1 + max(which for which, _, _ in plan)], refs[-1]
    for (which, at, size), ref in zip(plan, refs[len(lefts) : -1]):
        term = dot_nn(lefts[which][:, at : at + size], ref[...])
        acc = term if acc is None else acc + term
    out_ref[...] = acc


def pieces_matmul(lefts, piece_lists):
    plan, pieces = [], []
    for which, some in enumerate(piece_lists):
        at = 0
        for piece in some:
            plan.append((which, at, piece.shape[0]))
            pieces.append(piece)
            at += piece.shape[0]
    rows, width = lefts[0].shape[0], pieces[0].shape[1]
    tile = min(1024 if width > 4096 else 512, width)
    return pl.pallas_call(
        functools.partial(pieces_kernel, plan),
        grid=(width // tile,),
        in_specs=[pl.BlockSpec(left.shape, lambda n: (0, 0)) for left in lefts]
        + [pl.BlockSpec((piece.shape[0], tile), lambda n: (0, n)) for piece in pieces],
        out_specs=pl.BlockSpec((rows, tile), lambda n: (0, n)),
        out_shape=jax.ShapeDtypeStruct((rows, width), F32),
        compiler_params=pltpu.CompilerParams(vmem_limit_bytes=VMEM),
        cost_estimate=cost(6),
        name="dense_matmul",
    )(*lefts, *pieces)


def pieces_back_kernel(sizes, left_ref, *refs):
    n = pl.program_id(0)
    out_ref, acc = refs[-2:]

    @pl.when(n == 0)
    def _():
        acc[...] = jnp.zeros_like(acc)

    at = 0
    for ref, size in zip(refs[:-2], sizes):
        acc[:, at : at + size] += dot_nt(left_ref[...], ref[...])
        at += size

    @pl.when(n == pl.num_programs(0) - 1)
    def _():
        out_ref[...] = acc[...].astype(out_ref.dtype)


def pieces_back(left, pieces, dtype):
    rows, width = left.shape
    tile = min(512, width)
    sizes = [piece.shape[0] for piece in pieces]
    return pl.pallas_call(
        functools.partial(pieces_back_kernel, sizes),
        grid=(width // tile,),
        in_specs=[pl.BlockSpec((rows, tile), lambda n: (0, n))]
        + [pl.BlockSpec((size, tile), lambda n: (0, n)) for size in sizes],
        out_specs=pl.BlockSpec((rows, sum(sizes)), lambda n: (0, 0)),
        out_shape=jax.ShapeDtypeStruct((rows, sum(sizes)), dtype),
        scratch_shapes=[pltpu.VMEM((rows, sum(sizes)), F32)],
        compiler_params=pltpu.CompilerParams(vmem_limit_bytes=VMEM),
        cost_estimate=cost(6),
        name="dense_back",
    )(left, *pieces)


def prep_head(raw, gain, cosine, sine):
    inverse = lax.rsqrt(jnp.mean(raw * raw, axis=-1, keepdims=True) + NORM_EPS)
    scaled = raw * inverse * gain
    turned = scaled * cosine + pltpu.roll(scaled, HD // 2, 1) * sine
    return turned.astype(BF16), inverse


def head_cols(index):
    return pl.ds(pl.multiple_of(index * HD, HD), HD)


def prep_kv_kernel(raw_ref, cos_ref, sin_ref, gain_ref, out_ref):
    for h in range(KV):
        span = slice(h * HD, (h + 1) * HD)
        keys, _ = prep_head(raw_ref[:, span], gain_ref[...], cos_ref[...], sin_ref[...])
        out_ref[:, span] = keys
    out_ref[:, KV * HD :] = raw_ref[:, KV * HD :].astype(BF16)


def prep_kv(raw, cosine, sine, gain):
    rows, width = raw.shape[0], 2 * KV * HD
    whole = lambda a: pl.BlockSpec(a.shape, lambda i: (0, 0))
    return pl.pallas_call(
        prep_kv_kernel,
        grid=(1,),
        in_specs=[
            pl.BlockSpec((rows, width), lambda i: (0, raw.shape[1] // width - 1)),
            whole(cosine),
            whole(sine),
            whole(gain),
        ],
        out_specs=pl.BlockSpec((rows, width), lambda i: (0, 0)),
        out_shape=jax.ShapeDtypeStruct((rows, width), BF16),
        compiler_params=pltpu.CompilerParams(vmem_limit_bytes=VMEM),
        cost_estimate=cost(1),
        name="prep_kv",
    )(raw, cosine, sine, gain)


def head_back(raw, inverse, grad, gain, cosine, sine):
    scaled_grad = grad * cosine + pltpu.roll(grad * sine, HD // 2, 1)
    unit = raw * inverse
    gain_grad = jnp.sum(scaled_grad * unit, axis=0, keepdims=True)
    unit_grad = scaled_grad * gain
    mean = jnp.mean(unit_grad * unit, axis=-1, keepdims=True)
    return inverse * (unit_grad - unit * mean), gain_grad


def kv_back_kernel(raw_ref, grad_ref, cos_ref, sin_ref, gain_ref, out_ref, gain_grad_ref):
    total = jnp.zeros((1, HD), F32)
    for h in range(KV):
        span = slice(h * HD, (h + 1) * HD)
        raw = raw_ref[:, span]
        cosine, sine, gain = cos_ref[...], sin_ref[...], gain_ref[...]
        _, inverse = prep_head(raw, gain, cosine, sine)
        grad = grad_ref[:, 2 * h * HD : (2 * h + 1) * HD].astype(F32)
        raw_grad, gain_grad = head_back(raw, inverse, grad, gain, cosine, sine)
        out_ref[:, span] = raw_grad.astype(BF16)
        out_ref[:, (KV + h) * HD : (KV + h + 1) * HD] = grad_ref[
            :, (2 * h + 1) * HD : (2 * h + 2) * HD
        ]
        total = total + gain_grad
    gain_grad_ref[...] = jnp.broadcast_to(total, gain_grad_ref.shape)


def kv_back(raw, grad, cosine, sine, gain):
    rows, width = raw.shape[0], 2 * KV * HD
    whole = lambda a: pl.BlockSpec(a.shape, lambda i: (0, 0))
    return pl.pallas_call(
        kv_back_kernel,
        grid=(1,),
        in_specs=[
            pl.BlockSpec((rows, width), lambda i: (0, raw.shape[1] // width - 1)),
            whole(grad),
            whole(cosine),
            whole(sine),
            whole(gain),
        ],
        out_specs=[
            pl.BlockSpec((rows, width), lambda i: (0, 0)),
            pl.BlockSpec((8, HD), lambda i: (0, 0)),
        ],
        out_shape=[
            jax.ShapeDtypeStruct((rows, width), BF16),
            jax.ShapeDtypeStruct((8, HD), F32),
        ],
        compiler_params=pltpu.CompilerParams(vmem_limit_bytes=VMEM),
        cost_estimate=cost(1),
        name="kv_back",
    )(raw, grad, cosine, sine, gain)


def attend_kernel(
    place,
    raw_ref,
    key_a,
    key_b,
    value_a,
    value_b,
    bias_ref,
    cos_ref,
    sin_ref,
    gain_ref,
    mine_ref,
    other_ref,
    log_ref,
):
    half = key_a.shape[0]
    chunk = min(512, half)
    to_log2 = LOG2E * HD**-0.5
    count = raw_ref.shape[1] // HD

    def one_head(at_head, out_ref, column):
        head = place[KV + at_head]
        query, _ = prep_head(
            raw_ref[:, head_cols(head)], gain_ref[...], cos_ref[...], sin_ref[...]
        )
        total = jnp.zeros((query.shape[0], 1), F32)
        acc = jnp.zeros(query.shape, F32)
        for side, (key_ref, value_ref) in enumerate(((key_a, value_a), (key_b, value_b))):
            for at in range(0, half, chunk):
                scores = dot_nt(query, key_ref[at : at + chunk, :])
                first = side * half + at
                weights = jnp.exp2(scores * to_log2 + bias_ref[:, first : first + chunk])
                total = total + jnp.sum(weights, axis=1, keepdims=True)
                acc = acc + dot_nn(weights.astype(BF16), value_ref[at : at + chunk, :])
        out_ref[:, head_cols(column)] = (acc / total).astype(BF16)
        logs = jnp.transpose(jnp.broadcast_to(jnp.log2(total), query.shape))
        log_ref[0, pl.ds(at_head, 1), :] = logs[0:1, :]

    @pl.loop(0, count // 2)
    def _(i):
        one_head(i, mine_ref, i)
        one_head(count // 2 + i, other_ref, i)


def attend_specs(rows, group, half, tables):
    whole = lambda h, place: (0, 0)
    side = lambda first: pl.BlockSpec((half, HD), lambda h, place: (0, first + h))
    return [
        pl.BlockSpec((rows, group), lambda h, place: (0, h)),
        side(0),
        side(0),
        side(KV),
        side(KV),
    ] + [pl.BlockSpec(t.shape, whole) for t in tables]


def attend(place, raw, kv_mine, kv_other, bias, cosine, sine, gain):
    rows = raw.shape[0]
    group = HEADS * HD // KV
    half = kv_mine.shape[0]
    tables = (bias, cosine, sine, gain)
    half_spec = pl.BlockSpec((rows, group // 2), lambda h, place: (0, place[h]))
    return pl.pallas_call(
        attend_kernel,
        grid_spec=pltpu.PrefetchScalarGridSpec(
            num_scalar_prefetch=1,
            grid=(KV,),
            in_specs=attend_specs(rows, group, half, tables),
            out_specs=[
                half_spec,
                half_spec,
                pl.BlockSpec((1, HEADS // KV, rows), lambda h, place: (h, 0, 0)),
            ],
        ),
        out_shape=[
            jax.ShapeDtypeStruct((rows, HEADS * HD // 2), BF16),
            jax.ShapeDtypeStruct((rows, HEADS * HD // 2), BF16),
            jax.ShapeDtypeStruct((KV, HEADS // KV, rows), F32),
        ],
        compiler_params=pltpu.CompilerParams(vmem_limit_bytes=VMEM),
        cost_estimate=cost(2),
        name="attend",
    )(place, raw, kv_mine, kv_other, kv_mine, kv_other, *tables)


def attend_back_kernel(
    place,
    raw_ref,
    key_a,
    key_b,
    value_a,
    value_b,
    bias_ref,
    cos_ref,
    sin_ref,
    gain_ref,
    grad_mine,
    grad_other,
    out_mine,
    out_other,
    log_ref,
    raw_grad_ref,
    kv_grad_ref,
    gain_grad_ref,
    key_acc,
    value_acc,
):
    h = pl.program_id(0)
    half = key_a.shape[0]
    chunk = min(512, half)
    scale = HD**-0.5
    to_log2 = LOG2E * scale
    count = raw_ref.shape[1] // HD
    key_acc[...] = jnp.zeros_like(key_acc)
    value_acc[...] = jnp.zeros_like(value_acc)

    @pl.when(h == 0)
    def _():
        gain_grad_ref[...] = jnp.zeros_like(gain_grad_ref)

    def one_head(at_head, grad_ref, out_ref, column):
        head = place[KV + at_head]
        raw = raw_ref[:, head_cols(head)]
        cosine, sine, gain = cos_ref[...], sin_ref[...], gain_ref[...]
        query, inverse = prep_head(raw, gain, cosine, sine)
        grad = grad_ref[:, head_cols(column)]
        product = grad.astype(F32) * out_ref[:, head_cols(column)].astype(F32)
        inner = jnp.sum(jnp.transpose(product), axis=0, keepdims=True)
        logs = log_ref[0, pl.ds(at_head, 1), :]
        query_grad = jnp.zeros(query.shape, F32)
        for side, (key_ref, value_ref) in enumerate(((key_a, value_a), (key_b, value_b))):
            for at in range(0, half, chunk):
                keys = key_ref[at : at + chunk, :]
                first = side * half + at
                span = slice(first, first + chunk)
                scores = dot_nt(keys, query)
                probs = jnp.exp2(scores * to_log2 + bias_ref[span, :] - logs)
                prob_grad = dot_nt(value_ref[at : at + chunk, :], grad)
                score_grad = (probs * (prob_grad - inner)).astype(BF16)
                value_acc[span, :] += dot_nn(probs.astype(BF16), grad)
                key_acc[span, :] += dot_nn(score_grad, query)
                query_grad = query_grad + dot_tn(score_grad, keys)
        query_grad = (query_grad * scale).astype(BF16).astype(F32)
        raw_grad, gain_grad = head_back(raw, inverse, query_grad, gain, cosine, sine)
        gain_grad_ref[0:1, :] += gain_grad
        raw_grad_ref[:, head_cols(head)] = raw_grad.astype(BF16)

    @pl.loop(0, count // 2)
    def _(i):
        one_head(i, grad_mine, out_mine, i)
        one_head(count // 2 + i, grad_other, out_other, i)

    heads = kv_grad_ref.shape[1] // HD // 2
    kv_grad_ref[:, head_cols(h)] = (key_acc[...] * scale).astype(BF16)
    kv_grad_ref[:, head_cols(heads + h)] = value_acc[...].astype(BF16)


def attend_back(
    first, count, place, raw, kv_mine, kv_other, bias, cosine, sine, gain, grad, outs, logs
):
    rows = raw.shape[0]
    group = HEADS * HD // KV
    half = kv_mine.shape[0]
    tables = (bias, cosine, sine, gain)
    half_spec = pl.BlockSpec((rows, group // 2), lambda h, place: (0, place[first + h]))
    other_spec = pl.BlockSpec((rows, group // 2), lambda h, place: (0, KV + place[first + h]))
    whole = lambda h, place: (0, 0)
    side = lambda at: pl.BlockSpec((half, HD), lambda h, place: (0, at + first + h))
    return pl.pallas_call(
        attend_back_kernel,
        grid_spec=pltpu.PrefetchScalarGridSpec(
            num_scalar_prefetch=1,
            grid=(count,),
            in_specs=[
                pl.BlockSpec((rows, group), lambda h, place: (0, first + h)),
                side(0),
                side(0),
                side(KV),
                side(KV),
            ]
            + [pl.BlockSpec(t.shape, whole) for t in tables]
            + [half_spec, other_spec, half_spec, half_spec]
            + [pl.BlockSpec((1,) + logs.shape[1:], lambda h, place: (first + h, 0, 0))],
            out_specs=[
                pl.BlockSpec((rows, group), lambda h, place: (0, h)),
                pl.BlockSpec((2 * half, 2 * count * HD), whole),
                pl.BlockSpec((8, HD), whole),
            ],
            scratch_shapes=[pltpu.VMEM((2 * half, HD), F32), pltpu.VMEM((2 * half, HD), F32)],
        ),
        out_shape=[
            jax.ShapeDtypeStruct((rows, count * group), BF16),
            jax.ShapeDtypeStruct((2 * half, 2 * count * HD), BF16),
            jax.ShapeDtypeStruct((8, HD), F32),
        ],
        compiler_params=pltpu.CompilerParams(vmem_limit_bytes=VMEM),
        cost_estimate=cost(9),
        name="attend_back",
    )(place, raw, kv_mine, kv_other, kv_mine, kv_other, *tables, grad, grad, *outs, logs)


def pick_rows(spot_row, cap):
    places = lax.broadcasted_iota(jnp.int32, (cap, spot_row.shape[1]), 0)
    return jnp.where(places == spot_row, 1.0, 0.0).astype(BF16)


def put_rows(spot_col, cap):
    places = lax.broadcasted_iota(jnp.int32, (spot_col.shape[0], cap), 1)
    return jnp.where(places == spot_col, 1.0, 0.0).astype(BF16)


def pick_kernel(cap, rows_ref, spot_ref, out_ref):
    block = spot_ref.shape[2]
    for e in range(spot_ref.shape[0]):
        for b in range(spot_ref.shape[1]):
            pick = pick_rows(spot_ref[e, b : b + 1, :], cap)
            rows = rows_ref[b * block : (b + 1) * block, :]
            out_ref[e, b * cap : (b + 1) * cap, :] = dot_nn(pick, rows).astype(BF16)


def pick(rows, spots, cap, width):
    experts, blocks, block = spots.shape
    tile = min(512, width)
    return pl.pallas_call(
        functools.partial(pick_kernel, cap),
        grid=(width // tile,),
        in_specs=[
            pl.BlockSpec((blocks * block, tile), lambda n: (0, n)),
            pl.BlockSpec(spots.shape, lambda n: (0, 0, 0)),
        ],
        out_specs=pl.BlockSpec((experts, blocks * cap, tile), lambda n: (0, 0, n)),
        out_shape=jax.ShapeDtypeStruct((experts, blocks * cap, width), BF16),
        compiler_params=pltpu.CompilerParams(vmem_limit_bytes=VMEM),
        cost_estimate=cost(3),
        name="pick",
    )(rows, spots)


def expert_kernel(
    cap,
    first_ref,
    rows_ref,
    spot_ref,
    mark_ref,
    cot_ref,
    router_ref,
    weight_ref,
    row_out,
    act_out,
    pre_out,
    extra_out,
):
    shards, _, depth, all_ff = weight_ref.shape
    ff = all_ff // 3
    experts = first_ref[1]
    block = spot_ref.shape[2]
    blocks = spot_ref.shape[1]
    marks = []
    for b in range(blocks):
        pick = pick_rows(spot_ref[0, b : b + 1, :], cap)
        span = slice(b * block, (b + 1) * block)
        row_out[0, b * cap : (b + 1) * cap, :] = dot_nn(pick, rows_ref[span, :]).astype(BF16)
        marks.append(dot_nn(pick, mark_ref[span, :]))
    marked = jnp.concatenate(marks, axis=0) > 0.5
    rows = row_out[0]
    logits = dot_nn(rows, router_ref[...])
    peak = jnp.max(jnp.where(marked, logits, MASKED_SCORE), axis=1, keepdims=True)
    weights = jnp.where(marked, jnp.exp(jnp.where(marked, logits - peak, 0.0)), 0.0)
    lanes = lax.broadcasted_iota(jnp.int32, weights.shape, 1)
    own = first_ref[0] + pl.program_id(0)
    total = jnp.sum(weights, axis=1, keepdims=True)
    gate = jnp.sum(jnp.where(lanes == own, weights, 0.0), axis=1, keepdims=True)
    gate = gate / jnp.where(total > 0.0, total, 1.0)
    pre = dot_nn(rows, weight_ref[:, :, :, : 2 * ff].reshape(shards * depth, 2 * ff))
    act_grad = dot_nn(cot_ref[0], weight_ref[:, :, :, 2 * ff :].reshape(shards * depth, ff))
    gate_pre, up_pre = pre[:, :ff], pre[:, ff:]
    sig = 1.0 / (1.0 + jnp.exp(-gate_pre))
    silu = gate_pre * sig
    act = silu * up_pre
    gate_grad = jnp.sum(act * act_grad, axis=1, keepdims=True)
    act_grad = act_grad * gate
    act_out[0] = (act * gate).astype(BF16)
    slope = sig * (1.0 + gate_pre * (1.0 - sig))
    pre_out[0, :, :ff] = (act_grad * up_pre * slope).astype(BF16)
    pre_out[0, :, ff:] = (act_grad * silu).astype(BF16)
    high = gate_grad.astype(BF16).astype(F32)
    low = gate_grad - high
    extra = jnp.where(lanes == own, high, jnp.where(lanes == own + experts, low, 0.0))
    extra_out[0] = extra.astype(BF16)


def expert_rows(first, rows, spots, marks, cot_rows, router, weights, cap):
    experts, blocks, block = spots.shape
    shards, _, depth, all_ff = weights.shape
    both = all_ff // 3 * 2
    width = rows.shape[1]
    count = blocks * cap
    one = lambda *shape: pl.BlockSpec((1,) + shape, lambda e, first: (e,) + (0,) * len(shape))
    whole = lambda a: pl.BlockSpec(a.shape, lambda e, first: (0, 0))
    return pl.pallas_call(
        functools.partial(expert_kernel, cap),
        grid_spec=pltpu.PrefetchScalarGridSpec(
            num_scalar_prefetch=1,
            grid=(experts,),
            in_specs=[
                whole(rows),
                one(blocks, block),
                whole(marks),
                one(count, width),
                whole(router),
                pl.BlockSpec((shards, 1, depth, all_ff), lambda e, first: (0, e, 0, 0)),
            ],
            out_specs=[
                one(count, width),
                one(count, both // 2),
                one(count, both),
                one(count, EXTRA),
            ],
        ),
        out_shape=[
            jax.ShapeDtypeStruct((experts, count, width), BF16),
            jax.ShapeDtypeStruct((experts, count, both // 2), BF16),
            jax.ShapeDtypeStruct((experts, count, both), BF16),
            jax.ShapeDtypeStruct((experts, count, EXTRA), BF16),
        ],
        compiler_params=pltpu.CompilerParams(vmem_limit_bytes=VMEM),
        cost_estimate=cost(11),
        name="expert_rows",
    )(first, rows, spots, marks, cot_rows, router, weights)


def rows_back_kernel(cap, shards, left_ref, spot_ref, *refs):
    out_ref, acc = refs[-2:]
    e = pl.program_id(0)
    blocks, block, wide = out_ref.shape
    depth = refs[0].shape[2]

    @pl.when(e == 0)
    def _():
        acc[...] = jnp.zeros_like(acc)

    lane = lax.broadcasted_iota(jnp.int32, spot_ref.shape, 1)
    spot = jnp.sum(jnp.where(lane == e, spot_ref[...], 0), axis=1, keepdims=True)
    puts = [put_rows(spot[b * block : (b + 1) * block], cap) for b in range(blocks)]
    for r in range(shards):
        rows = dot_nt(left_ref[0], refs[r][0, 0]).astype(BF16)
        for b in range(blocks):
            acc[b * block : (b + 1) * block, r * depth : (r + 1) * depth] += dot_nn(
                puts[b], rows[b * cap : (b + 1) * cap, :]
            )
    if len(refs) > shards + 2:
        for b in range(blocks):
            acc[b * block : (b + 1) * block, wide - EXTRA :] += dot_nn(
                puts[b], refs[shards][0, b * cap : (b + 1) * cap, :]
            )

    @pl.when(e == pl.num_programs(0) - 1)
    def _():
        out_ref[...] = acc[...].astype(BF16).reshape(out_ref.shape)


def rows_back(left, weights, at, spot_cols, cap, extra=None):
    experts, count, size = left.shape
    shards, _, depth, _ = weights.shape
    blocks = count // cap
    block = spot_cols.shape[0] // blocks
    width = depth * shards + (0 if extra is None else EXTRA)
    shape = (blocks, block, width)
    one = lambda *shape: pl.BlockSpec((1,) + shape, lambda e: (e,) + (0,) * len(shape))
    shard = lambda r: pl.BlockSpec((1, 1, depth, size), lambda e: (r, e, 0, at))
    extras = [] if extra is None else [extra]
    return pl.pallas_call(
        functools.partial(rows_back_kernel, cap, shards),
        grid=(experts,),
        in_specs=[one(count, size), pl.BlockSpec(spot_cols.shape, lambda e: (0, 0))]
        + [shard(r) for r in range(shards)]
        + [one(count, EXTRA)] * len(extras),
        out_specs=pl.BlockSpec(shape, lambda e: (0, 0, 0)),
        out_shape=jax.ShapeDtypeStruct(shape, BF16),
        scratch_shapes=[pltpu.VMEM((blocks * block, width), F32)],
        compiler_params=pltpu.CompilerParams(vmem_limit_bytes=VMEM),
        cost_estimate=cost(5 if extra is None else 10),
        name="mixtures" if extra is None else "row_grads",
    )(left, spot_cols, *[weights] * shards, *extras)


def expert_grad_kernel(row_a, row_b, cot_a, cot_b, pre_a, pre_b, act_a, act_b, out_ref):
    both = pre_a.shape[2]
    total = dot_tn(row_a[0], pre_a[0]) + dot_tn(row_b[0], pre_b[0])
    out_ref[0, 0, :, :both] = total.astype(BF16)
    total = dot_tn(cot_a[0], act_a[0]) + dot_tn(cot_b[0], act_b[0])
    out_ref[0, 0, :, both:] = total.astype(BF16)


def expert_grads(rows, cots, pres, acts, shards):
    experts, count, width = rows[0].shape
    both, ff = pres[0].shape[2], acts[0].shape[2]
    depth = width // shards
    part = pl.BlockSpec((1, count, depth), lambda e, n: (e, 0, n))
    full = lambda size: pl.BlockSpec((1, count, size), lambda e, n: (e, 0, 0))
    return pl.pallas_call(
        expert_grad_kernel,
        grid=(experts, shards),
        in_specs=[part] * 4 + [full(both)] * 2 + [full(ff)] * 2,
        out_specs=pl.BlockSpec((1, 1, depth, both + ff), lambda e, n: (n, e, 0, 0)),
        out_shape=jax.ShapeDtypeStruct((shards, experts, depth, both + ff), BF16),
        compiler_params=pltpu.CompilerParams(vmem_limit_bytes=VMEM),
        cost_estimate=cost(18),
        name="expert_grads",
    )(rows[0], rows[1], cots[0], cots[1], pres[0], pres[1], acts[0], acts[1])


def body(
    layer_input,
    w_query,
    w_key,
    w_value,
    w_out,
    attn_gain,
    query_gain,
    key_gain,
    ffn_gain,
    w_router,
    w_gate,
    w_up,
    w_down,
    routes,
    pic_starts,
    cotangent,
):
    tok_count, model_width = layer_input.shape
    top_count = routes.shape[1]
    ga_count = lax.axis_size("ga")
    z_count = lax.axis_size("z")
    ea_count = 2 * z_count
    core = lax.axis_index("core")
    chip = lax.axis_index("z")
    local_experts, _, ff = w_gate.shape
    expert_total = local_experts * ea_count
    cap = max(2, 9 * tok_count * top_count // (8 * expert_total))
    group_size = HEADS // KV
    kv_width = KV * HD
    q_width = HEADS * HD

    small = [attn_gain, query_gain, key_gain, ffn_gain, w_router.reshape(-1)]
    small_all = ga_gather_small(jnp.concatenate(small))
    at, smalls = 0, []
    for piece in small:
        smalls.append(small_all[:, at : at + piece.shape[0]].reshape(-1))
        at += piece.shape[0]
    attn_gain_f, query_gain_f, key_gain_f, ffn_gain_f = [s.astype(F32) for s in smalls[:4]]
    router_full = smalls[4].reshape(model_width, expert_total)
    router_wide = jnp.pad(router_full, ((0, 0), (0, EXTRA - expert_total)))

    qkv_weights = (w_query, w_key, w_value)
    qkv_own = jnp.concatenate([core_halves(w)[0] for w in qkv_weights], axis=1)

    marks = jnp.sum(
        (routes[:, :, None] == jnp.arange(EXTRA, dtype=jnp.int32)[None, None, :]).astype(F32), axis=1
    )
    cot_steps = []
    qkv_first = ga_first_hop(after(qkv_own, small_all))
    cot_mine = line_gather(
        after(jnp.concatenate([cotangent, marks.astype(BF16)], axis=1), small_all), steps=cot_steps
    )
    qkv_twin = jnp.concatenate(
        [core_halves(after(w, *cot_steps[0]))[1] for w in qkv_weights], axis=1
    )
    qkv_second = ga_second_hop(qkv_first, 0, 1, cot_steps[1])
    qkv_mine = qkv_first + qkv_second
    qkv_swapped = swap_pieces(qkv_mine[1:] if ga_count == 4 else qkv_mine)
    qkv_other = ([qkv_twin] if ga_count == 4 else []) + qkv_swapped
    cot_mine = after(jnp.concatenate(cot_mine), *qkv_second)
    cot_sides = [cot_mine, swap_core(cot_mine)]
    first_expert = (chip * 2 + core) * local_experts
    mark_sides, spot_rows, spot_cols, cot_rows = [], [], [], []
    before = jnp.tril(jnp.ones((tok_count, tok_count), BF16))
    for side in cot_sides:
        side_marks = side[:, model_width:]
        chosen = lax.dynamic_slice_in_dim(side_marks, first_expert, local_experts, 1)
        chosen = chosen.reshape(z_count, tok_count, local_experts)
        rank = jnp.einsum("ts,bse->bte", before, chosen, preferred_element_type=F32)
        spots = jnp.where(chosen > 0, rank - 1.0, -1.0).astype(jnp.int32)
        mark_sides.append(side_marks)
        spot_rows.append(jnp.transpose(spots, (2, 0, 1)))
        spot_cols.append(spots.reshape(z_count * tok_count, local_experts))
        cot_rows.append(pick(side, spot_rows[-1], cap, model_width))

    ea_index = chip * 2 + core
    positions = ea_index * tok_count + jnp.arange(tok_count, dtype=jnp.int32)
    holder = ((chip - jnp.arange(z_count)) % z_count * 2)[None, :] + jnp.stack([core, 1 - core])[
        :, None
    ]
    key_pos = (holder.reshape(-1, 1) * tok_count + jnp.arange(tok_count)[None, :]).reshape(-1)
    key_pos = key_pos.astype(jnp.int32)
    allowed = allowed_mask(pic_starts[0], positions, key_pos)
    bias = jnp.where(allowed, 0.0, MASKED_SCORE).astype(F32)
    bias_turned = jnp.where(jnp.transpose(allowed), 0.0, MASKED_SCORE).astype(F32)
    frequency = ROPE_THETA ** (-jnp.arange(HD // 2, dtype=F32) * 2.0 / HD)
    angles = positions.astype(F32)[:, None] * frequency[None, :]
    cosine = jnp.concatenate([jnp.cos(angles), jnp.cos(angles)], axis=1)
    sine = jnp.concatenate([-jnp.sin(angles), jnp.sin(angles)], axis=1)
    per_key = max(1, ga_count // KV)
    ga_index = lax.axis_index("ga")
    run = group_size // 2 // per_key
    step = jnp.arange(per_key) ^ (ga_index % per_key)
    own_heads = (step[:, None] * 2 * run + jnp.arange(run)[None, :]).reshape(-1)
    key_place = jnp.arange(KV) ^ (ga_index // per_key)
    place = jnp.concatenate(
        [key_place, own_heads + core * run, own_heads + (1 - core) * run]
    ).astype(jnp.int32)

    input_f = layer_input.astype(F32)
    normed = rms_norm(input_f, attn_gain_f).astype(BF16)
    normed_mine = split_cols(normed, core)
    normed_other = split_cols(normed, 1 - core)
    normed_used = after(normed_mine, bias, bias_turned, cosine, sine)
    qkv = pieces_matmul((normed_used, normed_other), (qkv_mine, qkv_other))
    query_gain_row, key_gain_row = query_gain_f.reshape(1, HD), key_gain_f.reshape(1, HD)
    kv_own = prep_kv(qkv, cosine, sine, key_gain_row)

    out_own, out_twin = core_halves(w_out)
    out_first = ga_first_hop(after(out_own, *qkv_second))
    kv_steps = []
    kv_mine, kv_other = ea_gather(
        kv_own, {2: cot_rows[:1], 3: cot_rows[1:] + out_first[1:]}, kv_steps
    )
    out_second = ga_second_hop(out_first, 0, 1, ())
    out_mine = out_first + out_second
    out_swapped = swap_pieces(out_mine[1:] if ga_count == 4 else out_mine)
    out_other = ([out_twin] if ga_count == 4 else []) + out_swapped
    expert_own = jnp.concatenate([w_gate, w_up, jnp.swapaxes(w_down, 1, 2)], axis=2)
    expert_all = lax.all_gather(after(expert_own, *out_first[1:], *kv_steps[1]), "ga", axis=0)

    att_mine, att_other, log_rows = attend(
        place,
        after(qkv, *out_second),
        kv_mine,
        kv_other,
        bias,
        cosine,
        sine,
        query_gain_row,
    )
    hidden = input_f + pieces_matmul((att_mine, att_other), (out_mine, out_other))
    ffn_in = rms_norm(hidden, ffn_gain_f).astype(BF16)

    row_mine = after(jnp.concatenate(line_gather(ffn_in)), expert_all)
    row_sides = [row_mine, swap_core(row_mine)]
    logits = dot_nn(ffn_in, router_full)
    own_marks = marks[:, :expert_total] > 0
    peak = jnp.max(jnp.where(own_marks, logits, MASKED_SCORE), axis=1, keepdims=True)
    weights = jnp.exp(jnp.where(own_marks, logits - peak, MASKED_SCORE))
    gates = weights / jnp.sum(weights, axis=1, keepdims=True)

    first = jnp.stack([first_expert, expert_total]).astype(jnp.int32)
    picked, acts, pres, extras = [], [], [], []
    for side in range(2):
        rows, act, pre, extra = expert_rows(
            first,
            row_sides[side],
            spot_rows[side],
            mark_sides[side],
            cot_rows[side],
            router_wide,
            expert_all,
            cap,
        )
        picked.append(rows)
        acts.append(act)
        pres.append(pre)
        extras.append(extra)
    expert_grad = expert_grads(picked, cot_rows, pres, acts, ga_count)
    expert_sum = lax.psum_scatter(expert_grad, "ga", scatter_dimension=0)
    row_other = rows_back(
        after(pres[1], expert_grad), expert_all, 0, spot_cols[1], cap, extras[1]
    )
    row_mine = rows_back(
        after(pres[0], row_other), expert_all, 0, spot_cols[0], cap, extras[0]
    )
    rows = LineSum(core_slots(row_mine, row_other))
    held = rows.step()
    mix_other = rows_back(after(acts[1], rows.slots[1]), expert_all, 2, spot_cols[1], cap)
    rows.step(mix_other)
    mix_mine = rows_back(after(acts[0], *held), expert_all, 2, spot_cols[0], cap)
    mix = LineSum(core_slots(mix_mine, mix_other))
    rows.step(mix_mine)
    row_sum = after(rows.result(), *mix.slots)

    grad_out = cotangent.astype(F32)
    gate_grad = (
        row_sum[:, model_width : model_width + expert_total].astype(F32)
        + row_sum[:, model_width + expert_total : model_width + 2 * expert_total].astype(F32)
    )
    inner = jnp.sum(gates * gate_grad, axis=1, keepdims=True)
    logit_grad = gates * (gate_grad - inner)
    router_grad = lax.dot_general(
        ffn_in.astype(F32), logit_grad, (((0,), (0,)), ((), ())), precision=PRECISE
    )
    ffn_in_grad = row_sum[:, :model_width].astype(F32) + jnp.dot(
        logit_grad, router_full.astype(F32).T, precision=PRECISE
    )
    unused, ffn_back = jax.vjp(rms_norm, hidden, ffn_gain_f)
    hidden_part, ffn_gain_grad = ffn_back(ffn_in_grad)
    hidden_grad = grad_out + hidden_part
    branch_grad = hidden_grad.astype(BF16)
    out_terms = [dot_tn(device_cols(a), branch_grad) for a in (att_mine, att_other)]
    out_terms[1] = out_terms[1].astype(BF16)
    att_grads = pieces_back(after(branch_grad, out_terms[1]), out_mine + out_other, BF16)
    raw_grads, kv_grads, gain_grads = [], [], []

    def back(head, *before):
        raw_grad, kv_grad, gain_grad = attend_back(
            head,
            1,
            place,
            qkv,
            kv_mine,
            kv_other,
            bias_turned,
            cosine,
            sine,
            query_gain_row,
            after(att_grads, *before),
            (att_mine, att_other),
            log_rows,
        )
        raw_grads.append(raw_grad)
        kv_grads.append(kv_grad)
        gain_grads.append(gain_grad[0])

    def weight_terms(grad):
        return dot_tn(normed_mine, grad), dot_tn(normed_other, grad).astype(BF16)

    held = [mix.step(*rows.held)]
    back(0, out_terms[1], expert_sum, *mix.sent)
    held.append(mix.step(raw_grads[0]))
    out_total = core_sum(*out_terms)
    out_share = lax.psum_scatter(out_total, "ga", scatter_dimension=0, tiled=True)
    back(1, raw_grads[0], out_total, *held[0])
    held.append(mix.step(raw_grads[1]))
    query_parts = [jnp.concatenate(raw_grads[:2], axis=1)]
    query_terms = [weight_terms(query_parts[0])]
    back(2, raw_grads[1], *held[1])
    query_totals = [core_sum(*query_terms[0])]
    back(3, raw_grads[2], query_terms[0][1], out_share, *held[2])
    query_firsts = [ga_sum_first(query_totals[0])]
    mix_sum = mix.result()
    layer_output = (hidden + mix_sum.astype(F32)).astype(BF16)
    query_parts.append(jnp.concatenate(raw_grads[2:], axis=1))
    query_terms.append(weight_terms(query_parts[1]))
    query_gain_grad = sum(gain_grads)
    kv_grad = after(jnp.concatenate(kv_grads, axis=1), *held[2])
    kv_grad = kv_grad.reshape(2, z_count, tok_count, 2 * kv_width)
    keys_values = LineSum(core_slots(kv_grad[0], kv_grad[1]))
    keys_values.step(query_terms[1][1], *query_firsts[0])
    query_shares = [ga_sum_second(query_firsts[0])]
    query_totals.append(core_sum(*query_terms[1]))
    out_all = z_all_sum(out_share)
    keys_values.step(query_totals[1], out_all)
    query_firsts.append(ga_sum_first(after(query_totals[1], query_shares[0])))
    keys_values.step(query_shares[0])
    kv_raw_grad, key_gain_grad = kv_back(
        qkv, after(keys_values.result(), *query_firsts[1]), cosine, sine, key_gain_row
    )
    key_gain_grad = key_gain_grad[0]
    chunks = query_parts + [kv_raw_grad]
    qkv_grad = jnp.concatenate(chunks, axis=1)
    both_grads = pieces_back(qkv_grad, qkv_mine + qkv_other, F32)
    query_shares.append(ga_sum_second(query_firsts[1], [both_grads]))
    kv_total = core_sum(*weight_terms(kv_raw_grad))
    kv_first = ga_sum_first(after(kv_total, query_shares[1]))
    query_alls = [z_all_sum(after(share, out_all)) for share in query_shares]
    kv_share = ga_sum_second((kv_first[0],) + tuple(after(p, *query_alls) for p in kv_first[1:]))
    kv_sum = whole_shard([z_all_sum_small(kv_share)])
    out_sum = whole_shard([out_all])
    query_sum = whole_shard(query_alls)
    key_sum, value_sum = kv_sum[:, :kv_width], kv_sum[:, kv_width:]
    both_grads = after(both_grads, *query_alls)
    half_width = model_width // 2
    normed_grad = join_cols(both_grads[:, :half_width], both_grads[:, half_width:])
    unused, attn_back = jax.vjp(rms_norm, input_f, attn_gain_f)
    input_part, attn_gain_grad = attn_back(normed_grad)
    input_grad = (hidden_grad + input_part).astype(BF16)

    tiny = [attn_gain_grad, query_gain_grad, key_gain_grad, ffn_gain_grad, router_grad.reshape(-1)]
    tiny_own = sum_small(jnp.concatenate([t.reshape(ga_count, -1) for t in tiny], axis=1))
    at, tiny_sums = 0, []
    for piece in tiny:
        width = piece.shape[0] // ga_count
        tiny_sums.append(tiny_own[at : at + width])
        at += width
    attn_sum, qgain_sum, kgain_sum, ffn_sum, router_sum = tiny_sums
    return (
        layer_output,
        input_grad,
        query_sum,
        key_sum,
        value_sum,
        out_sum,
        attn_sum,
        qgain_sum,
        kgain_sum,
        ffn_sum,
        router_sum.reshape(-1, expert_total),
        expert_sum[:, :, :ff].astype(F32),
        expert_sum[:, :, ff : 2 * ff].astype(F32),
        jnp.swapaxes(expert_sum[:, :, 2 * ff :], 1, 2).astype(F32),
    )


def solution(mesh):
    ga_count, ea_count = mesh.shape["ga"], mesh.shape["ea"]
    inner = Mesh(mesh.devices.reshape(ga_count, ea_count // 2, 2), ("ga", "z", "core"))
    everyone = ("ga", "z", "core")
    owners = ("z", "core")
    in_specs = (
        P(everyone, None),
        P("ga", None),
        P("ga", None),
        P("ga", None),
        P("ga", None),
        P("ga"),
        P("ga"),
        P("ga"),
        P("ga"),
        P("ga", None),
        P(owners, "ga", None),
        P(owners, "ga", None),
        P(owners, None, "ga"),
        P(everyone, None),
        P("ga", None),
        P(everyone, None),
    )
    out_specs = (
        P(everyone, None),
        P(everyone, None),
        P("ga", None),
        P("ga", None),
        P("ga", None),
        P("ga", None),
        P("ga"),
        P("ga"),
        P("ga"),
        P("ga"),
        P("ga", None),
        P(owners, "ga", None),
        P(owners, "ga", None),
        P(owners, None, "ga"),
    )
    return jax.shard_map(body, mesh=inner, in_specs=in_specs, out_specs=out_specs, check_vma=False)
```

```python
import functools

import jax
import jax.numpy as jnp
from jax import lax
from jax.experimental import pallas as pl
from jax.experimental.pallas import tpu as pltpu
from jax.sharding import Mesh
from jax.sharding import PartitionSpec as P

HEADS = 32
KV = 4
HD = 128
PIC = 256


NORM_EPS = 1e-06
ROPE_THETA = 1000000.0
MASKED_SCORE = -1e30
PRECISE = lax.Precision.HIGHEST
F32 = jnp.float32
BF16 = jnp.bfloat16
EXTRA = 128
LOG2E = 1.4426950408889634
VMEM = 56 << 20


def rms_norm(values, norm_gain):
    inverse = lax.rsqrt(jnp.mean(values * values, axis=-1, keepdims=True) + NORM_EPS)
    return values * inverse * norm_gain


def piece_ids(starts, positions):
    inside = (
        (starts[:, None] >= 0)
        & (positions[None, :] >= starts[:, None])
        & (positions[None, :] < starts[:, None] + PIC)
    )
    labels = jnp.arange(1, starts.shape[0] + 1, dtype=jnp.int32)[:, None]
    return jnp.sum(jnp.where(inside, labels, 0), axis=0)


def allowed_mask(starts, query_pos, key_pos):
    query_piece = piece_ids(starts, query_pos)
    key_piece = piece_ids(starts, key_pos)
    causal = key_pos[None, :] <= query_pos[:, None]
    shared = (query_piece[:, None] == key_piece[None, :]) & (query_piece[:, None] > 0)
    return causal | shared


def dot_nn(left, right):
    return lax.dot_general(left, right, (((1,), (0,)), ((), ())), preferred_element_type=F32)


def dot_tn(left, right):
    return lax.dot_general(left, right, (((0,), (0,)), ((), ())), preferred_element_type=F32)


def dot_nt(left, right):
    return lax.dot_general(left, right, (((1,), (1,)), ((), ())), preferred_element_type=F32)


def after(value, *others):
    return lax.optimization_barrier((value,) + others)[0]


def swap_core(value):
    return lax.ppermute(value, "core", [(0, 1), (1, 0)])


def swap_axis(value, axis, bit):
    return lax.ppermute(value, axis, [(i, i ^ bit) for i in range(lax.axis_size(axis))])


def plus(*terms):
    total = terms[0].astype(F32)
    for term in terms[1:]:
        total = total + term.astype(F32)
    return total.astype(BF16)


def line_gather(value, before=None, steps=None):
    count = lax.axis_size("z")
    place = lax.axis_index("z")
    below, above = {}, {}
    up = down = value
    for step in range(1, count):
        if before and step in before:
            up, down = lax.optimization_barrier((up, down) + tuple(before[step]))[:2]
        up = lax.ppermute(up, "z", [(p, p + 1) for p in range(step - 1, count - 1)])
        down = lax.ppermute(down, "z", [(p, p - 1) for p in range(1, count - step + 1)])
        up, down = lax.optimization_barrier((up, down))
        below[step], above[step] = up, down
        if steps is not None:
            steps.append((up, down))
    return [value] + [
        jnp.where(place >= step, below[step], above[count - step]) for step in range(1, count)
    ]


class LineSum:
    def __init__(self, slots):
        self.slots, self.done = slots, 0

    def step(self, *before):
        count = lax.axis_size("z")
        self.done += 1
        up, down = self.slots[self.done], self.slots[count - self.done]
        if before:
            up, down = lax.optimization_barrier((up, down) + before)[:2]
        if self.done > 1:
            up, down = plus(up, self.held[0]), plus(down, self.held[1])
        self.sent = (up, down)
        up = lax.ppermute(up, "z", [(p, p + 1) for p in range(self.done)])
        down = lax.ppermute(
            down, "z", [(p, p - 1) for p in range(count - 1, count - 1 - self.done, -1)]
        )
        self.held = lax.optimization_barrier((up, down))
        return self.held

    def result(self):
        while self.done < lax.axis_size("z") - 1:
            self.step()
        return plus(self.slots[0], *self.held)


def ea_gather(value, before=None, steps=None):
    mine = jnp.concatenate(line_gather(value, before, steps))
    return mine, swap_core(mine)


def core_slots(mine, other):
    got = swap_core(other)
    return [plus(mine[s], got[s]) for s in range(lax.axis_size("z"))]


def z_all_sum(value):
    return lax.psum(value, "z")


def z_all_sum_small(value):
    count = lax.axis_size("z")
    place = lax.axis_index("z")
    bits, bit = [], 1
    while bit < count:
        rows = value.shape[0] // 2
        upper = (place // bit) % 2
        keep = lax.dynamic_slice_in_dim(value, upper * rows, rows, 0)
        send = lax.dynamic_slice_in_dim(value, (1 - upper) * rows, rows, 0)
        value = plus(keep, swap_axis(send, "z", bit))
        bits.append(bit)
        bit *= 2
    for bit in reversed(bits):
        got = swap_axis(value, "z", bit)
        upper = (place // bit) % 2
        low, high = jnp.where(upper == 0, value, got), jnp.where(upper == 0, got, value)
        value = jnp.concatenate([low, high])
    return value


def ga_order():
    return lax.axis_index("ga") ^ jnp.arange(lax.axis_size("ga"))


def ga_first_hop(value):
    if lax.axis_size("ga") != 4:
        whole = lax.all_gather(value, "ga", axis=0)
        return [jnp.take(whole, ga_order(), axis=0).reshape((-1,) + value.shape[1:])]
    return [value, swap_axis(value, "ga", 1), swap_axis(value, "ga", 2)]


def ga_second_hop(first, part, parts, before):
    if len(first) == 1:
        return []
    half = first[0].shape[0] // 2
    rows = half // parts
    to_y = first[1][part * rows : (part + 1) * rows]
    to_x = first[2][half + part * rows : half + (part + 1) * rows]
    to_y, to_x = lax.optimization_barrier((to_y, to_x) + tuple(before))[:2]
    return [swap_axis(to_y, "ga", 2), swap_axis(to_x, "ga", 1)]


def ga_sum_first(value):
    if lax.axis_size("ga") != 4:
        return (value,)
    rows = value.shape[0] // 4
    half = rows // 2
    own, for_x, for_y = [value[r * rows : (r + 1) * rows] for r in range(3)]
    low = swap_axis(value[3 * rows : 3 * rows + half], "ga", 1)
    high = swap_axis(value[3 * rows + half :], "ga", 2)
    to_x = jnp.concatenate([for_x[:half], plus(for_x[half:], high)])
    to_y = jnp.concatenate([plus(for_y[:half], low), for_y[half:]])
    return own, to_x, to_y


def ga_sum_second(parts, before=()):
    if len(parts) == 1:
        return ga_sum_whole(parts[0])
    own, to_x, to_y = parts
    terms = (own, swap_axis(to_x, "ga", 1), swap_axis(to_y, "ga", 2))
    return plus(*lax.optimization_barrier(terms + tuple(before))[:3])


def ga_sum_whole(value):
    blocks = value.reshape((lax.axis_size("ga"), -1) + value.shape[1:])
    blocks = jnp.take(blocks, ga_order(), axis=0).reshape(value.shape)
    return lax.psum_scatter(blocks, "ga", scatter_dimension=0, tiled=True)


def ga_gather_small(value):
    count = lax.axis_size("ga")
    held, bit = value[None], 1
    while bit < count:
        held = jnp.concatenate([held, swap_axis(held, "ga", bit)])
        bit *= 2
    return jnp.take(held, ga_order(), axis=0)


def sum_small(rows):
    total = rows + swap_core(rows)
    count, bit = lax.axis_size("z"), 1
    while bit < count:
        total = total + swap_axis(total, "z", bit)
        bit *= 2
    count = lax.axis_size("ga")
    total = jnp.take(total, ga_order(), axis=0)
    while count > 1:
        count //= 2
        total = total[:count] + swap_axis(total[count:], "ga", count)
    return total[0]


def core_halves(value):
    core = lax.axis_index("core")
    rows = value.shape[0] // 2
    return (
        lax.dynamic_slice_in_dim(value, core * rows, rows, 0),
        lax.dynamic_slice_in_dim(value, (1 - core) * rows, rows, 0),
    )


def swap_pieces(pieces):
    return [swap_core(piece) for piece in pieces]


def split_cols(value, half):
    groups = lax.axis_size("ga")
    width = value.shape[1] // groups // 2
    order = ga_order()
    return jnp.concatenate(
        [
            lax.dynamic_slice_in_dim(value, (order[r] * 2 + half) * width, width, 1)
            for r in range(groups)
        ],
        axis=1,
    )


def device_cols(value):
    groups = lax.axis_size("ga")
    width = value.shape[1] // groups
    order = ga_order()
    return jnp.concatenate(
        [lax.dynamic_slice_in_dim(value, order[g] * width, width, 1) for g in range(groups)], axis=1
    )


def join_cols(mine, other):
    groups = lax.axis_size("ga")
    core = lax.axis_index("core")
    width = mine.shape[1] // groups
    order = ga_order()
    parts = []
    for g in range(groups):
        a = lax.dynamic_slice_in_dim(mine, order[g] * width, width, 1)
        b = lax.dynamic_slice_in_dim(other, order[g] * width, width, 1)
        parts += [jnp.where(core == 0, a, b), jnp.where(core == 0, b, a)]
    return jnp.concatenate(parts, axis=1)


def core_sum(mine, other, before=()):
    got = swap_core(other)
    return plus(mine, after(got, *before) if before else got)


def whole_shard(shares):
    core = lax.axis_index("core")
    rows = shares[0].shape[0]
    out = jnp.zeros((2 * rows, sum(share.shape[1] for share in shares)), F32)
    at = 0
    for share in shares:
        for half, part in ((core, share), (1 - core, swap_core(share))):
            out = lax.dynamic_update_slice(out, part.astype(F32), (half * rows, at))
        at += share.shape[1]
    return out


def cost(micros):
    return pl.CostEstimate(flops=micros * 10**9, bytes_accessed=1024, transcendentals=0)


def pieces_kernel(plan, *refs):
    acc = None
    lefts, out_ref = refs[: 1 + max(which for which, _, _ in plan)], refs[-1]
    for (which, at, size), ref in zip(plan, refs[len(lefts) : -1]):
        term = dot_nn(lefts[which][:, at : at + size], ref[...])
        acc = term if acc is None else acc + term
    out_ref[...] = acc


def pieces_matmul(lefts, piece_lists):
    plan, pieces = [], []
    for which, some in enumerate(piece_lists):
        at = 0
        for piece in some:
            plan.append((which, at, piece.shape[0]))
            pieces.append(piece)
            at += piece.shape[0]
    rows, width = lefts[0].shape[0], pieces[0].shape[1]
    tile = min(1024 if width > 4096 else 512, width)
    return pl.pallas_call(
        functools.partial(pieces_kernel, plan),
        grid=(width // tile,),
        in_specs=[pl.BlockSpec(left.shape, lambda n: (0, 0)) for left in lefts]
        + [pl.BlockSpec((piece.shape[0], tile), lambda n: (0, n)) for piece in pieces],
        out_specs=pl.BlockSpec((rows, tile), lambda n: (0, n)),
        out_shape=jax.ShapeDtypeStruct((rows, width), F32),
        compiler_params=pltpu.CompilerParams(vmem_limit_bytes=VMEM),
        cost_estimate=cost(6),
        name="dense_matmul",
    )(*lefts, *pieces)


def pieces_back_kernel(sizes, left_ref, *refs):
    n = pl.program_id(0)
    out_ref, acc = refs[-2:]

    @pl.when(n == 0)
    def _():
        acc[...] = jnp.zeros_like(acc)

    at = 0
    for ref, size in zip(refs[:-2], sizes):
        acc[:, at : at + size] += dot_nt(left_ref[...], ref[...])
        at += size

    @pl.when(n == pl.num_programs(0) - 1)
    def _():
        out_ref[...] = acc[...].astype(out_ref.dtype)


def pieces_back(left, pieces, dtype):
    rows, width = left.shape
    tile = min(512, width)
    sizes = [piece.shape[0] for piece in pieces]
    return pl.pallas_call(
        functools.partial(pieces_back_kernel, sizes),
        grid=(width // tile,),
        in_specs=[pl.BlockSpec((rows, tile), lambda n: (0, n))]
        + [pl.BlockSpec((size, tile), lambda n: (0, n)) for size in sizes],
        out_specs=pl.BlockSpec((rows, sum(sizes)), lambda n: (0, 0)),
        out_shape=jax.ShapeDtypeStruct((rows, sum(sizes)), dtype),
        scratch_shapes=[pltpu.VMEM((rows, sum(sizes)), F32)],
        compiler_params=pltpu.CompilerParams(vmem_limit_bytes=VMEM),
        cost_estimate=cost(6),
        name="dense_back",
    )(left, *pieces)


def prep_head(raw, gain, cosine, sine):
    inverse = lax.rsqrt(jnp.mean(raw * raw, axis=-1, keepdims=True) + NORM_EPS)
    scaled = raw * inverse * gain
    turned = scaled * cosine + pltpu.roll(scaled, HD // 2, 1) * sine
    return turned.astype(BF16), inverse


def head_cols(index):
    return pl.ds(pl.multiple_of(index * HD, HD), HD)


def prep_kv_kernel(raw_ref, cos_ref, sin_ref, gain_ref, out_ref):
    for h in range(KV):
        span = slice(h * HD, (h + 1) * HD)
        keys, _ = prep_head(raw_ref[:, span], gain_ref[...], cos_ref[...], sin_ref[...])
        out_ref[:, span] = keys
    out_ref[:, KV * HD :] = raw_ref[:, KV * HD :].astype(BF16)


def prep_kv(raw, cosine, sine, gain):
    rows, width = raw.shape[0], 2 * KV * HD
    whole = lambda a: pl.BlockSpec(a.shape, lambda i: (0, 0))
    return pl.pallas_call(
        prep_kv_kernel,
        grid=(1,),
        in_specs=[
            pl.BlockSpec((rows, width), lambda i: (0, raw.shape[1] // width - 1)),
            whole(cosine),
            whole(sine),
            whole(gain),
        ],
        out_specs=pl.BlockSpec((rows, width), lambda i: (0, 0)),
        out_shape=jax.ShapeDtypeStruct((rows, width), BF16),
        compiler_params=pltpu.CompilerParams(vmem_limit_bytes=VMEM),
        cost_estimate=cost(1),
        name="prep_kv",
    )(raw, cosine, sine, gain)


def head_back(raw, inverse, grad, gain, cosine, sine):
    scaled_grad = grad * cosine + pltpu.roll(grad * sine, HD // 2, 1)
    unit = raw * inverse
    gain_grad = jnp.sum(scaled_grad * unit, axis=0, keepdims=True)
    unit_grad = scaled_grad * gain
    mean = jnp.mean(unit_grad * unit, axis=-1, keepdims=True)
    return inverse * (unit_grad - unit * mean), gain_grad


def kv_back_kernel(raw_ref, grad_ref, cos_ref, sin_ref, gain_ref, out_ref, gain_grad_ref):
    total = jnp.zeros((1, HD), F32)
    for h in range(KV):
        span = slice(h * HD, (h + 1) * HD)
        raw = raw_ref[:, span]
        cosine, sine, gain = cos_ref[...], sin_ref[...], gain_ref[...]
        _, inverse = prep_head(raw, gain, cosine, sine)
        grad = grad_ref[:, 2 * h * HD : (2 * h + 1) * HD].astype(F32)
        raw_grad, gain_grad = head_back(raw, inverse, grad, gain, cosine, sine)
        out_ref[:, span] = raw_grad.astype(BF16)
        out_ref[:, (KV + h) * HD : (KV + h + 1) * HD] = grad_ref[
            :, (2 * h + 1) * HD : (2 * h + 2) * HD
        ]
        total = total + gain_grad
    gain_grad_ref[...] = jnp.broadcast_to(total, gain_grad_ref.shape)


def kv_back(raw, grad, cosine, sine, gain):
    rows, width = raw.shape[0], 2 * KV * HD
    whole = lambda a: pl.BlockSpec(a.shape, lambda i: (0, 0))
    return pl.pallas_call(
        kv_back_kernel,
        grid=(1,),
        in_specs=[
            pl.BlockSpec((rows, width), lambda i: (0, raw.shape[1] // width - 1)),
            whole(grad),
            whole(cosine),
            whole(sine),
            whole(gain),
        ],
        out_specs=[
            pl.BlockSpec((rows, width), lambda i: (0, 0)),
            pl.BlockSpec((8, HD), lambda i: (0, 0)),
        ],
        out_shape=[
            jax.ShapeDtypeStruct((rows, width), BF16),
            jax.ShapeDtypeStruct((8, HD), F32),
        ],
        compiler_params=pltpu.CompilerParams(vmem_limit_bytes=VMEM),
        cost_estimate=cost(1),
        name="kv_back",
    )(raw, grad, cosine, sine, gain)


def attend_kernel(
    place,
    raw_ref,
    key_a,
    key_b,
    value_a,
    value_b,
    bias_ref,
    cos_ref,
    sin_ref,
    gain_ref,
    mine_ref,
    other_ref,
    log_ref,
):
    half = key_a.shape[0]
    chunk = min(512, half)
    to_log2 = LOG2E * HD**-0.5
    count = raw_ref.shape[1] // HD

    def one_head(at_head, out_ref, column):
        head = place[KV + at_head]
        query, _ = prep_head(
            raw_ref[:, head_cols(head)], gain_ref[...], cos_ref[...], sin_ref[...]
        )
        total = jnp.zeros((query.shape[0], 1), F32)
        acc = jnp.zeros(query.shape, F32)
        for side, (key_ref, value_ref) in enumerate(((key_a, value_a), (key_b, value_b))):
            for at in range(0, half, chunk):
                scores = dot_nt(query, key_ref[at : at + chunk, :])
                first = side * half + at
                weights = jnp.exp2(scores * to_log2 + bias_ref[:, first : first + chunk])
                total = total + jnp.sum(weights, axis=1, keepdims=True)
                acc = acc + dot_nn(weights.astype(BF16), value_ref[at : at + chunk, :])
        out_ref[:, head_cols(column)] = (acc / total).astype(BF16)
        logs = jnp.transpose(jnp.broadcast_to(jnp.log2(total), query.shape))
        log_ref[0, pl.ds(at_head, 1), :] = logs[0:1, :]

    @pl.loop(0, count // 2)
    def _(i):
        one_head(i, mine_ref, i)
        one_head(count // 2 + i, other_ref, i)


def attend_specs(rows, group, half, tables):
    whole = lambda h, place: (0, 0)
    side = lambda first: pl.BlockSpec((half, HD), lambda h, place: (0, first + h))
    return [
        pl.BlockSpec((rows, group), lambda h, place: (0, h)),
        side(0),
        side(0),
        side(KV),
        side(KV),
    ] + [pl.BlockSpec(t.shape, whole) for t in tables]


def attend(place, raw, kv_mine, kv_other, bias, cosine, sine, gain):
    rows = raw.shape[0]
    group = HEADS * HD // KV
    half = kv_mine.shape[0]
    tables = (bias, cosine, sine, gain)
    half_spec = pl.BlockSpec((rows, group // 2), lambda h, place: (0, place[h]))
    return pl.pallas_call(
        attend_kernel,
        grid_spec=pltpu.PrefetchScalarGridSpec(
            num_scalar_prefetch=1,
            grid=(KV,),
            in_specs=attend_specs(rows, group, half, tables),
            out_specs=[
                half_spec,
                half_spec,
                pl.BlockSpec((1, HEADS // KV, rows), lambda h, place: (h, 0, 0)),
            ],
        ),
        out_shape=[
            jax.ShapeDtypeStruct((rows, HEADS * HD // 2), BF16),
            jax.ShapeDtypeStruct((rows, HEADS * HD // 2), BF16),
            jax.ShapeDtypeStruct((KV, HEADS // KV, rows), F32),
        ],
        compiler_params=pltpu.CompilerParams(vmem_limit_bytes=VMEM),
        cost_estimate=cost(2),
        name="attend",
    )(place, raw, kv_mine, kv_other, kv_mine, kv_other, *tables)


def attend_back_kernel(
    place,
    raw_ref,
    key_a,
    key_b,
    value_a,
    value_b,
    bias_ref,
    cos_ref,
    sin_ref,
    gain_ref,
    grad_mine,
    grad_other,
    out_mine,
    out_other,
    log_ref,
    raw_grad_ref,
    kv_grad_ref,
    gain_grad_ref,
    key_acc,
    value_acc,
):
    h = pl.program_id(0)
    half = key_a.shape[0]
    chunk = min(512, half)
    scale = HD**-0.5
    to_log2 = LOG2E * scale
    count = raw_ref.shape[1] // HD
    key_acc[...] = jnp.zeros_like(key_acc)
    value_acc[...] = jnp.zeros_like(value_acc)

    @pl.when(h == 0)
    def _():
        gain_grad_ref[...] = jnp.zeros_like(gain_grad_ref)

    def one_head(at_head, grad_ref, out_ref, column):
        head = place[KV + at_head]
        raw = raw_ref[:, head_cols(head)]
        cosine, sine, gain = cos_ref[...], sin_ref[...], gain_ref[...]
        query, inverse = prep_head(raw, gain, cosine, sine)
        grad = grad_ref[:, head_cols(column)]
        product = grad.astype(F32) * out_ref[:, head_cols(column)].astype(F32)
        inner = jnp.sum(jnp.transpose(product), axis=0, keepdims=True)
        logs = log_ref[0, pl.ds(at_head, 1), :]
        query_grad = jnp.zeros(query.shape, F32)
        for side, (key_ref, value_ref) in enumerate(((key_a, value_a), (key_b, value_b))):
            for at in range(0, half, chunk):
                keys = key_ref[at : at + chunk, :]
                first = side * half + at
                span = slice(first, first + chunk)
                scores = dot_nt(keys, query)
                probs = jnp.exp2(scores * to_log2 + bias_ref[span, :] - logs)
                prob_grad = dot_nt(value_ref[at : at + chunk, :], grad)
                score_grad = (probs * (prob_grad - inner)).astype(BF16)
                value_acc[span, :] += dot_nn(probs.astype(BF16), grad)
                key_acc[span, :] += dot_nn(score_grad, query)
                query_grad = query_grad + dot_tn(score_grad, keys)
        query_grad = (query_grad * scale).astype(BF16).astype(F32)
        raw_grad, gain_grad = head_back(raw, inverse, query_grad, gain, cosine, sine)
        gain_grad_ref[0:1, :] += gain_grad
        raw_grad_ref[:, head_cols(head)] = raw_grad.astype(BF16)

    @pl.loop(0, count // 2)
    def _(i):
        one_head(i, grad_mine, out_mine, i)
        one_head(count // 2 + i, grad_other, out_other, i)

    heads = kv_grad_ref.shape[1] // HD // 2
    kv_grad_ref[:, head_cols(h)] = (key_acc[...] * scale).astype(BF16)
    kv_grad_ref[:, head_cols(heads + h)] = value_acc[...].astype(BF16)


def attend_back(
    first, count, place, raw, kv_mine, kv_other, bias, cosine, sine, gain, grad, outs, logs
):
    rows = raw.shape[0]
    group = HEADS * HD // KV
    half = kv_mine.shape[0]
    tables = (bias, cosine, sine, gain)
    half_spec = pl.BlockSpec((rows, group // 2), lambda h, place: (0, place[first + h]))
    other_spec = pl.BlockSpec((rows, group // 2), lambda h, place: (0, KV + place[first + h]))
    whole = lambda h, place: (0, 0)
    side = lambda at: pl.BlockSpec((half, HD), lambda h, place: (0, at + first + h))
    return pl.pallas_call(
        attend_back_kernel,
        grid_spec=pltpu.PrefetchScalarGridSpec(
            num_scalar_prefetch=1,
            grid=(count,),
            in_specs=[
                pl.BlockSpec((rows, group), lambda h, place: (0, first + h)),
                side(0),
                side(0),
                side(KV),
                side(KV),
            ]
            + [pl.BlockSpec(t.shape, whole) for t in tables]
            + [half_spec, other_spec, half_spec, half_spec]
            + [pl.BlockSpec((1,) + logs.shape[1:], lambda h, place: (first + h, 0, 0))],
            out_specs=[
                pl.BlockSpec((rows, group), lambda h, place: (0, h)),
                pl.BlockSpec((2 * half, 2 * count * HD), whole),
                pl.BlockSpec((8, HD), whole),
            ],
            scratch_shapes=[pltpu.VMEM((2 * half, HD), F32), pltpu.VMEM((2 * half, HD), F32)],
        ),
        out_shape=[
            jax.ShapeDtypeStruct((rows, count * group), BF16),
            jax.ShapeDtypeStruct((2 * half, 2 * count * HD), BF16),
            jax.ShapeDtypeStruct((8, HD), F32),
        ],
        compiler_params=pltpu.CompilerParams(vmem_limit_bytes=VMEM),
        cost_estimate=cost(9),
        name="attend_back",
    )(place, raw, kv_mine, kv_other, kv_mine, kv_other, *tables, grad, grad, *outs, logs)


def pick_rows(spot_row, cap):
    places = lax.broadcasted_iota(jnp.int32, (cap, spot_row.shape[1]), 0)
    return jnp.where(places == spot_row, 1.0, 0.0).astype(BF16)


def put_rows(spot_col, cap):
    places = lax.broadcasted_iota(jnp.int32, (spot_col.shape[0], cap), 1)
    return jnp.where(places == spot_col, 1.0, 0.0).astype(BF16)


def pick_kernel(cap, rows_ref, spot_ref, out_ref):
    block = spot_ref.shape[2]
    for e in range(spot_ref.shape[0]):
        for b in range(spot_ref.shape[1]):
            pick = pick_rows(spot_ref[e, b : b + 1, :], cap)
            rows = rows_ref[b * block : (b + 1) * block, :]
            out_ref[e, b * cap : (b + 1) * cap, :] = dot_nn(pick, rows).astype(BF16)


def pick(rows, spots, cap, width):
    experts, blocks, block = spots.shape
    tile = min(512, width)
    return pl.pallas_call(
        functools.partial(pick_kernel, cap),
        grid=(width // tile,),
        in_specs=[
            pl.BlockSpec((blocks * block, tile), lambda n: (0, n)),
            pl.BlockSpec(spots.shape, lambda n: (0, 0, 0)),
        ],
        out_specs=pl.BlockSpec((experts, blocks * cap, tile), lambda n: (0, 0, n)),
        out_shape=jax.ShapeDtypeStruct((experts, blocks * cap, width), BF16),
        compiler_params=pltpu.CompilerParams(vmem_limit_bytes=VMEM),
        cost_estimate=cost(3),
        name="pick",
    )(rows, spots)


def expert_kernel(
    cap,
    first_ref,
    rows_ref,
    spot_ref,
    mark_ref,
    cot_ref,
    router_ref,
    weight_ref,
    row_out,
    act_out,
    pre_out,
    extra_out,
):
    shards, _, depth, all_ff = weight_ref.shape
    ff = all_ff // 3
    experts = first_ref[1]
    block = spot_ref.shape[2]
    blocks = spot_ref.shape[1]
    marks = []
    for b in range(blocks):
        pick = pick_rows(spot_ref[0, b : b + 1, :], cap)
        span = slice(b * block, (b + 1) * block)
        row_out[0, b * cap : (b + 1) * cap, :] = dot_nn(pick, rows_ref[span, :]).astype(BF16)
        marks.append(dot_nn(pick, mark_ref[span, :]))
    marked = jnp.concatenate(marks, axis=0) > 0.5
    rows = row_out[0]
    logits = dot_nn(rows, router_ref[...])
    peak = jnp.max(jnp.where(marked, logits, MASKED_SCORE), axis=1, keepdims=True)
    weights = jnp.where(marked, jnp.exp(jnp.where(marked, logits - peak, 0.0)), 0.0)
    lanes = lax.broadcasted_iota(jnp.int32, weights.shape, 1)
    own = first_ref[0] + pl.program_id(0)
    total = jnp.sum(weights, axis=1, keepdims=True)
    gate = jnp.sum(jnp.where(lanes == own, weights, 0.0), axis=1, keepdims=True)
    gate = gate / jnp.where(total > 0.0, total, 1.0)
    pre = dot_nn(rows, weight_ref[:, :, :, : 2 * ff].reshape(shards * depth, 2 * ff))
    act_grad = dot_nn(cot_ref[0], weight_ref[:, :, :, 2 * ff :].reshape(shards * depth, ff))
    gate_pre, up_pre = pre[:, :ff], pre[:, ff:]
    sig = 1.0 / (1.0 + jnp.exp(-gate_pre))
    silu = gate_pre * sig
    act = silu * up_pre
    gate_grad = jnp.sum(act * act_grad, axis=1, keepdims=True)
    act_grad = act_grad * gate
    act_out[0] = (act * gate).astype(BF16)
    slope = sig * (1.0 + gate_pre * (1.0 - sig))
    pre_out[0, :, :ff] = (act_grad * up_pre * slope).astype(BF16)
    pre_out[0, :, ff:] = (act_grad * silu).astype(BF16)
    high = gate_grad.astype(BF16).astype(F32)
    low = gate_grad - high
    extra = jnp.where(lanes == own, high, jnp.where(lanes == own + experts, low, 0.0))
    extra_out[0] = extra.astype(BF16)


def expert_rows(first, rows, spots, marks, cot_rows, router, weights, cap):
    experts, blocks, block = spots.shape
    shards, _, depth, all_ff = weights.shape
    both = all_ff // 3 * 2
    width = rows.shape[1]
    count = blocks * cap
    one = lambda *shape: pl.BlockSpec((1,) + shape, lambda e, first: (e,) + (0,) * len(shape))
    whole = lambda a: pl.BlockSpec(a.shape, lambda e, first: (0, 0))
    return pl.pallas_call(
        functools.partial(expert_kernel, cap),
        grid_spec=pltpu.PrefetchScalarGridSpec(
            num_scalar_prefetch=1,
            grid=(experts,),
            in_specs=[
                whole(rows),
                one(blocks, block),
                whole(marks),
                one(count, width),
                whole(router),
                pl.BlockSpec((shards, 1, depth, all_ff), lambda e, first: (0, e, 0, 0)),
            ],
            out_specs=[
                one(count, width),
                one(count, both // 2),
                one(count, both),
                one(count, EXTRA),
            ],
        ),
        out_shape=[
            jax.ShapeDtypeStruct((experts, count, width), BF16),
            jax.ShapeDtypeStruct((experts, count, both // 2), BF16),
            jax.ShapeDtypeStruct((experts, count, both), BF16),
            jax.ShapeDtypeStruct((experts, count, EXTRA), BF16),
        ],
        compiler_params=pltpu.CompilerParams(vmem_limit_bytes=VMEM),
        cost_estimate=cost(11),
        name="expert_rows",
    )(first, rows, spots, marks, cot_rows, router, weights)


def rows_back_kernel(cap, shards, left_ref, spot_ref, *refs):
    out_ref, acc = refs[-2:]
    e = pl.program_id(0)
    blocks, block, wide = out_ref.shape
    depth = refs[0].shape[2]

    @pl.when(e == 0)
    def _():
        acc[...] = jnp.zeros_like(acc)

    lane = lax.broadcasted_iota(jnp.int32, spot_ref.shape, 1)
    spot = jnp.sum(jnp.where(lane == e, spot_ref[...], 0), axis=1, keepdims=True)
    puts = [put_rows(spot[b * block : (b + 1) * block], cap) for b in range(blocks)]
    for r in range(shards):
        rows = dot_nt(left_ref[0], refs[r][0, 0]).astype(BF16)
        for b in range(blocks):
            acc[b * block : (b + 1) * block, r * depth : (r + 1) * depth] += dot_nn(
                puts[b], rows[b * cap : (b + 1) * cap, :]
            )
    if len(refs) > shards + 2:
        for b in range(blocks):
            acc[b * block : (b + 1) * block, wide - EXTRA :] += dot_nn(
                puts[b], refs[shards][0, b * cap : (b + 1) * cap, :]
            )

    @pl.when(e == pl.num_programs(0) - 1)
    def _():
        out_ref[...] = acc[...].astype(BF16).reshape(out_ref.shape)


def rows_back(left, weights, at, spot_cols, cap, extra=None):
    experts, count, size = left.shape
    shards, _, depth, _ = weights.shape
    blocks = count // cap
    block = spot_cols.shape[0] // blocks
    width = depth * shards + (0 if extra is None else EXTRA)
    shape = (blocks, block, width)
    one = lambda *shape: pl.BlockSpec((1,) + shape, lambda e: (e,) + (0,) * len(shape))
    shard = lambda r: pl.BlockSpec((1, 1, depth, size), lambda e: (r, e, 0, at))
    extras = [] if extra is None else [extra]
    return pl.pallas_call(
        functools.partial(rows_back_kernel, cap, shards),
        grid=(experts,),
        in_specs=[one(count, size), pl.BlockSpec(spot_cols.shape, lambda e: (0, 0))]
        + [shard(r) for r in range(shards)]
        + [one(count, EXTRA)] * len(extras),
        out_specs=pl.BlockSpec(shape, lambda e: (0, 0, 0)),
        out_shape=jax.ShapeDtypeStruct(shape, BF16),
        scratch_shapes=[pltpu.VMEM((blocks * block, width), F32)],
        compiler_params=pltpu.CompilerParams(vmem_limit_bytes=VMEM),
        cost_estimate=cost(5 if extra is None else 10),
        name="mixtures" if extra is None else "row_grads",
    )(left, spot_cols, *[weights] * shards, *extras)


def expert_grad_kernel(row_a, row_b, cot_a, cot_b, pre_a, pre_b, act_a, act_b, out_ref):
    both = pre_a.shape[2]
    total = dot_tn(row_a[0], pre_a[0]) + dot_tn(row_b[0], pre_b[0])
    out_ref[0, 0, :, :both] = total.astype(BF16)
    total = dot_tn(cot_a[0], act_a[0]) + dot_tn(cot_b[0], act_b[0])
    out_ref[0, 0, :, both:] = total.astype(BF16)


def expert_grads(rows, cots, pres, acts, shards):
    experts, count, width = rows[0].shape
    both, ff = pres[0].shape[2], acts[0].shape[2]
    depth = width // shards
    part = pl.BlockSpec((1, count, depth), lambda e, n: (e, 0, n))
    full = lambda size: pl.BlockSpec((1, count, size), lambda e, n: (e, 0, 0))
    return pl.pallas_call(
        expert_grad_kernel,
        grid=(experts, shards),
        in_specs=[part] * 4 + [full(both)] * 2 + [full(ff)] * 2,
        out_specs=pl.BlockSpec((1, 1, depth, both + ff), lambda e, n: (n, e, 0, 0)),
        out_shape=jax.ShapeDtypeStruct((shards, experts, depth, both + ff), BF16),
        compiler_params=pltpu.CompilerParams(vmem_limit_bytes=VMEM),
        cost_estimate=cost(18),
        name="expert_grads",
    )(rows[0], rows[1], cots[0], cots[1], pres[0], pres[1], acts[0], acts[1])


def body(
    layer_input,
    w_query,
    w_key,
    w_value,
    w_out,
    attn_gain,
    query_gain,
    key_gain,
    ffn_gain,
    w_router,
    w_gate,
    w_up,
    w_down,
    routes,
    pic_starts,
    cotangent,
):
    tok_count, model_width = layer_input.shape
    top_count = routes.shape[1]
    ga_count = lax.axis_size("ga")
    z_count = lax.axis_size("z")
    ea_count = 2 * z_count
    core = lax.axis_index("core")
    chip = lax.axis_index("z")
    local_experts, _, ff = w_gate.shape
    expert_total = local_experts * ea_count
    cap = max(2, 9 * tok_count * top_count // (8 * expert_total))
    group_size = HEADS // KV
    kv_width = KV * HD
    q_width = HEADS * HD

    small = [attn_gain, query_gain, key_gain, ffn_gain, w_router.reshape(-1)]
    small_all = ga_gather_small(jnp.concatenate(small))
    at, smalls = 0, []
    for piece in small:
        smalls.append(small_all[:, at : at + piece.shape[0]].reshape(-1))
        at += piece.shape[0]
    attn_gain_f, query_gain_f, key_gain_f, ffn_gain_f = [s.astype(F32) for s in smalls[:4]]
    router_full = smalls[4].reshape(model_width, expert_total)
    router_wide = jnp.pad(router_full, ((0, 0), (0, EXTRA - expert_total)))

    qkv_weights = (w_query, w_key, w_value)
    qkv_own = jnp.concatenate([core_halves(w)[0] for w in qkv_weights], axis=1)

    marks = jnp.sum(
        (routes[:, :, None] == jnp.arange(EXTRA, dtype=jnp.int32)[None, None, :]).astype(F32), axis=1
    )
    cot_steps = []
    qkv_first = ga_first_hop(after(qkv_own, small_all))
    cot_mine = line_gather(
        after(jnp.concatenate([cotangent, marks.astype(BF16)], axis=1), small_all), steps=cot_steps
    )
    qkv_twin = jnp.concatenate(
        [core_halves(after(w, *cot_steps[0]))[1] for w in qkv_weights], axis=1
    )
    qkv_second = ga_second_hop(qkv_first, 0, 1, cot_steps[1])
    qkv_mine = qkv_first + qkv_second
    qkv_swapped = swap_pieces(qkv_mine[1:] if ga_count == 4 else qkv_mine)
    qkv_other = ([qkv_twin] if ga_count == 4 else []) + qkv_swapped
    cot_mine = after(jnp.concatenate(cot_mine), *qkv_second)
    cot_sides = [cot_mine, swap_core(cot_mine)]
    first_expert = (chip * 2 + core) * local_experts
    mark_sides, spot_rows, spot_cols, cot_rows = [], [], [], []
    before = jnp.tril(jnp.ones((tok_count, tok_count), BF16))
    for side in cot_sides:
        side_marks = side[:, model_width:]
        chosen = lax.dynamic_slice_in_dim(side_marks, first_expert, local_experts, 1)
        chosen = chosen.reshape(z_count, tok_count, local_experts)
        rank = jnp.einsum("ts,bse->bte", before, chosen, preferred_element_type=F32)
        spots = jnp.where(chosen > 0, rank - 1.0, -1.0).astype(jnp.int32)
        mark_sides.append(side_marks)
        spot_rows.append(jnp.transpose(spots, (2, 0, 1)))
        spot_cols.append(spots.reshape(z_count * tok_count, local_experts))
        cot_rows.append(pick(side, spot_rows[-1], cap, model_width))

    ea_index = chip * 2 + core
    positions = ea_index * tok_count + jnp.arange(tok_count, dtype=jnp.int32)
    holder = ((chip - jnp.arange(z_count)) % z_count * 2)[None, :] + jnp.stack([core, 1 - core])[
        :, None
    ]
    key_pos = (holder.reshape(-1, 1) * tok_count + jnp.arange(tok_count)[None, :]).reshape(-1)
    key_pos = key_pos.astype(jnp.int32)
    allowed = allowed_mask(pic_starts[0], positions, key_pos)
    bias = jnp.where(allowed, 0.0, MASKED_SCORE).astype(F32)
    bias_turned = jnp.where(jnp.transpose(allowed), 0.0, MASKED_SCORE).astype(F32)
    frequency = ROPE_THETA ** (-jnp.arange(HD // 2, dtype=F32) * 2.0 / HD)
    angles = positions.astype(F32)[:, None] * frequency[None, :]
    cosine = jnp.concatenate([jnp.cos(angles), jnp.cos(angles)], axis=1)
    sine = jnp.concatenate([-jnp.sin(angles), jnp.sin(angles)], axis=1)
    per_key = max(1, ga_count // KV)
    ga_index = lax.axis_index("ga")
    run = group_size // 2 // per_key
    step = jnp.arange(per_key) ^ (ga_index % per_key)
    own_heads = (step[:, None] * 2 * run + jnp.arange(run)[None, :]).reshape(-1)
    key_place = jnp.arange(KV) ^ (ga_index // per_key)
    place = jnp.concatenate(
        [key_place, own_heads + core * run, own_heads + (1 - core) * run]
    ).astype(jnp.int32)

    input_f = layer_input.astype(F32)
    normed = rms_norm(input_f, attn_gain_f).astype(BF16)
    normed_mine = split_cols(normed, core)
    normed_other = split_cols(normed, 1 - core)
    normed_used = after(normed_mine, bias, bias_turned, cosine, sine)
    qkv = pieces_matmul((normed_used, normed_other), (qkv_mine, qkv_other))
    query_gain_row, key_gain_row = query_gain_f.reshape(1, HD), key_gain_f.reshape(1, HD)
    kv_own = prep_kv(qkv, cosine, sine, key_gain_row)

    out_own, out_twin = core_halves(w_out)
    out_first = ga_first_hop(after(out_own, *qkv_second))
    kv_steps = []
    kv_mine, kv_other = ea_gather(
        kv_own, {2: cot_rows[:1], 3: cot_rows[1:] + out_first[1:]}, kv_steps
    )
    out_second = ga_second_hop(out_first, 0, 1, ())
    out_mine = out_first + out_second
    expert_own = jnp.concatenate([w_gate, w_up, jnp.swapaxes(w_down, 1, 2)], axis=2)
    expert_all = lax.all_gather(after(expert_own, *out_first[1:], *kv_steps[1]), "ga", axis=0)

    att_mine, att_other, log_rows = attend(
        place,
        qkv,
        kv_mine,
        kv_other,
        bias,
        cosine,
        sine,
        query_gain_row,
    )
    out_swapped = swap_pieces(out_first[1:] if ga_count == 4 else out_first)
    out_swapped += swap_pieces([after(piece, att_mine) for piece in out_second])
    out_other = ([out_twin] if ga_count == 4 else []) + out_swapped
    hidden = input_f + pieces_matmul((att_mine, att_other), (out_mine, out_other))
    ffn_in = rms_norm(hidden, ffn_gain_f).astype(BF16)

    row_mine = after(jnp.concatenate(line_gather(ffn_in)), expert_all)
    row_sides = [row_mine, swap_core(row_mine)]
    logits = dot_nn(ffn_in, router_full)
    own_marks = marks[:, :expert_total] > 0
    peak = jnp.max(jnp.where(own_marks, logits, MASKED_SCORE), axis=1, keepdims=True)
    weights = jnp.exp(jnp.where(own_marks, logits - peak, MASKED_SCORE))
    gates = weights / jnp.sum(weights, axis=1, keepdims=True)

    first = jnp.stack([first_expert, expert_total]).astype(jnp.int32)
    picked, acts, pres, extras = [], [], [], []
    for side in range(2):
        rows, act, pre, extra = expert_rows(
            first,
            row_sides[side],
            spot_rows[side],
            mark_sides[side],
            cot_rows[side],
            router_wide,
            expert_all,
            cap,
        )
        picked.append(rows)
        acts.append(act)
        pres.append(pre)
        extras.append(extra)
    expert_grad = expert_grads(picked, cot_rows, pres, acts, ga_count)
    expert_sum = lax.psum_scatter(expert_grad, "ga", scatter_dimension=0)
    row_other = rows_back(
        after(pres[1], expert_grad), expert_all, 0, spot_cols[1], cap, extras[1]
    )
    row_mine = rows_back(
        after(pres[0], row_other), expert_all, 0, spot_cols[0], cap, extras[0]
    )
    rows = LineSum(core_slots(row_mine, row_other))
    held = rows.step()
    mix_other = rows_back(after(acts[1], rows.slots[1]), expert_all, 2, spot_cols[1], cap)
    rows.step(mix_other)
    mix_mine = rows_back(after(acts[0], *held), expert_all, 2, spot_cols[0], cap)
    mix = LineSum(core_slots(mix_mine, mix_other))
    rows.step(mix_mine)
    row_sum = after(rows.result(), *mix.slots)

    grad_out = cotangent.astype(F32)
    gate_grad = (
        row_sum[:, model_width : model_width + expert_total].astype(F32)
        + row_sum[:, model_width + expert_total : model_width + 2 * expert_total].astype(F32)
    )
    inner = jnp.sum(gates * gate_grad, axis=1, keepdims=True)
    logit_grad = gates * (gate_grad - inner)
    router_grad = lax.dot_general(
        ffn_in.astype(F32), logit_grad, (((0,), (0,)), ((), ())), precision=PRECISE
    )
    ffn_in_grad = row_sum[:, :model_width].astype(F32) + jnp.dot(
        logit_grad, router_full.astype(F32).T, precision=PRECISE
    )
    unused, ffn_back = jax.vjp(rms_norm, hidden, ffn_gain_f)
    hidden_part, ffn_gain_grad = ffn_back(ffn_in_grad)
    hidden_grad = grad_out + hidden_part
    branch_grad = hidden_grad.astype(BF16)
    out_terms = [dot_tn(device_cols(a), branch_grad) for a in (att_mine, att_other)]
    out_terms[1] = out_terms[1].astype(BF16)
    att_grads = pieces_back(after(branch_grad, out_terms[1]), out_mine + out_other, BF16)
    raw_grads, kv_grads, gain_grads = [], [], []

    def back(head, *before):
        raw_grad, kv_grad, gain_grad = attend_back(
            head,
            1,
            place,
            qkv,
            kv_mine,
            kv_other,
            bias_turned,
            cosine,
            sine,
            query_gain_row,
            after(att_grads, *before),
            (att_mine, att_other),
            log_rows,
        )
        raw_grads.append(raw_grad)
        kv_grads.append(kv_grad)
        gain_grads.append(gain_grad[0])

    def weight_terms(grad):
        return dot_tn(normed_mine, grad), dot_tn(normed_other, grad).astype(BF16)

    held = [mix.step(*rows.held)]
    back(0, out_terms[1], expert_sum, *mix.sent)
    held.append(mix.step(raw_grads[0]))
    out_total = core_sum(*out_terms, before=[att_grads])
    out_share = lax.psum_scatter(out_total, "ga", scatter_dimension=0, tiled=True)
    back(1, raw_grads[0], out_total, *held[0])
    held.append(mix.step(raw_grads[1]))
    query_parts = [jnp.concatenate(raw_grads[:2], axis=1)]
    query_terms = [weight_terms(query_parts[0])]
    back(2, raw_grads[1], *held[1])
    query_totals = [core_sum(*query_terms[0])]
    back(3, raw_grads[2], query_terms[0][1], out_share, *held[2])
    query_firsts = [ga_sum_first(query_totals[0])]
    mix_sum = mix.result()
    layer_output = (hidden + mix_sum.astype(F32)).astype(BF16)
    query_parts.append(jnp.concatenate(raw_grads[2:], axis=1))
    query_terms.append(weight_terms(query_parts[1]))
    query_gain_grad = sum(gain_grads)
    kv_grad = after(jnp.concatenate(kv_grads, axis=1), *held[2])
    kv_grad = kv_grad.reshape(2, z_count, tok_count, 2 * kv_width)
    keys_values = LineSum(core_slots(kv_grad[0], kv_grad[1]))
    keys_values.step(query_terms[1][1], *query_firsts[0])
    query_shares = [ga_sum_second(query_firsts[0])]
    query_totals.append(core_sum(*query_terms[1]))
    out_all = z_all_sum(out_share)
    keys_values.step(query_totals[1], out_all)
    query_firsts.append(ga_sum_first(after(query_totals[1], query_shares[0])))
    keys_values.step(query_shares[0])
    kv_raw_grad, key_gain_grad = kv_back(
        qkv, after(keys_values.result(), *query_firsts[1]), cosine, sine, key_gain_row
    )
    key_gain_grad = key_gain_grad[0]
    chunks = query_parts + [kv_raw_grad]
    qkv_grad = jnp.concatenate(chunks, axis=1)
    both_grads = pieces_back(qkv_grad, qkv_mine + qkv_other, F32)
    query_shares.append(ga_sum_second(query_firsts[1], [both_grads]))
    kv_total = core_sum(*weight_terms(kv_raw_grad))
    kv_first = ga_sum_first(after(kv_total, query_shares[1]))
    query_alls = [z_all_sum(after(share, out_all)) for share in query_shares]
    kv_share = ga_sum_second(kv_first)
    kv_sum = whole_shard([z_all_sum_small(after(kv_share, *query_alls))])
    out_sum = whole_shard([out_all])
    query_sum = whole_shard(query_alls)
    key_sum, value_sum = kv_sum[:, :kv_width], kv_sum[:, kv_width:]
    both_grads = after(both_grads, query_shares[1])
    half_width = model_width // 2
    normed_grad = join_cols(both_grads[:, :half_width], both_grads[:, half_width:])
    unused, attn_back = jax.vjp(rms_norm, input_f, attn_gain_f)
    input_part, attn_gain_grad = attn_back(normed_grad)
    input_grad = (hidden_grad + input_part).astype(BF16)

    tiny = [attn_gain_grad, query_gain_grad, key_gain_grad, ffn_gain_grad, router_grad.reshape(-1)]
    tiny_rows = jnp.concatenate([t.reshape(ga_count, -1) for t in tiny], axis=1)
    tiny_own = sum_small(after(tiny_rows, *query_alls))
    at, tiny_sums = 0, []
    for piece in tiny:
        width = piece.shape[0] // ga_count
        tiny_sums.append(tiny_own[at : at + width])
        at += width
    attn_sum, qgain_sum, kgain_sum, ffn_sum, router_sum = tiny_sums
    return (
        layer_output,
        input_grad,
        query_sum,
        key_sum,
        value_sum,
        out_sum,
        attn_sum,
        qgain_sum,
        kgain_sum,
        ffn_sum,
        router_sum.reshape(-1, expert_total),
        expert_sum[:, :, :ff].astype(F32),
        expert_sum[:, :, ff : 2 * ff].astype(F32),
        jnp.swapaxes(expert_sum[:, :, 2 * ff :], 1, 2).astype(F32),
    )


def solution(mesh):
    ga_count, ea_count = mesh.shape["ga"], mesh.shape["ea"]
    inner = Mesh(mesh.devices.reshape(ga_count, ea_count // 2, 2), ("ga", "z", "core"))
    everyone = ("ga", "z", "core")
    owners = ("z", "core")
    in_specs = (
        P(everyone, None),
        P("ga", None),
        P("ga", None),
        P("ga", None),
        P("ga", None),
        P("ga"),
        P("ga"),
        P("ga"),
        P("ga"),
        P("ga", None),
        P(owners, "ga", None),
        P(owners, "ga", None),
        P(owners, None, "ga"),
        P(everyone, None),
        P("ga", None),
        P(everyone, None),
    )
    out_specs = (
        P(everyone, None),
        P(everyone, None),
        P("ga", None),
        P("ga", None),
        P("ga", None),
        P("ga", None),
        P("ga"),
        P("ga"),
        P("ga"),
        P("ga"),
        P("ga", None),
        P(owners, "ga", None),
        P(owners, "ga", None),
        P(owners, None, "ga"),
    )
    return jax.shard_map(body, mesh=inner, in_specs=in_specs, out_specs=out_specs, check_vma=False)
```

```python
import functools

import jax
import jax.numpy as jnp
from jax import lax
from jax.experimental import pallas as pl
from jax.experimental.pallas import tpu as pltpu
from jax.sharding import Mesh
from jax.sharding import PartitionSpec as P

HEADS = 32
KV = 4
HD = 128
PIC = 256


NORM_EPS = 1e-06
ROPE_THETA = 1000000.0
MASKED_SCORE = -1e30
PRECISE = lax.Precision.HIGHEST
F32 = jnp.float32
BF16 = jnp.bfloat16
EXTRA = 128
LOG2E = 1.4426950408889634
VMEM = 56 << 20


def rms_norm(values, norm_gain):
    inverse = lax.rsqrt(jnp.mean(values * values, axis=-1, keepdims=True) + NORM_EPS)
    return values * inverse * norm_gain


def piece_ids(starts, positions):
    inside = (
        (starts[:, None] >= 0)
        & (positions[None, :] >= starts[:, None])
        & (positions[None, :] < starts[:, None] + PIC)
    )
    labels = jnp.arange(1, starts.shape[0] + 1, dtype=jnp.int32)[:, None]
    return jnp.sum(jnp.where(inside, labels, 0), axis=0)


def allowed_mask(starts, query_pos, key_pos):
    query_piece = piece_ids(starts, query_pos)
    key_piece = piece_ids(starts, key_pos)
    causal = key_pos[None, :] <= query_pos[:, None]
    shared = (query_piece[:, None] == key_piece[None, :]) & (query_piece[:, None] > 0)
    return causal | shared


def dot_nn(left, right):
    return lax.dot_general(left, right, (((1,), (0,)), ((), ())), preferred_element_type=F32)


def dot_tn(left, right):
    return lax.dot_general(left, right, (((0,), (0,)), ((), ())), preferred_element_type=F32)


def dot_nt(left, right):
    return lax.dot_general(left, right, (((1,), (1,)), ((), ())), preferred_element_type=F32)


def after(value, *others):
    return lax.optimization_barrier((value,) + others)[0]


def swap_core(value):
    return lax.ppermute(value, "core", [(0, 1), (1, 0)])


def swap_axis(value, axis, bit):
    return lax.ppermute(value, axis, [(i, i ^ bit) for i in range(lax.axis_size(axis))])


def plus(*terms):
    total = terms[0].astype(F32)
    for term in terms[1:]:
        total = total + term.astype(F32)
    return total.astype(BF16)


def line_gather(value, before=None, steps=None):
    count = lax.axis_size("z")
    place = lax.axis_index("z")
    below, above = {}, {}
    up = down = value
    for step in range(1, count):
        if before and step in before:
            up, down = lax.optimization_barrier((up, down) + tuple(before[step]))[:2]
        up = lax.ppermute(up, "z", [(p, p + 1) for p in range(step - 1, count - 1)])
        down = lax.ppermute(down, "z", [(p, p - 1) for p in range(1, count - step + 1)])
        up, down = lax.optimization_barrier((up, down))
        below[step], above[step] = up, down
        if steps is not None:
            steps.append((up, down))
    return [value] + [
        jnp.where(place >= step, below[step], above[count - step]) for step in range(1, count)
    ]


class LineSum:
    def __init__(self, slots):
        self.slots, self.done = slots, 0

    def step(self, *before):
        count = lax.axis_size("z")
        self.done += 1
        up, down = self.slots[self.done], self.slots[count - self.done]
        if before:
            up, down = lax.optimization_barrier((up, down) + before)[:2]
        if self.done > 1:
            up, down = plus(up, self.held[0]), plus(down, self.held[1])
        self.sent = (up, down)
        up = lax.ppermute(up, "z", [(p, p + 1) for p in range(self.done)])
        down = lax.ppermute(
            down, "z", [(p, p - 1) for p in range(count - 1, count - 1 - self.done, -1)]
        )
        self.held = lax.optimization_barrier((up, down))
        return self.held

    def result(self):
        while self.done < lax.axis_size("z") - 1:
            self.step()
        return plus(self.slots[0], *self.held)


def ea_gather(value, before=None, steps=None):
    mine = jnp.concatenate(line_gather(value, before, steps))
    return mine, swap_core(mine)


def core_slots(mine, other):
    got = swap_core(other)
    return [plus(mine[s], got[s]) for s in range(lax.axis_size("z"))]


def z_all_sum(value):
    return lax.psum(value, "z")


def z_all_sum_small(value):
    count = lax.axis_size("z")
    place = lax.axis_index("z")
    bits, bit = [], 1
    while bit < count:
        rows = value.shape[0] // 2
        upper = (place // bit) % 2
        keep = lax.dynamic_slice_in_dim(value, upper * rows, rows, 0)
        send = lax.dynamic_slice_in_dim(value, (1 - upper) * rows, rows, 0)
        value = plus(keep, swap_axis(send, "z", bit))
        bits.append(bit)
        bit *= 2
    for bit in reversed(bits):
        got = swap_axis(value, "z", bit)
        upper = (place // bit) % 2
        low, high = jnp.where(upper == 0, value, got), jnp.where(upper == 0, got, value)
        value = jnp.concatenate([low, high])
    return value


def ga_order():
    return lax.axis_index("ga") ^ jnp.arange(lax.axis_size("ga"))


def ga_first_hop(value):
    if lax.axis_size("ga") != 4:
        whole = lax.all_gather(value, "ga", axis=0)
        return [jnp.take(whole, ga_order(), axis=0).reshape((-1,) + value.shape[1:])]
    return [value, swap_axis(value, "ga", 1), swap_axis(value, "ga", 2)]


def ga_second_hop(first, part, parts, before):
    if len(first) == 1:
        return []
    half = first[0].shape[0] // 2
    rows = half // parts
    to_y = first[1][part * rows : (part + 1) * rows]
    to_x = first[2][half + part * rows : half + (part + 1) * rows]
    to_y, to_x = lax.optimization_barrier((to_y, to_x) + tuple(before))[:2]
    return [swap_axis(to_y, "ga", 2), swap_axis(to_x, "ga", 1)]


def ga_sum_first(value):
    if lax.axis_size("ga") != 4:
        return (value,)
    rows = value.shape[0] // 4
    half = rows // 2
    own, for_x, for_y = [value[r * rows : (r + 1) * rows] for r in range(3)]
    low = swap_axis(value[3 * rows : 3 * rows + half], "ga", 1)
    high = swap_axis(value[3 * rows + half :], "ga", 2)
    to_x = jnp.concatenate([for_x[:half], plus(for_x[half:], high)])
    to_y = jnp.concatenate([plus(for_y[:half], low), for_y[half:]])
    return own, to_x, to_y


def ga_sum_second(parts, before=()):
    if len(parts) == 1:
        return ga_sum_whole(parts[0])
    own, to_x, to_y = parts
    terms = (own, swap_axis(to_x, "ga", 1), swap_axis(to_y, "ga", 2))
    return plus(*lax.optimization_barrier(terms + tuple(before))[:3])


def ga_sum_whole(value):
    blocks = value.reshape((lax.axis_size("ga"), -1) + value.shape[1:])
    blocks = jnp.take(blocks, ga_order(), axis=0).reshape(value.shape)
    return lax.psum_scatter(blocks, "ga", scatter_dimension=0, tiled=True)


def ga_gather_small(value):
    count = lax.axis_size("ga")
    held, bit = value[None], 1
    while bit < count:
        held = jnp.concatenate([held, swap_axis(held, "ga", bit)])
        bit *= 2
    return jnp.take(held, ga_order(), axis=0)


def sum_small(rows):
    total = rows + swap_core(rows)
    count, bit = lax.axis_size("z"), 1
    while bit < count:
        total = total + swap_axis(total, "z", bit)
        bit *= 2
    count = lax.axis_size("ga")
    total = jnp.take(total, ga_order(), axis=0)
    while count > 1:
        count //= 2
        total = total[:count] + swap_axis(total[count:], "ga", count)
    return total[0]


def core_halves(value):
    core = lax.axis_index("core")
    rows = value.shape[0] // 2
    return (
        lax.dynamic_slice_in_dim(value, core * rows, rows, 0),
        lax.dynamic_slice_in_dim(value, (1 - core) * rows, rows, 0),
    )


def swap_pieces(pieces):
    return [swap_core(piece) for piece in pieces]


def split_cols(value, half):
    groups = lax.axis_size("ga")
    width = value.shape[1] // groups // 2
    order = ga_order()
    return jnp.concatenate(
        [
            lax.dynamic_slice_in_dim(value, (order[r] * 2 + half) * width, width, 1)
            for r in range(groups)
        ],
        axis=1,
    )


def device_cols(value):
    groups = lax.axis_size("ga")
    width = value.shape[1] // groups
    order = ga_order()
    return jnp.concatenate(
        [lax.dynamic_slice_in_dim(value, order[g] * width, width, 1) for g in range(groups)], axis=1
    )


def join_cols(mine, other):
    groups = lax.axis_size("ga")
    core = lax.axis_index("core")
    width = mine.shape[1] // groups
    order = ga_order()
    parts = []
    for g in range(groups):
        a = lax.dynamic_slice_in_dim(mine, order[g] * width, width, 1)
        b = lax.dynamic_slice_in_dim(other, order[g] * width, width, 1)
        parts += [jnp.where(core == 0, a, b), jnp.where(core == 0, b, a)]
    return jnp.concatenate(parts, axis=1)


def core_sum(mine, other, before=()):
    got = swap_core(other)
    return plus(mine, after(got, *before) if before else got)


def whole_shard(shares):
    core = lax.axis_index("core")
    rows = shares[0].shape[0]
    out = jnp.zeros((2 * rows, sum(share.shape[1] for share in shares)), F32)
    at = 0
    for share in shares:
        for half, part in ((core, share), (1 - core, swap_core(share))):
            out = lax.dynamic_update_slice(out, part.astype(F32), (half * rows, at))
        at += share.shape[1]
    return out


def cost(micros):
    return pl.CostEstimate(flops=micros * 10**9, bytes_accessed=1024, transcendentals=0)


def pieces_kernel(plan, *refs):
    acc = None
    lefts, out_ref = refs[: 1 + max(which for which, _, _ in plan)], refs[-1]
    for (which, at, size), ref in zip(plan, refs[len(lefts) : -1]):
        term = dot_nn(lefts[which][:, at : at + size], ref[...])
        acc = term if acc is None else acc + term
    out_ref[...] = acc


def pieces_matmul(lefts, piece_lists):
    plan, pieces = [], []
    for which, some in enumerate(piece_lists):
        at = 0
        for piece in some:
            plan.append((which, at, piece.shape[0]))
            pieces.append(piece)
            at += piece.shape[0]
    rows, width = lefts[0].shape[0], pieces[0].shape[1]
    tile = min(1024 if width > 4096 else 512, width)
    return pl.pallas_call(
        functools.partial(pieces_kernel, plan),
        grid=(width // tile,),
        in_specs=[pl.BlockSpec(left.shape, lambda n: (0, 0)) for left in lefts]
        + [pl.BlockSpec((piece.shape[0], tile), lambda n: (0, n)) for piece in pieces],
        out_specs=pl.BlockSpec((rows, tile), lambda n: (0, n)),
        out_shape=jax.ShapeDtypeStruct((rows, width), F32),
        compiler_params=pltpu.CompilerParams(vmem_limit_bytes=VMEM),
        cost_estimate=cost(6),
        name="dense_matmul",
    )(*lefts, *pieces)


def pieces_back_kernel(sizes, left_ref, *refs):
    n = pl.program_id(0)
    out_ref, acc = refs[-2:]

    @pl.when(n == 0)
    def _():
        acc[...] = jnp.zeros_like(acc)

    at = 0
    for ref, size in zip(refs[:-2], sizes):
        acc[:, at : at + size] += dot_nt(left_ref[...], ref[...])
        at += size

    @pl.when(n == pl.num_programs(0) - 1)
    def _():
        out_ref[...] = acc[...].astype(out_ref.dtype)


def pieces_back(left, pieces, dtype):
    rows, width = left.shape
    tile = min(512, width)
    sizes = [piece.shape[0] for piece in pieces]
    return pl.pallas_call(
        functools.partial(pieces_back_kernel, sizes),
        grid=(width // tile,),
        in_specs=[pl.BlockSpec((rows, tile), lambda n: (0, n))]
        + [pl.BlockSpec((size, tile), lambda n: (0, n)) for size in sizes],
        out_specs=pl.BlockSpec((rows, sum(sizes)), lambda n: (0, 0)),
        out_shape=jax.ShapeDtypeStruct((rows, sum(sizes)), dtype),
        scratch_shapes=[pltpu.VMEM((rows, sum(sizes)), F32)],
        compiler_params=pltpu.CompilerParams(vmem_limit_bytes=VMEM),
        cost_estimate=cost(6),
        name="dense_back",
    )(left, *pieces)


def prep_head(raw, gain, cosine, sine):
    inverse = lax.rsqrt(jnp.mean(raw * raw, axis=-1, keepdims=True) + NORM_EPS)
    scaled = raw * inverse * gain
    turned = scaled * cosine + pltpu.roll(scaled, HD // 2, 1) * sine
    return turned.astype(BF16), inverse


def head_cols(index):
    return pl.ds(pl.multiple_of(index * HD, HD), HD)


def prep_kv_kernel(raw_ref, cos_ref, sin_ref, gain_ref, out_ref):
    for h in range(KV):
        span = slice(h * HD, (h + 1) * HD)
        keys, _ = prep_head(raw_ref[:, span], gain_ref[...], cos_ref[...], sin_ref[...])
        out_ref[:, span] = keys
    out_ref[:, KV * HD :] = raw_ref[:, KV * HD :].astype(BF16)


def prep_kv(raw, cosine, sine, gain):
    rows, width = raw.shape[0], 2 * KV * HD
    whole = lambda a: pl.BlockSpec(a.shape, lambda i: (0, 0))
    return pl.pallas_call(
        prep_kv_kernel,
        grid=(1,),
        in_specs=[
            pl.BlockSpec((rows, width), lambda i: (0, raw.shape[1] // width - 1)),
            whole(cosine),
            whole(sine),
            whole(gain),
        ],
        out_specs=pl.BlockSpec((rows, width), lambda i: (0, 0)),
        out_shape=jax.ShapeDtypeStruct((rows, width), BF16),
        compiler_params=pltpu.CompilerParams(vmem_limit_bytes=VMEM),
        cost_estimate=cost(1),
        name="prep_kv",
    )(raw, cosine, sine, gain)


def head_back(raw, inverse, grad, gain, cosine, sine):
    scaled_grad = grad * cosine + pltpu.roll(grad * sine, HD // 2, 1)
    unit = raw * inverse
    gain_grad = jnp.sum(scaled_grad * unit, axis=0, keepdims=True)
    unit_grad = scaled_grad * gain
    mean = jnp.mean(unit_grad * unit, axis=-1, keepdims=True)
    return inverse * (unit_grad - unit * mean), gain_grad


def kv_back_kernel(raw_ref, grad_ref, cos_ref, sin_ref, gain_ref, out_ref, gain_grad_ref):
    total = jnp.zeros((1, HD), F32)
    for h in range(KV):
        span = slice(h * HD, (h + 1) * HD)
        raw = raw_ref[:, span]
        cosine, sine, gain = cos_ref[...], sin_ref[...], gain_ref[...]
        _, inverse = prep_head(raw, gain, cosine, sine)
        grad = grad_ref[:, 2 * h * HD : (2 * h + 1) * HD].astype(F32)
        raw_grad, gain_grad = head_back(raw, inverse, grad, gain, cosine, sine)
        out_ref[:, span] = raw_grad.astype(BF16)
        out_ref[:, (KV + h) * HD : (KV + h + 1) * HD] = grad_ref[
            :, (2 * h + 1) * HD : (2 * h + 2) * HD
        ]
        total = total + gain_grad
    gain_grad_ref[...] = jnp.broadcast_to(total, gain_grad_ref.shape)


def kv_back(raw, grad, cosine, sine, gain):
    rows, width = raw.shape[0], 2 * KV * HD
    whole = lambda a: pl.BlockSpec(a.shape, lambda i: (0, 0))
    return pl.pallas_call(
        kv_back_kernel,
        grid=(1,),
        in_specs=[
            pl.BlockSpec((rows, width), lambda i: (0, raw.shape[1] // width - 1)),
            whole(grad),
            whole(cosine),
            whole(sine),
            whole(gain),
        ],
        out_specs=[
            pl.BlockSpec((rows, width), lambda i: (0, 0)),
            pl.BlockSpec((8, HD), lambda i: (0, 0)),
        ],
        out_shape=[
            jax.ShapeDtypeStruct((rows, width), BF16),
            jax.ShapeDtypeStruct((8, HD), F32),
        ],
        compiler_params=pltpu.CompilerParams(vmem_limit_bytes=VMEM),
        cost_estimate=cost(1),
        name="kv_back",
    )(raw, grad, cosine, sine, gain)


def attend_kernel(
    place,
    raw_ref,
    key_a,
    key_b,
    value_a,
    value_b,
    bias_ref,
    cos_ref,
    sin_ref,
    gain_ref,
    mine_ref,
    other_ref,
    log_ref,
):
    half = key_a.shape[0]
    chunk = min(512, half)
    to_log2 = LOG2E * HD**-0.5
    count = raw_ref.shape[1] // HD

    def one_head(at_head, out_ref, column):
        head = place[KV + at_head]
        query, _ = prep_head(
            raw_ref[:, head_cols(head)], gain_ref[...], cos_ref[...], sin_ref[...]
        )
        total = jnp.zeros((query.shape[0], 1), F32)
        acc = jnp.zeros(query.shape, F32)
        for side, (key_ref, value_ref) in enumerate(((key_a, value_a), (key_b, value_b))):
            for at in range(0, half, chunk):
                scores = dot_nt(query, key_ref[at : at + chunk, :])
                first = side * half + at
                weights = jnp.exp2(scores * to_log2 + bias_ref[:, first : first + chunk])
                total = total + jnp.sum(weights, axis=1, keepdims=True)
                acc = acc + dot_nn(weights.astype(BF16), value_ref[at : at + chunk, :])
        out_ref[:, head_cols(column)] = (acc / total).astype(BF16)
        logs = jnp.transpose(jnp.broadcast_to(jnp.log2(total), query.shape))
        log_ref[0, pl.ds(at_head, 1), :] = logs[0:1, :]

    @pl.loop(0, count // 2)
    def _(i):
        one_head(i, mine_ref, i)
        one_head(count // 2 + i, other_ref, i)


def attend_specs(rows, group, half, tables):
    whole = lambda h, place: (0, 0)
    side = lambda first: pl.BlockSpec((half, HD), lambda h, place: (0, first + h))
    return [
        pl.BlockSpec((rows, group), lambda h, place: (0, h)),
        side(0),
        side(0),
        side(KV),
        side(KV),
    ] + [pl.BlockSpec(t.shape, whole) for t in tables]


def attend(place, raw, kv_mine, kv_other, bias, cosine, sine, gain):
    rows = raw.shape[0]
    group = HEADS * HD // KV
    half = kv_mine.shape[0]
    tables = (bias, cosine, sine, gain)
    half_spec = pl.BlockSpec((rows, group // 2), lambda h, place: (0, place[h]))
    return pl.pallas_call(
        attend_kernel,
        grid_spec=pltpu.PrefetchScalarGridSpec(
            num_scalar_prefetch=1,
            grid=(KV,),
            in_specs=attend_specs(rows, group, half, tables),
            out_specs=[
                half_spec,
                half_spec,
                pl.BlockSpec((1, HEADS // KV, rows), lambda h, place: (h, 0, 0)),
            ],
        ),
        out_shape=[
            jax.ShapeDtypeStruct((rows, HEADS * HD // 2), BF16),
            jax.ShapeDtypeStruct((rows, HEADS * HD // 2), BF16),
            jax.ShapeDtypeStruct((KV, HEADS // KV, rows), F32),
        ],
        compiler_params=pltpu.CompilerParams(vmem_limit_bytes=VMEM),
        cost_estimate=cost(2),
        name="attend",
    )(place, raw, kv_mine, kv_other, kv_mine, kv_other, *tables)


def attend_back_kernel(
    place,
    raw_ref,
    key_a,
    key_b,
    value_a,
    value_b,
    bias_ref,
    cos_ref,
    sin_ref,
    gain_ref,
    grad_mine,
    grad_other,
    out_mine,
    out_other,
    log_ref,
    raw_grad_ref,
    kv_grad_ref,
    gain_grad_ref,
    key_acc,
    value_acc,
):
    h = pl.program_id(0)
    half = key_a.shape[0]
    chunk = min(512, half)
    scale = HD**-0.5
    to_log2 = LOG2E * scale
    count = raw_ref.shape[1] // HD
    key_acc[...] = jnp.zeros_like(key_acc)
    value_acc[...] = jnp.zeros_like(value_acc)

    @pl.when(h == 0)
    def _():
        gain_grad_ref[...] = jnp.zeros_like(gain_grad_ref)

    def one_head(at_head, grad_ref, out_ref, column):
        head = place[KV + at_head]
        raw = raw_ref[:, head_cols(head)]
        cosine, sine, gain = cos_ref[...], sin_ref[...], gain_ref[...]
        query, inverse = prep_head(raw, gain, cosine, sine)
        grad = grad_ref[:, head_cols(column)]
        product = grad.astype(F32) * out_ref[:, head_cols(column)].astype(F32)
        inner = jnp.sum(jnp.transpose(product), axis=0, keepdims=True)
        logs = log_ref[0, pl.ds(at_head, 1), :]
        query_grad = jnp.zeros(query.shape, F32)
        for side, (key_ref, value_ref) in enumerate(((key_a, value_a), (key_b, value_b))):
            for at in range(0, half, chunk):
                keys = key_ref[at : at + chunk, :]
                first = side * half + at
                span = slice(first, first + chunk)
                scores = dot_nt(keys, query)
                probs = jnp.exp2(scores * to_log2 + bias_ref[span, :] - logs)
                prob_grad = dot_nt(value_ref[at : at + chunk, :], grad)
                score_grad = (probs * (prob_grad - inner)).astype(BF16)
                value_acc[span, :] += dot_nn(probs.astype(BF16), grad)
                key_acc[span, :] += dot_nn(score_grad, query)
                query_grad = query_grad + dot_tn(score_grad, keys)
        query_grad = (query_grad * scale).astype(BF16).astype(F32)
        raw_grad, gain_grad = head_back(raw, inverse, query_grad, gain, cosine, sine)
        gain_grad_ref[0:1, :] += gain_grad
        raw_grad_ref[:, head_cols(head)] = raw_grad.astype(BF16)

    @pl.loop(0, count // 2)
    def _(i):
        one_head(i, grad_mine, out_mine, i)
        one_head(count // 2 + i, grad_other, out_other, i)

    heads = kv_grad_ref.shape[1] // HD // 2
    kv_grad_ref[:, head_cols(h)] = (key_acc[...] * scale).astype(BF16)
    kv_grad_ref[:, head_cols(heads + h)] = value_acc[...].astype(BF16)


def attend_back(
    first, count, place, raw, kv_mine, kv_other, bias, cosine, sine, gain, grad, outs, logs
):
    rows = raw.shape[0]
    group = HEADS * HD // KV
    half = kv_mine.shape[0]
    tables = (bias, cosine, sine, gain)
    half_spec = pl.BlockSpec((rows, group // 2), lambda h, place: (0, place[first + h]))
    other_spec = pl.BlockSpec((rows, group // 2), lambda h, place: (0, KV + place[first + h]))
    whole = lambda h, place: (0, 0)
    side = lambda at: pl.BlockSpec((half, HD), lambda h, place: (0, at + first + h))
    return pl.pallas_call(
        attend_back_kernel,
        grid_spec=pltpu.PrefetchScalarGridSpec(
            num_scalar_prefetch=1,
            grid=(count,),
            in_specs=[
                pl.BlockSpec((rows, group), lambda h, place: (0, first + h)),
                side(0),
                side(0),
                side(KV),
                side(KV),
            ]
            + [pl.BlockSpec(t.shape, whole) for t in tables]
            + [half_spec, other_spec, half_spec, half_spec]
            + [pl.BlockSpec((1,) + logs.shape[1:], lambda h, place: (first + h, 0, 0))],
            out_specs=[
                pl.BlockSpec((rows, group), lambda h, place: (0, h)),
                pl.BlockSpec((2 * half, 2 * count * HD), whole),
                pl.BlockSpec((8, HD), whole),
            ],
            scratch_shapes=[pltpu.VMEM((2 * half, HD), F32), pltpu.VMEM((2 * half, HD), F32)],
        ),
        out_shape=[
            jax.ShapeDtypeStruct((rows, count * group), BF16),
            jax.ShapeDtypeStruct((2 * half, 2 * count * HD), BF16),
            jax.ShapeDtypeStruct((8, HD), F32),
        ],
        compiler_params=pltpu.CompilerParams(vmem_limit_bytes=VMEM),
        cost_estimate=cost(9),
        name="attend_back",
    )(place, raw, kv_mine, kv_other, kv_mine, kv_other, *tables, grad, grad, *outs, logs)


def pick_rows(spot_row, cap):
    places = lax.broadcasted_iota(jnp.int32, (cap, spot_row.shape[1]), 0)
    return jnp.where(places == spot_row, 1.0, 0.0).astype(BF16)


def put_rows(spot_col, cap):
    places = lax.broadcasted_iota(jnp.int32, (spot_col.shape[0], cap), 1)
    return jnp.where(places == spot_col, 1.0, 0.0).astype(BF16)


def pick_kernel(cap, rows_ref, spot_ref, out_ref):
    block = spot_ref.shape[2]
    for e in range(spot_ref.shape[0]):
        for b in range(spot_ref.shape[1]):
            pick = pick_rows(spot_ref[e, b : b + 1, :], cap)
            rows = rows_ref[b * block : (b + 1) * block, :]
            out_ref[e, b * cap : (b + 1) * cap, :] = dot_nn(pick, rows).astype(BF16)


def pick(rows, spots, cap, width):
    experts, blocks, block = spots.shape
    tile = min(512, width)
    return pl.pallas_call(
        functools.partial(pick_kernel, cap),
        grid=(width // tile,),
        in_specs=[
            pl.BlockSpec((blocks * block, tile), lambda n: (0, n)),
            pl.BlockSpec(spots.shape, lambda n: (0, 0, 0)),
        ],
        out_specs=pl.BlockSpec((experts, blocks * cap, tile), lambda n: (0, 0, n)),
        out_shape=jax.ShapeDtypeStruct((experts, blocks * cap, width), BF16),
        compiler_params=pltpu.CompilerParams(vmem_limit_bytes=VMEM),
        cost_estimate=cost(3),
        name="pick",
    )(rows, spots)


def expert_kernel(
    cap,
    first_ref,
    rows_ref,
    spot_ref,
    mark_ref,
    cot_ref,
    router_ref,
    weight_ref,
    row_out,
    act_out,
    pre_out,
    extra_out,
):
    shards, _, depth, all_ff = weight_ref.shape
    ff = all_ff // 3
    experts = first_ref[1]
    block = spot_ref.shape[2]
    blocks = spot_ref.shape[1]
    marks = []
    for b in range(blocks):
        pick = pick_rows(spot_ref[0, b : b + 1, :], cap)
        span = slice(b * block, (b + 1) * block)
        row_out[0, b * cap : (b + 1) * cap, :] = dot_nn(pick, rows_ref[span, :]).astype(BF16)
        marks.append(dot_nn(pick, mark_ref[span, :]))
    marked = jnp.concatenate(marks, axis=0) > 0.5
    rows = row_out[0]
    logits = dot_nn(rows, router_ref[...])
    peak = jnp.max(jnp.where(marked, logits, MASKED_SCORE), axis=1, keepdims=True)
    weights = jnp.where(marked, jnp.exp(jnp.where(marked, logits - peak, 0.0)), 0.0)
    lanes = lax.broadcasted_iota(jnp.int32, weights.shape, 1)
    own = first_ref[0] + pl.program_id(0)
    total = jnp.sum(weights, axis=1, keepdims=True)
    gate = jnp.sum(jnp.where(lanes == own, weights, 0.0), axis=1, keepdims=True)
    gate = gate / jnp.where(total > 0.0, total, 1.0)
    pre = dot_nn(rows, weight_ref[:, :, :, : 2 * ff].reshape(shards * depth, 2 * ff))
    act_grad = dot_nn(cot_ref[0], weight_ref[:, :, :, 2 * ff :].reshape(shards * depth, ff))
    gate_pre, up_pre = pre[:, :ff], pre[:, ff:]
    sig = 1.0 / (1.0 + jnp.exp(-gate_pre))
    silu = gate_pre * sig
    act = silu * up_pre
    gate_grad = jnp.sum(act * act_grad, axis=1, keepdims=True)
    act_grad = act_grad * gate
    act_out[0] = (act * gate).astype(BF16)
    slope = sig * (1.0 + gate_pre * (1.0 - sig))
    pre_out[0, :, :ff] = (act_grad * up_pre * slope).astype(BF16)
    pre_out[0, :, ff:] = (act_grad * silu).astype(BF16)
    high = gate_grad.astype(BF16).astype(F32)
    low = gate_grad - high
    extra = jnp.where(lanes == own, high, jnp.where(lanes == own + experts, low, 0.0))
    extra_out[0] = extra.astype(BF16)


def expert_rows(first, rows, spots, marks, cot_rows, router, weights, cap):
    experts, blocks, block = spots.shape
    shards, _, depth, all_ff = weights.shape
    both = all_ff // 3 * 2
    width = rows.shape[1]
    count = blocks * cap
    one = lambda *shape: pl.BlockSpec((1,) + shape, lambda e, first: (e,) + (0,) * len(shape))
    whole = lambda a: pl.BlockSpec(a.shape, lambda e, first: (0, 0))
    return pl.pallas_call(
        functools.partial(expert_kernel, cap),
        grid_spec=pltpu.PrefetchScalarGridSpec(
            num_scalar_prefetch=1,
            grid=(experts,),
            in_specs=[
                whole(rows),
                one(blocks, block),
                whole(marks),
                one(count, width),
                whole(router),
                pl.BlockSpec((shards, 1, depth, all_ff), lambda e, first: (0, e, 0, 0)),
            ],
            out_specs=[
                one(count, width),
                one(count, both // 2),
                one(count, both),
                one(count, EXTRA),
            ],
        ),
        out_shape=[
            jax.ShapeDtypeStruct((experts, count, width), BF16),
            jax.ShapeDtypeStruct((experts, count, both // 2), BF16),
            jax.ShapeDtypeStruct((experts, count, both), BF16),
            jax.ShapeDtypeStruct((experts, count, EXTRA), BF16),
        ],
        compiler_params=pltpu.CompilerParams(vmem_limit_bytes=VMEM),
        cost_estimate=cost(11),
        name="expert_rows",
    )(first, rows, spots, marks, cot_rows, router, weights)


def rows_back_kernel(cap, shards, left_ref, spot_ref, *refs):
    out_ref, acc = refs[-2:]
    e = pl.program_id(0)
    blocks, block, wide = out_ref.shape
    depth = refs[0].shape[2]

    @pl.when(e == 0)
    def _():
        acc[...] = jnp.zeros_like(acc)

    lane = lax.broadcasted_iota(jnp.int32, spot_ref.shape, 1)
    spot = jnp.sum(jnp.where(lane == e, spot_ref[...], 0), axis=1, keepdims=True)
    puts = [put_rows(spot[b * block : (b + 1) * block], cap) for b in range(blocks)]
    for r in range(shards):
        rows = dot_nt(left_ref[0], refs[r][0, 0]).astype(BF16)
        for b in range(blocks):
            acc[b * block : (b + 1) * block, r * depth : (r + 1) * depth] += dot_nn(
                puts[b], rows[b * cap : (b + 1) * cap, :]
            )
    if len(refs) > shards + 2:
        for b in range(blocks):
            acc[b * block : (b + 1) * block, wide - EXTRA :] += dot_nn(
                puts[b], refs[shards][0, b * cap : (b + 1) * cap, :]
            )

    @pl.when(e == pl.num_programs(0) - 1)
    def _():
        out_ref[...] = acc[...].astype(BF16).reshape(out_ref.shape)


def rows_back(left, weights, at, spot_cols, cap, extra=None):
    experts, count, size = left.shape
    shards, _, depth, _ = weights.shape
    blocks = count // cap
    block = spot_cols.shape[0] // blocks
    width = depth * shards + (0 if extra is None else EXTRA)
    shape = (blocks, block, width)
    one = lambda *shape: pl.BlockSpec((1,) + shape, lambda e: (e,) + (0,) * len(shape))
    shard = lambda r: pl.BlockSpec((1, 1, depth, size), lambda e: (r, e, 0, at))
    extras = [] if extra is None else [extra]
    return pl.pallas_call(
        functools.partial(rows_back_kernel, cap, shards),
        grid=(experts,),
        in_specs=[one(count, size), pl.BlockSpec(spot_cols.shape, lambda e: (0, 0))]
        + [shard(r) for r in range(shards)]
        + [one(count, EXTRA)] * len(extras),
        out_specs=pl.BlockSpec(shape, lambda e: (0, 0, 0)),
        out_shape=jax.ShapeDtypeStruct(shape, BF16),
        scratch_shapes=[pltpu.VMEM((blocks * block, width), F32)],
        compiler_params=pltpu.CompilerParams(vmem_limit_bytes=VMEM),
        cost_estimate=cost(5 if extra is None else 10),
        name="mixtures" if extra is None else "row_grads",
    )(left, spot_cols, *[weights] * shards, *extras)


def expert_grad_kernel(row_a, row_b, cot_a, cot_b, pre_a, pre_b, act_a, act_b, out_ref):
    both = pre_a.shape[2]
    total = dot_tn(row_a[0], pre_a[0]) + dot_tn(row_b[0], pre_b[0])
    out_ref[0, 0, :, :both] = total.astype(BF16)
    total = dot_tn(cot_a[0], act_a[0]) + dot_tn(cot_b[0], act_b[0])
    out_ref[0, 0, :, both:] = total.astype(BF16)


def expert_grads(rows, cots, pres, acts, shards):
    experts, count, width = rows[0].shape
    both, ff = pres[0].shape[2], acts[0].shape[2]
    depth = width // shards
    part = pl.BlockSpec((1, count, depth), lambda e, n: (e, 0, n))
    full = lambda size: pl.BlockSpec((1, count, size), lambda e, n: (e, 0, 0))
    return pl.pallas_call(
        expert_grad_kernel,
        grid=(experts, shards),
        in_specs=[part] * 4 + [full(both)] * 2 + [full(ff)] * 2,
        out_specs=pl.BlockSpec((1, 1, depth, both + ff), lambda e, n: (n, e, 0, 0)),
        out_shape=jax.ShapeDtypeStruct((shards, experts, depth, both + ff), BF16),
        compiler_params=pltpu.CompilerParams(vmem_limit_bytes=VMEM),
        cost_estimate=cost(18),
        name="expert_grads",
    )(rows[0], rows[1], cots[0], cots[1], pres[0], pres[1], acts[0], acts[1])


def body(
    layer_input,
    w_query,
    w_key,
    w_value,
    w_out,
    attn_gain,
    query_gain,
    key_gain,
    ffn_gain,
    w_router,
    w_gate,
    w_up,
    w_down,
    routes,
    pic_starts,
    cotangent,
):
    tok_count, model_width = layer_input.shape
    top_count = routes.shape[1]
    ga_count = lax.axis_size("ga")
    z_count = lax.axis_size("z")
    ea_count = 2 * z_count
    core = lax.axis_index("core")
    chip = lax.axis_index("z")
    local_experts, _, ff = w_gate.shape
    expert_total = local_experts * ea_count
    cap = max(2, 9 * tok_count * top_count // (8 * expert_total))
    group_size = HEADS // KV
    kv_width = KV * HD
    q_width = HEADS * HD

    small = [attn_gain, query_gain, key_gain, ffn_gain, w_router.reshape(-1)]
    small_all = ga_gather_small(jnp.concatenate(small))
    at, smalls = 0, []
    for piece in small:
        smalls.append(small_all[:, at : at + piece.shape[0]].reshape(-1))
        at += piece.shape[0]
    attn_gain_f, query_gain_f, key_gain_f, ffn_gain_f = [s.astype(F32) for s in smalls[:4]]
    router_full = smalls[4].reshape(model_width, expert_total)
    router_wide = jnp.pad(router_full, ((0, 0), (0, EXTRA - expert_total)))

    qkv_weights = (w_query, w_key, w_value)
    qkv_own = jnp.concatenate([core_halves(w)[0] for w in qkv_weights], axis=1)

    marks = jnp.sum(
        (routes[:, :, None] == jnp.arange(EXTRA, dtype=jnp.int32)[None, None, :]).astype(F32), axis=1
    )
    cot_steps = []
    qkv_first = ga_first_hop(after(qkv_own, small_all))
    cot_mine = line_gather(
        after(jnp.concatenate([cotangent, marks.astype(BF16)], axis=1), small_all), steps=cot_steps
    )
    qkv_twin = jnp.concatenate(
        [core_halves(after(w, *cot_steps[0]))[1] for w in qkv_weights], axis=1
    )
    qkv_second = ga_second_hop(qkv_first, 0, 1, cot_steps[1])
    qkv_mine = qkv_first + qkv_second
    qkv_swapped = swap_pieces(qkv_mine[1:] if ga_count == 4 else qkv_mine)
    qkv_other = ([qkv_twin] if ga_count == 4 else []) + qkv_swapped
    cot_mine = after(jnp.concatenate(cot_mine), *qkv_second)
    cot_sides = [cot_mine, swap_core(cot_mine)]
    first_expert = (chip * 2 + core) * local_experts
    mark_sides, spot_rows, spot_cols, cot_rows = [], [], [], []
    before = jnp.tril(jnp.ones((tok_count, tok_count), BF16))
    for side in cot_sides:
        side_marks = side[:, model_width:]
        chosen = lax.dynamic_slice_in_dim(side_marks, first_expert, local_experts, 1)
        chosen = chosen.reshape(z_count, tok_count, local_experts)
        rank = jnp.einsum("ts,bse->bte", before, chosen, preferred_element_type=F32)
        spots = jnp.where(chosen > 0, rank - 1.0, -1.0).astype(jnp.int32)
        mark_sides.append(side_marks)
        spot_rows.append(jnp.transpose(spots, (2, 0, 1)))
        spot_cols.append(spots.reshape(z_count * tok_count, local_experts))
        cot_rows.append(pick(side, spot_rows[-1], cap, model_width))

    ea_index = chip * 2 + core
    positions = ea_index * tok_count + jnp.arange(tok_count, dtype=jnp.int32)
    holder = ((chip - jnp.arange(z_count)) % z_count * 2)[None, :] + jnp.stack([core, 1 - core])[
        :, None
    ]
    key_pos = (holder.reshape(-1, 1) * tok_count + jnp.arange(tok_count)[None, :]).reshape(-1)
    key_pos = key_pos.astype(jnp.int32)
    allowed = allowed_mask(pic_starts[0], positions, key_pos)
    bias = jnp.where(allowed, 0.0, MASKED_SCORE).astype(F32)
    bias_turned = jnp.where(jnp.transpose(allowed), 0.0, MASKED_SCORE).astype(F32)
    frequency = ROPE_THETA ** (-jnp.arange(HD // 2, dtype=F32) * 2.0 / HD)
    angles = positions.astype(F32)[:, None] * frequency[None, :]
    cosine = jnp.concatenate([jnp.cos(angles), jnp.cos(angles)], axis=1)
    sine = jnp.concatenate([-jnp.sin(angles), jnp.sin(angles)], axis=1)
    per_key = max(1, ga_count // KV)
    ga_index = lax.axis_index("ga")
    run = group_size // 2 // per_key
    step = jnp.arange(per_key) ^ (ga_index % per_key)
    own_heads = (step[:, None] * 2 * run + jnp.arange(run)[None, :]).reshape(-1)
    key_place = jnp.arange(KV) ^ (ga_index // per_key)
    place = jnp.concatenate(
        [key_place, own_heads + core * run, own_heads + (1 - core) * run]
    ).astype(jnp.int32)

    input_f = layer_input.astype(F32)
    normed = rms_norm(input_f, attn_gain_f).astype(BF16)
    normed_mine = split_cols(normed, core)
    normed_other = split_cols(normed, 1 - core)
    normed_used = after(normed_mine, bias, bias_turned, cosine, sine)
    qkv = pieces_matmul((normed_used, normed_other), (qkv_mine, qkv_other))
    query_gain_row, key_gain_row = query_gain_f.reshape(1, HD), key_gain_f.reshape(1, HD)
    kv_own = prep_kv(qkv, cosine, sine, key_gain_row)

    out_own, out_twin = core_halves(w_out)
    out_first = ga_first_hop(after(out_own, *qkv_second))
    kv_steps = []
    kv_mine, kv_other = ea_gather(
        kv_own, {2: cot_rows[:1], 3: cot_rows[1:] + out_first[1:]}, kv_steps
    )
    out_second = ga_second_hop(out_first, 0, 1, ())
    out_mine = out_first + out_second
    expert_own = jnp.concatenate([w_gate, w_up, jnp.swapaxes(w_down, 1, 2)], axis=2)
    expert_all = lax.all_gather(after(expert_own, *out_first[1:], *kv_steps[1]), "ga", axis=0)

    att_mine, att_other, log_rows = attend(
        place,
        qkv,
        kv_mine,
        kv_other,
        bias,
        cosine,
        sine,
        query_gain_row,
    )
    out_swapped = swap_pieces(out_first[1:] if ga_count == 4 else out_first)
    out_swapped += swap_pieces([after(piece, att_mine) for piece in out_second])
    out_other = ([out_twin] if ga_count == 4 else []) + out_swapped
    hidden = input_f + pieces_matmul((att_mine, att_other), (out_mine, out_other))
    ffn_in = rms_norm(hidden, ffn_gain_f).astype(BF16)

    row_mine = after(jnp.concatenate(line_gather(ffn_in)), expert_all)
    row_sides = [row_mine, swap_core(row_mine)]
    logits = dot_nn(ffn_in, router_full)
    own_marks = marks[:, :expert_total] > 0
    peak = jnp.max(jnp.where(own_marks, logits, MASKED_SCORE), axis=1, keepdims=True)
    weights = jnp.exp(jnp.where(own_marks, logits - peak, MASKED_SCORE))
    gates = weights / jnp.sum(weights, axis=1, keepdims=True)

    first = jnp.stack([first_expert, expert_total]).astype(jnp.int32)
    picked, acts, pres, extras = [], [], [], []
    for side in range(2):
        rows, act, pre, extra = expert_rows(
            first,
            row_sides[side],
            spot_rows[side],
            mark_sides[side],
            cot_rows[side],
            router_wide,
            expert_all,
            cap,
        )
        picked.append(rows)
        acts.append(act)
        pres.append(pre)
        extras.append(extra)
    expert_grad = expert_grads(picked, cot_rows, pres, acts, ga_count)
    expert_sum = lax.psum_scatter(expert_grad, "ga", scatter_dimension=0)
    row_other = rows_back(
        after(pres[1], expert_grad), expert_all, 0, spot_cols[1], cap, extras[1]
    )
    row_mine = rows_back(
        after(pres[0], row_other), expert_all, 0, spot_cols[0], cap, extras[0]
    )
    rows = LineSum(core_slots(row_mine, row_other))
    held = rows.step()
    mix_other = rows_back(after(acts[1], rows.slots[1]), expert_all, 2, spot_cols[1], cap)
    rows.step(mix_other)
    mix_mine = rows_back(after(acts[0], *held), expert_all, 2, spot_cols[0], cap)
    mix = LineSum(core_slots(mix_mine, mix_other))
    rows.step(mix_mine)
    row_sum = after(rows.result(), *mix.slots)

    grad_out = cotangent.astype(F32)
    gate_grad = (
        row_sum[:, model_width : model_width + expert_total].astype(F32)
        + row_sum[:, model_width + expert_total : model_width + 2 * expert_total].astype(F32)
    )
    inner = jnp.sum(gates * gate_grad, axis=1, keepdims=True)
    logit_grad = gates * (gate_grad - inner)
    router_grad = lax.dot_general(
        ffn_in.astype(F32), logit_grad, (((0,), (0,)), ((), ())), precision=PRECISE
    )
    ffn_in_grad = row_sum[:, :model_width].astype(F32) + jnp.dot(
        logit_grad, router_full.astype(F32).T, precision=PRECISE
    )
    unused, ffn_back = jax.vjp(rms_norm, hidden, ffn_gain_f)
    hidden_part, ffn_gain_grad = ffn_back(ffn_in_grad)
    hidden_grad = grad_out + hidden_part
    branch_grad = hidden_grad.astype(BF16)
    out_terms = [dot_tn(device_cols(a), branch_grad) for a in (att_mine, att_other)]
    out_terms[1] = out_terms[1].astype(BF16)
    held = [mix.step(*rows.held)]
    att_grads = pieces_back(
        after(branch_grad, out_terms[1], *held[0]), out_mine + out_other, BF16
    )
    raw_grads, kv_grads, gain_grads = [], [], []

    def back(head, *before):
        raw_grad, kv_grad, gain_grad = attend_back(
            head,
            1,
            place,
            qkv,
            kv_mine,
            kv_other,
            bias_turned,
            cosine,
            sine,
            query_gain_row,
            after(att_grads, *before),
            (att_mine, att_other),
            log_rows,
        )
        raw_grads.append(raw_grad)
        kv_grads.append(kv_grad)
        gain_grads.append(gain_grad[0])

    def weight_terms(grad):
        return dot_tn(normed_mine, grad), dot_tn(normed_other, grad).astype(BF16)

    back(0, out_terms[1], expert_sum, *mix.sent)
    held.append(mix.step(raw_grads[0]))
    out_total = core_sum(*out_terms, before=[att_grads])
    out_share = lax.psum_scatter(out_total, "ga", scatter_dimension=0, tiled=True)
    back(1, raw_grads[0], out_total, *held[0])
    held.append(mix.step(raw_grads[1]))
    query_parts = [jnp.concatenate(raw_grads[:2], axis=1)]
    query_terms = [weight_terms(query_parts[0])]
    back(2, raw_grads[1], *held[1])
    query_totals = [core_sum(*query_terms[0])]
    back(3, raw_grads[2], query_terms[0][1], out_share, *held[2])
    query_firsts = [ga_sum_first(query_totals[0])]
    mix_sum = mix.result()
    layer_output = (hidden + mix_sum.astype(F32)).astype(BF16)
    query_parts.append(jnp.concatenate(raw_grads[2:], axis=1))
    query_terms.append(weight_terms(query_parts[1]))
    query_gain_grad = sum(gain_grads)
    kv_grad = after(jnp.concatenate(kv_grads, axis=1), *held[2])
    kv_grad = kv_grad.reshape(2, z_count, tok_count, 2 * kv_width)
    keys_values = LineSum(core_slots(kv_grad[0], kv_grad[1]))
    out_all = z_all_sum(out_share)
    keys_values.step(query_terms[1][1], *query_firsts[0], out_all)
    query_shares = [ga_sum_second(query_firsts[0])]
    query_totals.append(core_sum(*query_terms[1]))
    keys_values.step(query_totals[1])
    query_firsts.append(ga_sum_first(after(query_totals[1], query_shares[0])))
    keys_values.step(query_shares[0])
    kv_raw_grad, key_gain_grad = kv_back(
        qkv, after(keys_values.result(), *query_firsts[1]), cosine, sine, key_gain_row
    )
    key_gain_grad = key_gain_grad[0]
    chunks = query_parts + [kv_raw_grad]
    qkv_grad = jnp.concatenate(chunks, axis=1)
    both_grads = pieces_back(qkv_grad, qkv_mine + qkv_other, F32)
    query_shares.append(ga_sum_second(query_firsts[1], [both_grads]))
    kv_total = core_sum(*weight_terms(kv_raw_grad))
    kv_first = ga_sum_first(after(kv_total, query_shares[1]))
    query_alls = [z_all_sum(after(share, out_all)) for share in query_shares]
    kv_share = ga_sum_second(kv_first)
    kv_sum = whole_shard([z_all_sum_small(after(kv_share, *query_alls))])
    out_sum = whole_shard([out_all])
    query_sum = whole_shard(query_alls)
    key_sum, value_sum = kv_sum[:, :kv_width], kv_sum[:, kv_width:]
    both_grads = after(both_grads, query_shares[1])
    half_width = model_width // 2
    normed_grad = join_cols(both_grads[:, :half_width], both_grads[:, half_width:])
    unused, attn_back = jax.vjp(rms_norm, input_f, attn_gain_f)
    input_part, attn_gain_grad = attn_back(normed_grad)
    input_grad = (hidden_grad + input_part).astype(BF16)

    tiny = [attn_gain_grad, query_gain_grad, key_gain_grad, ffn_gain_grad, router_grad.reshape(-1)]
    tiny_rows = jnp.concatenate([t.reshape(ga_count, -1) for t in tiny], axis=1)
    tiny_own = sum_small(after(tiny_rows, *query_alls))
    at, tiny_sums = 0, []
    for piece in tiny:
        width = piece.shape[0] // ga_count
        tiny_sums.append(tiny_own[at : at + width])
        at += width
    attn_sum, qgain_sum, kgain_sum, ffn_sum, router_sum = tiny_sums
    return (
        layer_output,
        input_grad,
        query_sum,
        key_sum,
        value_sum,
        out_sum,
        attn_sum,
        qgain_sum,
        kgain_sum,
        ffn_sum,
        router_sum.reshape(-1, expert_total),
        expert_sum[:, :, :ff].astype(F32),
        expert_sum[:, :, ff : 2 * ff].astype(F32),
        jnp.swapaxes(expert_sum[:, :, 2 * ff :], 1, 2).astype(F32),
    )


def solution(mesh):
    ga_count, ea_count = mesh.shape["ga"], mesh.shape["ea"]
    inner = Mesh(mesh.devices.reshape(ga_count, ea_count // 2, 2), ("ga", "z", "core"))
    everyone = ("ga", "z", "core")
    owners = ("z", "core")
    in_specs = (
        P(everyone, None),
        P("ga", None),
        P("ga", None),
        P("ga", None),
        P("ga", None),
        P("ga"),
        P("ga"),
        P("ga"),
        P("ga"),
        P("ga", None),
        P(owners, "ga", None),
        P(owners, "ga", None),
        P(owners, None, "ga"),
        P(everyone, None),
        P("ga", None),
        P(everyone, None),
    )
    out_specs = (
        P(everyone, None),
        P(everyone, None),
        P("ga", None),
        P("ga", None),
        P("ga", None),
        P("ga", None),
        P("ga"),
        P("ga"),
        P("ga"),
        P("ga"),
        P("ga", None),
        P(owners, "ga", None),
        P(owners, "ga", None),
        P(owners, None, "ga"),
    )
    return jax.shard_map(body, mesh=inner, in_specs=in_specs, out_specs=out_specs, check_vma=False)
```
